32 devices in a mesh: groups: 2 (over x), seq: 16 (over z, y, core).
Axes of the slice: x: 2, y: 2, z: 4, core: 2. Of those that a mesh axis runs over, the one named last changes fastest.
Arguments:
- tokens: bfloat16 [96, 5120], P(('groups', 'seq')), parts along dimension 0, may hold values from -6 to 6
- modulation: float32 [6, 5120], replicated, may hold values from -2.5 to 2.5
- w_qkv: bfloat16 [3, 5120, 2560], P(None, None, 'seq'), may hold values from -0.078125 to 0.078125
- norm_gains: float32 [2, 2560], replicated, may hold values from 0.56 to 12
- cache_kv: bfloat16 [2, 2, 96, 2560], P(None, None, ('groups', 'seq')), parts along dimension 2, may hold values from -17 to 17
- w_out: bfloat16 [2560, 5120], P(None, 'seq'), may hold values from -0.125 to 0.125
- w_up: bfloat16 [5120, 13824], P(None, 'seq'), may hold values from -0.078125 to 0.078125
- w_down: bfloat16 [13824, 5120], P('seq'), may hold values from -0.0546875 to 0.0546875
Outputs:
- block_out: bfloat16 [96, 5120], P(('groups', 'seq')), parts along dimension 0
The draws below stay inside these ranges and needn't reach their ends.
There are 2 independent parts, one for each index of `groups`. The reference program is written for one: setup_inputs(seed, part) draws one part's arguments, and reference() takes and returns one part's arrays. A program takes and returns all parts, laid end to end along the dimension named above; an argument that names none is the same for every part. Nothing has to cross between parts.
All inputs are finite; a program needn't handle non-finite values.
Results may differ from the reference program's by a relative error of at most 0.017.
The reference program's roundings to bfloat16 on the way (of `normed`, `qkv`, `weights`, `attended`, `projected`, `normed2` and `hidden`) count: a program that leaves them out, or rounds other values in their place, can miss the bound.
Values may be sent and summed in bfloat16 or wider, within the bound.
No kernel may reach another device: no remote copies, remote signals or barrier semaphores. Data moves between devices by JAX's collectives and lax.ppermute only.
A program may use at most 128 MiB of HBM per device.

```python
import math
import jax
import jax.numpy as jnp
from jax import lax

D = 5120
FF = 13824
HEAD_DIM = 128
HEADS = 20
FRAMES = 2
ATTN = 2560
TOKENS = 48


def draw_norm_gains(key, part):
    key_one, key_two = jax.random.split(jax.random.fold_in(key, 11))
    lower, upper = (0.7, 1.6)
    head_scale = jnp.exp(jax.random.uniform(key_one, (2, HEADS, 1), jnp.float32, math.log(lower), math.log(upper)))
    channel = jax.random.uniform(key_two, (2, HEADS, HEAD_DIM), jnp.float32, 0.8, 1.2)
    return (head_scale * channel).reshape(2, HEADS * HEAD_DIM)


def draw_cache_kv(key, part):
    key_one, key_two, key_three = jax.random.split(jax.random.fold_in(key, 23), 3)
    shape = (FRAMES, TOKENS, HEADS, HEAD_DIM)
    head_scale = jnp.exp(jax.random.uniform(key_one, (1, 1, HEADS, 1), jnp.float32, math.log(0.7), math.log(1.6)))
    keys = jnp.clip(jax.random.normal(key_two, shape, jnp.float32), -4.0, 4.0) * head_scale
    values = jnp.clip(jax.random.normal(key_three, shape, jnp.float32), -4.0, 4.0)
    stacked = jnp.stack([keys, values]).reshape(2, FRAMES, TOKENS, HEADS * HEAD_DIM)
    return stacked.astype(jnp.bfloat16)


def levels(rng, dims, cuts, least, top_value):
    loudness, own = 1.0, jax.random.fold_in(rng, 6)
    for position, parts in cuts:
        heights = jnp.exp(jax.random.uniform(jax.random.fold_in(own, position), (parts,), jnp.float32, least / len(cuts), top_value / len(cuts)))
        loudness = loudness * jnp.repeat(heights, dims[position] // parts).reshape([-1 if axis == position else 1 for axis in range(len(dims))])
    return loudness


def scatter_about(own_key, shape, scale, reach, shards=(), dtype=jnp.bfloat16):
    values = scale * jax.random.normal(own_key, shape, jnp.float32)
    if shards:
        values = values * levels(own_key, shape, shards, -0.22, 0.18)
    return jnp.clip(values, -reach, reach).astype(dtype)


def setup_inputs(seed: int = 0, part: int = 0) -> dict:
    key_of = jax.random.split(jax.random.key(seed), 9)
    part_splits = jax.random.split(jax.random.fold_in(key_of[8], part), 9)
    return {
        "tokens": scatter_about(part_splits[0], (TOKENS, D), 1.0, 6.0, ((0, 16),)),
        "modulation": scatter_about(key_of[1], (6, D), 0.6, 2.5, (), jnp.float32),
        "w_qkv": scatter_about(key_of[2], (3, D, ATTN), D ** -0.5, 0.078125, ((2, 16),)),
        "norm_gains": draw_norm_gains(jax.random.fold_in(key_of[8], 71), part),
        "cache_kv": draw_cache_kv(jax.random.fold_in(jax.random.fold_in(key_of[8], part), 71), part),
        "w_out": scatter_about(key_of[5], (ATTN, D), ATTN ** -0.5, 0.125, ((1, 16),)),
        "w_up": scatter_about(key_of[6], (D, FF), D ** -0.5, 0.078125, ((1, 16),)),
        "w_down": scatter_about(key_of[7], (FF, D), FF ** -0.5, 0.0546875, ((0, 16),)),
    }


def layer_norm(values):
    center = values - lax.optimization_barrier(jnp.mean(values, axis=-1, keepdims=True))
    spread = lax.optimization_barrier(jnp.mean(center * center, axis=-1, keepdims=True))
    return center * lax.rsqrt(spread + 1e-06)

def rms_norm(values, gain):
    return values * lax.rsqrt(lax.optimization_barrier(jnp.mean(values * values, axis=-1, keepdims=True)) + 1e-06) * gain

def reference(tokens, modulation, w_qkv, norm_gains, cache_kv, w_out, w_up, w_down):
    residual = tokens.astype(jnp.float32)
    normed = (layer_norm(residual) * (1.0 + modulation[1]) + modulation[0]).astype(jnp.bfloat16)
    qkv = [jnp.dot(normed, w_qkv[index], preferred_element_type=jnp.float32).astype(jnp.bfloat16) for index in range(3)]
    queries = rms_norm(qkv[0].astype(jnp.float32), norm_gains[0]).astype(jnp.bfloat16)
    keys_now = rms_norm(qkv[1].astype(jnp.float32), norm_gains[1]).astype(jnp.bfloat16)
    keys = jnp.concatenate([cache_kv[0].reshape(FRAMES * TOKENS, ATTN), keys_now], axis=0)
    values = jnp.concatenate([cache_kv[1].reshape(FRAMES * TOKENS, ATTN), qkv[2]], axis=0)
    scale = 1.0 / math.sqrt(HEAD_DIM)
    query_heads = queries.reshape(TOKENS, HEADS, HEAD_DIM).transpose(1, 0, 2)
    key_heads = keys.reshape(-1, HEADS, HEAD_DIM).transpose(1, 0, 2)
    value_heads = values.reshape(-1, HEADS, HEAD_DIM).transpose(1, 0, 2)

    def one_head(operands):
        query_h, key_h, value_h = operands
        scores = jnp.dot(query_h, key_h.T, preferred_element_type=jnp.float32) * scale
        peak = lax.optimization_barrier(jnp.max(scores, axis=-1, keepdims=True))
        expo = jnp.exp(scores - peak)
        total = lax.optimization_barrier(jnp.sum(expo, axis=-1, keepdims=True))
        weights = expo.astype(jnp.bfloat16)
        return jnp.dot(weights, value_h, preferred_element_type=jnp.float32) / total
    heads_out = lax.map(one_head, (query_heads, key_heads, value_heads))
    attended = heads_out.transpose(1, 0, 2).reshape(TOKENS, ATTN).astype(jnp.bfloat16)
    projected = jnp.dot(attended, w_out, preferred_element_type=jnp.float32).astype(jnp.bfloat16)
    residual = residual + modulation[2] * projected.astype(jnp.float32)
    normed2 = (layer_norm(residual) * (1.0 + modulation[4]) + modulation[3]).astype(jnp.bfloat16)
    hidden = jax.nn.gelu(jnp.dot(normed2, w_up, preferred_element_type=jnp.float32), approximate=True).astype(jnp.bfloat16)
    feed = jnp.dot(hidden, w_down, preferred_element_type=jnp.float32)
    return (residual + modulation[5] * feed).astype(jnp.bfloat16)
```

```python
import math

import jax
import jax.numpy as jnp
from jax import lax
from jax.sharding import PartitionSpec as P

HEAD_DIM = 128
HEADS = 20


def layer_norm(values):
    center = values - jnp.mean(values, axis=-1, keepdims=True)
    spread = jnp.mean(center * center, axis=-1, keepdims=True)
    return center * lax.rsqrt(spread + 1e-06)


def rms_norm(values, gain):
    return values * lax.rsqrt(jnp.mean(values * values, axis=-1, keepdims=True) + 1e-06) * gain


def swap(values, offset):
    return lax.ppermute(values, "seq", [(i, i ^ offset) for i in range(16)])


def gather(block):
    planes = jnp.stack([block] + [swap(block, 4 * z) for z in (1, 2, 3)])
    half = jnp.concatenate([planes, swap(planes, 2)])
    return jnp.concatenate([half, swap(half, 1)])


def in_order(slots, me):
    apart = jnp.arange(16) ^ me
    return slots[(apart & 1) * 8 + ((apart >> 1) & 1) * 4 + (apart >> 2)]


def scatter_sum(partial, me):
    apart = jnp.arange(16) ^ me
    near = partial[apart].reshape(4, 2, 2, *partial.shape[1:])
    near = near[:, :, 0] + swap(near[:, :, 1].astype(jnp.bfloat16), 1).astype(jnp.float32)
    near = near[:, 0] + swap(near[:, 1].astype(jnp.bfloat16), 2).astype(jnp.float32)
    total = near[0]
    for z in (1, 2, 3):
        total = total + swap(near[z].astype(jnp.bfloat16), 4 * z).astype(jnp.float32)
    return total


def staged(tokens, modulation, w_qkv, norm_gains, cache_kv, w_out, w_up, w_down):
    own_rows = tokens.shape[0]
    rows = own_rows * 16
    width = HEADS * HEAD_DIM
    scale = 1.0 / math.sqrt(HEAD_DIM)
    me = lax.axis_index("seq")
    all_tokens = in_order(gather(tokens), me).reshape(rows, -1).astype(jnp.float32)
    cached = in_order(gather(cache_kv), me)
    cached = cached.transpose(1, 0, 2, 3, 4).reshape(2, -1, width)
    normed = (layer_norm(all_tokens) * (1.0 + modulation[1]) + modulation[0]).astype(jnp.bfloat16)
    qkv_cols = jnp.einsum("td,kda->kta", normed, w_qkv, preferred_element_type=jnp.float32).astype(jnp.bfloat16)
    qkv = in_order(gather(qkv_cols), me).transpose(1, 2, 0, 3).reshape(3, rows, width)
    queries = rms_norm(qkv[0].astype(jnp.float32), norm_gains[0]).astype(jnp.bfloat16)
    keys_now = rms_norm(qkv[1].astype(jnp.float32), norm_gains[1]).astype(jnp.bfloat16)
    keys = jnp.concatenate([cached[0], keys_now]).reshape(-1, HEADS, HEAD_DIM)
    values = jnp.concatenate([cached[1], qkv[2]]).reshape(-1, HEADS, HEAD_DIM)
    scores = (
        jnp.einsum("qhd,khd->hqk", queries.reshape(rows, HEADS, HEAD_DIM), keys, preferred_element_type=jnp.float32)
        * scale
    )
    expo = jnp.exp(scores - jnp.max(scores, axis=-1, keepdims=True))
    total = jnp.sum(expo, axis=-1, keepdims=True)
    summed = jnp.einsum("hqk,khd->hqd", expo.astype(jnp.bfloat16), values, preferred_element_type=jnp.float32) / total
    attended = summed.transpose(1, 0, 2).reshape(rows, width).astype(jnp.bfloat16)
    projected_cols = jnp.dot(attended, w_out, preferred_element_type=jnp.float32).astype(jnp.bfloat16)
    projected = in_order(gather(projected_cols), me).transpose(1, 0, 2).reshape(rows, -1)
    residual = all_tokens + modulation[2] * projected.astype(jnp.float32)
    normed2 = (layer_norm(residual) * (1.0 + modulation[4]) + modulation[3]).astype(jnp.bfloat16)
    hidden = jax.nn.gelu(
        jnp.dot(normed2, w_up, preferred_element_type=jnp.float32), approximate=True
    ).astype(jnp.bfloat16)
    partial = jnp.dot(hidden, w_down, preferred_element_type=jnp.float32)
    feed = scatter_sum(partial.reshape(16, own_rows, -1), me)
    own = lax.dynamic_index_in_dim(residual.reshape(16, own_rows, -1), me, 0, keepdims=False)
    return (own + modulation[5] * feed).astype(jnp.bfloat16)


def general(tokens, modulation, w_qkv, norm_gains, cache_kv, w_out, w_up, w_down):
    own_rows = tokens.shape[0]
    width = HEADS * HEAD_DIM
    scale = 1.0 / math.sqrt(HEAD_DIM)
    residual = tokens.astype(jnp.float32)
    normed = (layer_norm(residual) * (1.0 + modulation[1]) + modulation[0]).astype(jnp.bfloat16)
    qkv_cols = jnp.einsum(
        "td,kda->kta",
        lax.all_gather(normed, "seq", axis=0, tiled=True),
        w_qkv,
        preferred_element_type=jnp.float32,
    ).astype(jnp.bfloat16)
    qkv = lax.all_to_all(qkv_cols, "seq", split_axis=1, concat_axis=2, tiled=True)
    queries = rms_norm(qkv[0].astype(jnp.float32), norm_gains[0]).astype(jnp.bfloat16)
    keys_now = rms_norm(qkv[1].astype(jnp.float32), norm_gains[1]).astype(jnp.bfloat16)
    local_keys = jnp.concatenate([cache_kv[0].reshape(-1, width), keys_now], axis=0)
    local_values = jnp.concatenate([cache_kv[1].reshape(-1, width), qkv[2]], axis=0)
    query_heads = queries.reshape(own_rows, HEADS, HEAD_DIM)
    peak_old = jnp.full((own_rows, HEADS), -1e30, jnp.float32)
    key_piece = lax.all_gather(local_keys, "seq", axis=0, tiled=True)
    value_piece = lax.all_gather(local_values, "seq", axis=0, tiled=True)
    count = key_piece.shape[0]
    scores = (
        jnp.einsum(
            "qhd,khd->qhk",
            query_heads,
            key_piece.reshape(count, HEADS, HEAD_DIM),
            preferred_element_type=jnp.float32,
        )
        * scale
    )
    peak_new = jnp.maximum(peak_old, jnp.max(scores, axis=-1))
    expo = jnp.exp(scores - peak_new[..., None])
    total_new = jnp.sum(expo, axis=-1)
    weights = expo.astype(jnp.bfloat16)
    summed_new = jnp.einsum(
        "qhk,khd->qhd",
        weights,
        value_piece.reshape(count, HEADS, HEAD_DIM),
        preferred_element_type=jnp.float32,
    )
    attended = (summed_new / total_new[..., None]).reshape(own_rows, width).astype(jnp.bfloat16)
    projected_cols = jnp.dot(
        lax.all_gather(attended, "seq", axis=0, tiled=True),
        w_out,
        preferred_element_type=jnp.float32,
    ).astype(jnp.bfloat16)
    projected = lax.all_to_all(projected_cols, "seq", split_axis=0, concat_axis=1, tiled=True)
    residual = residual + modulation[2] * projected.astype(jnp.float32)
    normed2 = (layer_norm(residual) * (1.0 + modulation[4]) + modulation[3]).astype(jnp.bfloat16)
    hidden = jax.nn.gelu(
        jnp.dot(
            lax.all_gather(normed2, "seq", axis=0, tiled=True),
            w_up,
            preferred_element_type=jnp.float32,
        ),
        approximate=True,
    ).astype(jnp.bfloat16)
    feed = lax.psum_scatter(
        jnp.dot(hidden, w_down, preferred_element_type=jnp.float32),
        "seq",
        scatter_dimension=0,
        tiled=True,
    )
    return (residual + modulation[5] * feed).astype(jnp.bfloat16)


def solution(mesh):
    in_specs = (
        P(("groups", "seq"), None),
        P(),
        P(None, None, "seq"),
        P(),
        P(None, None, ("groups", "seq"), None),
        P(None, "seq"),
        P(None, "seq"),
        P("seq", None),
    )
    out_specs = P(("groups", "seq"), None)
    local = staged if mesh.shape["seq"] == 16 else general
    return jax.shard_map(local, mesh=mesh, in_specs=in_specs, out_specs=out_specs, check_vma=False)
```

```python
import math

import jax
import jax.numpy as jnp
from jax import lax
from jax.experimental import pallas as pl
from jax.experimental.pallas import tpu as pltpu
from jax.sharding import PartitionSpec as P

HEAD_DIM = 128
HEADS = 20


def layer_norm(values):
    center = values - jnp.mean(values, axis=-1, keepdims=True)
    spread = jnp.mean(center * center, axis=-1, keepdims=True)
    return center * lax.rsqrt(spread + 1e-06)


def rms_norm(values, gain):
    return values * lax.rsqrt(jnp.mean(values * values, axis=-1, keepdims=True) + 1e-06) * gain


VMEM = pl.BlockSpec(memory_space=pltpu.VMEM)
ANY = pl.BlockSpec(memory_space=pl.ANY)
NT = (((1,), (1,)), ((), ()))


def call(body, outs, *operands, any_space=(), scratch=(), limit=24, flops=0, moved=0):
    return pl.pallas_call(
        body,
        out_shape=[jax.ShapeDtypeStruct(shape, dtype) for shape, dtype in outs],
        in_specs=[ANY if i in any_space else VMEM for i in range(len(operands))],
        out_specs=[VMEM] * len(outs),
        scratch_shapes=list(scratch),
        compiler_params=pltpu.CompilerParams(vmem_limit_bytes=limit << 20),
        cost_estimate=pl.CostEstimate(flops=flops, bytes_accessed=moved, transcendentals=0),
    )(*operands)


def load(weights):
    rows, width = weights.shape
    cuts = [rows * i // 4 // 16 * 16 for i in range(4)] + [rows]

    def body(source, target, sems):
        copies = [
            pltpu.make_async_copy(source.at[pl.ds(a, b - a)], target.at[pl.ds(a, b - a)], sems.at[i])
            for i, (a, b) in enumerate(zip(cuts, cuts[1:]))
        ]
        for copy in copies:
            copy.start()
        for copy in copies:
            copy.wait()

    scratch = [pltpu.SemaphoreType.DMA((4,))]
    moved = rows * width * 4
    return call(body, [((rows, width), weights.dtype)], weights, any_space=(0,), scratch=scratch, moved=moved)[0]


def swap(values, offset):
    return lax.ppermute(values, "seq", [(i, i ^ offset) for i in range(16)])


def stack(pieces):
    def body(*refs):
        for i, ref in enumerate(refs[:-1]):
            refs[-1][i] = ref[...]

    return call(body, [((len(pieces), *pieces[0].shape), pieces[0].dtype)], *pieces)[0]


def gather(block, tie=lambda pieces: pieces):
    planes = stack(tie([block] + [swap(block, 4 * z) for z in (1, 2, 3)]))
    across = swap(planes, 2)
    return [planes, across, swap(planes, 1), swap(across, 1)]


def apart(slot, z):
    return 4 * z + 2 * (slot & 1) + (slot >> 1)


def place(stacks, target):
    me = lax.axis_index("seq")
    for slot, ref in enumerate(stacks):
        for z in range(4):
            target[me ^ apart(slot, z)] = ref[z]


def normalize(values, shift, gain):
    return (layer_norm(values) * (1.0 + gain) + shift).astype(jnp.bfloat16)


def project_qkv(s0, s1, s2, s3, mod, weights, tokens_out, qkv_out, slots, flat):
    place((s0, s1, s2, s3), slots)
    for j in range(16):
        flat[3 * j : 3 * j + 3, :] = slots[j].astype(jnp.float32)
    tokens = flat[...]
    tokens_out[...] = tokens.astype(jnp.bfloat16)
    normed = normalize(tokens, mod[0:1, :], mod[1:2, :])
    qkv_out[...] = lax.dot_general(normed, weights[...], NT, preferred_element_type=jnp.float32).astype(jnp.bfloat16)


def line_up(s0, s1, s2, s3, keys_out, values_out, keys, values):
    for slot, ref in enumerate((s0, s1, s2, s3)):
        for z in range(4):
            for token in range(3):
                row = 6 * (4 * slot + z) + 2 * token
                keys[row : row + 2, :] = ref[z, 0, token].astype(jnp.float32)
                values[row : row + 2, :] = ref[z, 1, token].astype(jnp.float32)
    keys_out[...] = keys[...].astype(jnp.bfloat16)
    values_out[...] = values[...].astype(jnp.bfloat16)


def attend(s0, s1, s2, s3, old_keys, old_values, gains, weights, out, slots, attended):
    place((s0, s1, s2, s3), slots)
    pieces = [slots[j].astype(jnp.float32) for j in range(16)]
    queries, keys, values = (
        jnp.concatenate([piece[:, 160 * i : 160 * i + 160] for piece in pieces], axis=1) for i in range(3)
    )
    queries = rms_norm(queries, gains[0:1, :]).astype(jnp.bfloat16)
    keys = jnp.concatenate([old_keys[...], rms_norm(keys, gains[1:2, :]).astype(jnp.bfloat16)], axis=0)
    values = jnp.concatenate([old_values[...], values.astype(jnp.bfloat16)], axis=0)
    for head in range(HEADS):
        cols = slice(HEAD_DIM * head, HEAD_DIM * (head + 1))
        scores = lax.dot_general(queries[:, cols], keys[:, cols], NT, preferred_element_type=jnp.float32)
        scores = scores * (1.0 / math.sqrt(HEAD_DIM))
        expo = jnp.exp(scores - jnp.max(scores, axis=-1, keepdims=True))
        total = jnp.sum(expo, axis=-1, keepdims=True)
        summed = jnp.dot(expo.astype(jnp.bfloat16), values[:, cols], preferred_element_type=jnp.float32)
        attended[:, cols] = (summed / total).astype(jnp.bfloat16)
    out[...] = lax.dot_general(attended[...], weights[...], NT, preferred_element_type=jnp.float32).astype(jnp.bfloat16)


def feed_forward(s0, s1, s2, s3, tokens, own, mod, w_up, w_down, keep, send, residual_out, slots):
    place((s0, s1, s2, s3), slots)
    projected = jnp.concatenate([slots[j] for j in range(16)], axis=1)
    gate = mod[2:3, :]
    residual = tokens[...].astype(jnp.float32) + gate * projected.astype(jnp.float32)
    normed = normalize(residual, mod[3:4, :], mod[4:5, :])
    hidden = lax.dot_general(normed, w_up[...], NT, preferred_element_type=jnp.float32)
    hidden = jax.nn.gelu(hidden, approximate=True).astype(jnp.bfloat16)
    me = lax.axis_index("seq")
    row = lax.broadcasted_iota(jnp.int32, (48, 48), 0)
    token = lax.broadcasted_iota(jnp.int32, (48, 48), 1)
    block = (row * 171) >> 9
    device = me ^ (4 * (block & 3) + 2 * ((block >> 2) & 1) + (block >> 3))
    pick = (token == 3 * device + row - 3 * block).astype(jnp.bfloat16)
    hidden = jnp.dot(pick, hidden, preferred_element_type=jnp.float32).astype(jnp.bfloat16)
    partial = jnp.dot(hidden, w_down[...], preferred_element_type=jnp.float32)
    keep[...] = partial[:24]
    send[...] = partial[24:].astype(jnp.bfloat16)
    mine = jnp.dot(pick[0:16], projected, preferred_element_type=jnp.float32)[0:3]
    residual_out[...] = own[...].astype(jnp.float32) + gate * mine


def add_near(keep, got, keep_out, send_out):
    total = keep[...] + got[...].astype(jnp.float32)
    keep_out[...] = total[:12]
    send_out[...] = total[12:].astype(jnp.bfloat16)


def add_plane(keep, got, keep_out, send1, send2, send3):
    total = keep[...] + got[...].astype(jnp.float32)
    keep_out[...] = total[0:3]
    for z, send in ((1, send1), (2, send2), (3, send3)):
        send[...] = total[3 * z : 3 * z + 3].astype(jnp.bfloat16)


def finish(keep, got1, got2, got3, residual, mod, out):
    total = keep[...]
    for got in (got1, got2, got3):
        total = total + got[...].astype(jnp.float32)
    out[...] = (residual[...] + mod[5:6, :] * total).astype(jnp.bfloat16)


def staged(tokens, modulation, w_qkv, norm_gains, cache_kv, w_out, w_up, w_down):
    f32, bf16 = jnp.float32, jnp.bfloat16
    w_qkv = load(jnp.swapaxes(w_qkv, 1, 2).reshape(480, 5120))

    def after_load(pieces):
        nonlocal w_qkv
        *pieces, w_qkv = lax.optimization_barrier((*pieces, w_qkv))
        return pieces

    token_stacks = gather(tokens, after_load)
    cache_stacks = gather(cache_kv.transpose(0, 2, 1, 3))
    all_tokens, qkv = call(
        project_qkv,
        [((48, 5120), bf16), ((48, 480), bf16)],
        *token_stacks,
        modulation,
        w_qkv,
        scratch=[pltpu.VMEM((16, 3, 5120), bf16), pltpu.VMEM((48, 5120), f32)],
        flops=2 * 48 * 5120 * 480,
    )
    old_keys, old_values = call(
        line_up, [((96, 2560), bf16)] * 2, *cache_stacks, scratch=[pltpu.VMEM((96, 2560), f32)] * 2, moved=8 << 20
    )
    projected = call(
        attend,
        [((48, 320), bf16)],
        *gather(qkv),
        old_keys,
        old_values,
        norm_gains,
        w_out.T,
        scratch=[pltpu.VMEM((16, 48, 480), bf16), pltpu.VMEM((48, 2560), bf16)],
        flops=2 * 48 * 2560 * 608,
    )[0]
    w_up, w_down = load(w_up.T), load(w_down)

    def after_loads(pieces):
        nonlocal w_up, w_down
        *pieces, w_up, w_down = lax.optimization_barrier((*pieces, w_up, w_down))
        return pieces

    keep, send, residual = call(
        feed_forward,
        [((24, 5120), f32), ((24, 5120), bf16), ((3, 5120), f32)],
        *gather(projected, after_loads),
        all_tokens,
        tokens,
        modulation,
        w_up,
        w_down,
        scratch=[pltpu.VMEM((16, 48, 320), bf16)],
        flops=4 * 48 * 5120 * 864,
    )
    keep, send = call(add_near, [((12, 5120), f32), ((12, 5120), bf16)], keep, swap(send, 1))
    keep, *sends = call(add_plane, [((3, 5120), f32)] + [((3, 5120), bf16)] * 3, keep, swap(send, 2))
    got = [swap(send, 4 * z) for z, send in zip((1, 2, 3), sends)]
    return call(finish, [((3, 5120), bf16)], keep, *got, residual, modulation)[0]


def general(tokens, modulation, w_qkv, norm_gains, cache_kv, w_out, w_up, w_down):
    own_rows = tokens.shape[0]
    width = HEADS * HEAD_DIM
    scale = 1.0 / math.sqrt(HEAD_DIM)
    residual = tokens.astype(jnp.float32)
    normed = (layer_norm(residual) * (1.0 + modulation[1]) + modulation[0]).astype(jnp.bfloat16)
    qkv_cols = jnp.einsum(
        "td,kda->kta",
        lax.all_gather(normed, "seq", axis=0, tiled=True),
        w_qkv,
        preferred_element_type=jnp.float32,
    ).astype(jnp.bfloat16)
    qkv = lax.all_to_all(qkv_cols, "seq", split_axis=1, concat_axis=2, tiled=True)
    queries = rms_norm(qkv[0].astype(jnp.float32), norm_gains[0]).astype(jnp.bfloat16)
    keys_now = rms_norm(qkv[1].astype(jnp.float32), norm_gains[1]).astype(jnp.bfloat16)
    local_keys = jnp.concatenate([cache_kv[0].reshape(-1, width), keys_now], axis=0)
    local_values = jnp.concatenate([cache_kv[1].reshape(-1, width), qkv[2]], axis=0)
    query_heads = queries.reshape(own_rows, HEADS, HEAD_DIM)
    peak_old = jnp.full((own_rows, HEADS), -1e30, jnp.float32)
    key_piece = lax.all_gather(local_keys, "seq", axis=0, tiled=True)
    value_piece = lax.all_gather(local_values, "seq", axis=0, tiled=True)
    count = key_piece.shape[0]
    scores = (
        jnp.einsum(
            "qhd,khd->qhk",
            query_heads,
            key_piece.reshape(count, HEADS, HEAD_DIM),
            preferred_element_type=jnp.float32,
        )
        * scale
    )
    peak_new = jnp.maximum(peak_old, jnp.max(scores, axis=-1))
    expo = jnp.exp(scores - peak_new[..., None])
    total_new = jnp.sum(expo, axis=-1)
    weights = expo.astype(jnp.bfloat16)
    summed_new = jnp.einsum(
        "qhk,khd->qhd",
        weights,
        value_piece.reshape(count, HEADS, HEAD_DIM),
        preferred_element_type=jnp.float32,
    )
    attended = (summed_new / total_new[..., None]).reshape(own_rows, width).astype(jnp.bfloat16)
    projected_cols = jnp.dot(
        lax.all_gather(attended, "seq", axis=0, tiled=True),
        w_out,
        preferred_element_type=jnp.float32,
    ).astype(jnp.bfloat16)
    projected = lax.all_to_all(projected_cols, "seq", split_axis=0, concat_axis=1, tiled=True)
    residual = residual + modulation[2] * projected.astype(jnp.float32)
    normed2 = (layer_norm(residual) * (1.0 + modulation[4]) + modulation[3]).astype(jnp.bfloat16)
    hidden = jax.nn.gelu(
        jnp.dot(
            lax.all_gather(normed2, "seq", axis=0, tiled=True),
            w_up,
            preferred_element_type=jnp.float32,
        ),
        approximate=True,
    ).astype(jnp.bfloat16)
    feed = lax.psum_scatter(
        jnp.dot(hidden, w_down, preferred_element_type=jnp.float32),
        "seq",
        scatter_dimension=0,
        tiled=True,
    )
    return (residual + modulation[5] * feed).astype(jnp.bfloat16)


def solution(mesh):
    in_specs = (
        P(("groups", "seq"), None),
        P(),
        P(None, None, "seq"),
        P(),
        P(None, None, ("groups", "seq"), None),
        P(None, "seq"),
        P(None, "seq"),
        P("seq", None),
    )
    out_specs = P(("groups", "seq"), None)
    local = staged if mesh.shape["seq"] == 16 else general
    return jax.shard_map(local, mesh=mesh, in_specs=in_specs, out_specs=out_specs, check_vma=False)
```

```python
import math

import jax
import jax.numpy as jnp
from jax import lax
from jax.experimental import pallas as pl
from jax.experimental.pallas import tpu as pltpu
from jax.sharding import PartitionSpec as P

HEAD_DIM = 128
HEADS = 20


def layer_norm(values):
    center = values - jnp.mean(values, axis=-1, keepdims=True)
    spread = jnp.mean(center * center, axis=-1, keepdims=True)
    return center * lax.rsqrt(spread + 1e-06)


def rms_norm(values, gain):
    return values * lax.rsqrt(jnp.mean(values * values, axis=-1, keepdims=True) + 1e-06) * gain


VMEM = pl.BlockSpec(memory_space=pltpu.VMEM)
HBM = pl.BlockSpec(memory_space=pltpu.HBM)
NT = (((1,), (1,)), ((), ()))


def call(body, outs, *operands, spec=VMEM, scratch=(), limit=24):
    return pl.pallas_call(
        body,
        out_shape=[jax.ShapeDtypeStruct(shape, dtype) for shape, dtype in outs],
        in_specs=[spec] * len(operands),
        out_specs=[VMEM] * len(outs),
        scratch_shapes=list(scratch),
        compiler_params=pltpu.CompilerParams(vmem_limit_bytes=limit << 20),
        cost_estimate=pl.CostEstimate(flops=0, bytes_accessed=0, transcendentals=0),
    )(*operands)


def load(*arrays):
    parts = []
    for i, array in enumerate(arrays):
        rows = array.shape[0]
        if array.size < 1 << 20:
            parts.append((i, None))
        else:
            cuts = [rows * k // 4 // 16 * 16 for k in range(4)] + [rows]
            parts += [(i, pl.ds(lo, hi - lo)) for lo, hi in zip(cuts, cuts[1:])]

    def body(*refs):
        sources, targets, sems = refs[: len(arrays)], refs[len(arrays) : -1], refs[-1]
        copies = []
        for n, (i, cut) in enumerate(parts):
            source, target = (sources[i], targets[i]) if cut is None else (sources[i].at[cut], targets[i].at[cut])
            copies.append(pltpu.make_async_copy(source, target, sems.at[n]))
        for copy in copies:
            copy.start()
        for copy in copies:
            copy.wait()

    outs = [(array.shape, array.dtype) for array in arrays]
    arrays = [pltpu.with_memory_space_constraint(array, pltpu.HBM) for array in arrays]
    return call(body, outs, *arrays, spec=HBM, scratch=[pltpu.SemaphoreType.DMA((len(parts),))])


def swap(values, offset):
    return lax.ppermute(values, "seq", [(i, i ^ offset) for i in range(16)])


def stack(pieces):
    def body(*refs):
        for i, ref in enumerate(refs[:-1]):
            refs[-1][i] = ref[...]

    return call(body, [((len(pieces), *pieces[0].shape), pieces[0].dtype)], *pieces)[0]


def load_beside(weights, before, beside):
    weights, _ = lax.optimization_barrier((weights, before))
    return lax.optimization_barrier((load(weights)[0], beside))


def gather(block, load_z=None, load_y=None):
    pieces = tuple(swap(block, 4 * z) for z in (1, 2, 3))
    if load_z is not None:
        load_z, pieces = load_beside(load_z, block, pieces)
    planes = stack([block, *pieces])
    across = swap(planes, 2)
    if load_y is not None:
        load_y, across = load_beside(load_y, planes, across)
    return [planes, across, swap(planes, 1), swap(across, 1)], load_z, load_y


def apart(slot, z):
    return 4 * z + 2 * (slot & 1) + (slot >> 1)


def place(stacks, target):
    me = lax.axis_index("seq")
    for slot, ref in enumerate(stacks):
        for z in range(4):
            target[me ^ apart(slot, z)] = ref[z]


def normalize(values, shift, gain):
    return (layer_norm(values) * (1.0 + gain) + shift).astype(jnp.bfloat16)


def project_qkv(s0, s1, s2, s3, mod, weights, tokens_out, qkv_out, slots, flat):
    place((s0, s1, s2, s3), slots)
    for j in range(16):
        flat[3 * j : 3 * j + 3, :] = slots[j].astype(jnp.float32)
    tokens = flat[...]
    tokens_out[...] = tokens.astype(jnp.bfloat16)
    normed = normalize(tokens, mod[0:1, :], mod[1:2, :])
    qkv_out[...] = lax.dot_general(normed, weights[...], NT, preferred_element_type=jnp.float32).astype(jnp.bfloat16)


def line_up(s0, s1, s2, s3, keys_out, values_out, keys, values):
    for slot, ref in enumerate((s0, s1, s2, s3)):
        for z in range(4):
            for token in range(3):
                row = 6 * (4 * slot + z) + 2 * token
                keys[row : row + 2, :] = ref[z, 0, token].astype(jnp.float32)
                values[row : row + 2, :] = ref[z, 1, token].astype(jnp.float32)
    keys_out[...] = keys[...].astype(jnp.bfloat16)
    values_out[...] = values[...].astype(jnp.bfloat16)


def attend(s0, s1, s2, s3, old_keys, old_values, gains, weights, out, slots, attended):
    place((s0, s1, s2, s3), slots)
    pieces = [slots[j].astype(jnp.float32) for j in range(16)]
    queries, keys, values = (
        jnp.concatenate([piece[:, 160 * i : 160 * i + 160] for piece in pieces], axis=1) for i in range(3)
    )
    queries = rms_norm(queries, gains[0:1, :]).astype(jnp.bfloat16)
    keys = jnp.concatenate([old_keys[...], rms_norm(keys, gains[1:2, :]).astype(jnp.bfloat16)], axis=0)
    values = jnp.concatenate([old_values[...], values.astype(jnp.bfloat16)], axis=0)
    for head in range(HEADS):
        cols = slice(HEAD_DIM * head, HEAD_DIM * (head + 1))
        scores = lax.dot_general(queries[:, cols], keys[:, cols], NT, preferred_element_type=jnp.float32)
        scores = scores * (1.0 / math.sqrt(HEAD_DIM))
        expo = jnp.exp(scores - jnp.max(scores, axis=-1, keepdims=True))
        total = jnp.sum(expo, axis=-1, keepdims=True)
        summed = jnp.dot(expo.astype(jnp.bfloat16), values[:, cols], preferred_element_type=jnp.float32)
        attended[:, cols] = (summed / total).astype(jnp.bfloat16)
    out[...] = lax.dot_general(attended[...], weights[...], NT, preferred_element_type=jnp.float32).astype(jnp.bfloat16)


def feed_forward(s0, s1, s2, s3, tokens, own, mod, w_up, w_down, keep, send, residual_out, slots):
    place((s0, s1, s2, s3), slots)
    projected = jnp.concatenate([slots[j] for j in range(16)], axis=1)
    gate = mod[2:3, :]
    residual = tokens[...].astype(jnp.float32) + gate * projected.astype(jnp.float32)
    normed = normalize(residual, mod[3:4, :], mod[4:5, :])
    hidden = lax.dot_general(normed, w_up[...], NT, preferred_element_type=jnp.float32)
    hidden = jax.nn.gelu(hidden, approximate=True).astype(jnp.bfloat16)
    me = lax.axis_index("seq")
    row = lax.broadcasted_iota(jnp.int32, (48, 48), 0)
    token = lax.broadcasted_iota(jnp.int32, (48, 48), 1)
    block = (row * 171) >> 9
    device = me ^ (4 * (block & 3) + 2 * ((block >> 2) & 1) + (block >> 3))
    pick = (token == 3 * device + row - 3 * block).astype(jnp.bfloat16)
    hidden = jnp.dot(pick, hidden, preferred_element_type=jnp.float32).astype(jnp.bfloat16)
    partial = jnp.dot(hidden, w_down[...], preferred_element_type=jnp.float32)
    keep[...] = partial[:24]
    send[...] = partial[24:].astype(jnp.bfloat16)
    mine = jnp.dot(pick[0:16], projected, preferred_element_type=jnp.float32)[0:3]
    residual_out[...] = own[...].astype(jnp.float32) + gate * mine


def add_near(keep, got, keep_out, send_out):
    total = keep[...] + got[...].astype(jnp.float32)
    keep_out[...] = total[:12]
    send_out[...] = total[12:].astype(jnp.bfloat16)


def add_plane(keep, got, keep_out, send1, send2, send3):
    total = keep[...] + got[...].astype(jnp.float32)
    keep_out[...] = total[0:3]
    for z, send in ((1, send1), (2, send2), (3, send3)):
        send[...] = total[3 * z : 3 * z + 3].astype(jnp.bfloat16)


def finish(keep, got1, got2, got3, residual, mod, out):
    total = keep[...]
    for got in (got1, got2, got3):
        total = total + got[...].astype(jnp.float32)
    out[...] = (residual[...] + mod[5:6, :] * total).astype(jnp.bfloat16)


def staged(tokens, modulation, w_qkv, norm_gains, cache_kv, w_out, w_up, w_down):
    f32, bf16 = jnp.float32, jnp.bfloat16
    w_qkv = jnp.swapaxes(w_qkv, 1, 2).reshape(480, 5120)
    cache_kv = cache_kv.transpose(0, 2, 1, 3)
    pieces = tuple(swap(tokens, 4 * z) for z in (1, 2, 3))
    cache_pieces = tuple(swap(cache_kv, 4 * z) for z in (1, 2, 3))
    tokens, modulation, norm_gains, cache_kv, w_qkv = load(tokens, modulation, norm_gains, cache_kv, w_qkv)
    pieces, tokens = lax.optimization_barrier((pieces, tokens))
    planes = stack([tokens, *pieces])
    across = swap(planes, 2)
    cache_planes = stack([cache_kv, *cache_pieces])
    across, cache_planes = lax.optimization_barrier((across, cache_planes))
    cache_across = swap(cache_planes, 2)
    all_tokens, qkv = call(
        project_qkv,
        [((48, 5120), bf16), ((48, 480), bf16)],
        planes,
        across,
        swap(planes, 1),
        swap(across, 1),
        modulation,
        w_qkv,
        scratch=[pltpu.VMEM((16, 3, 5120), bf16), pltpu.VMEM((48, 5120), f32)],
    )
    qkv_stacks, w_out, w_up = gather(qkv, w_out.T, w_up.T)
    old_keys, old_values = call(
        line_up,
        [((96, 2560), bf16)] * 2,
        cache_planes,
        cache_across,
        swap(cache_planes, 1),
        swap(cache_across, 1),
        scratch=[pltpu.VMEM((96, 2560), f32)] * 2,
    )
    projected = call(
        attend,
        [((48, 320), bf16)],
        *qkv_stacks,
        old_keys,
        old_values,
        norm_gains,
        w_out,
        scratch=[pltpu.VMEM((16, 48, 480), bf16), pltpu.VMEM((48, 2560), bf16)],
    )[0]
    projected_stacks, _, w_down = gather(projected, None, w_down)
    keep, send, residual = call(
        feed_forward,
        [((24, 5120), f32), ((24, 5120), bf16), ((3, 5120), f32)],
        *projected_stacks,
        all_tokens,
        tokens,
        modulation,
        w_up,
        w_down,
        scratch=[pltpu.VMEM((16, 48, 320), bf16)],
    )
    keep, send = call(add_near, [((12, 5120), f32), ((12, 5120), bf16)], keep, swap(send, 1))
    keep, *sends = call(add_plane, [((3, 5120), f32)] + [((3, 5120), bf16)] * 3, keep, swap(send, 2))
    got = [swap(send, 4 * z) for z, send in zip((1, 2, 3), sends)]
    return call(finish, [((3, 5120), bf16)], keep, *got, residual, modulation)[0]


def general(tokens, modulation, w_qkv, norm_gains, cache_kv, w_out, w_up, w_down):
    own_rows = tokens.shape[0]
    width = HEADS * HEAD_DIM
    scale = 1.0 / math.sqrt(HEAD_DIM)
    residual = tokens.astype(jnp.float32)
    normed = (layer_norm(residual) * (1.0 + modulation[1]) + modulation[0]).astype(jnp.bfloat16)
    qkv_cols = jnp.einsum(
        "td,kda->kta",
        lax.all_gather(normed, "seq", axis=0, tiled=True),
        w_qkv,
        preferred_element_type=jnp.float32,
    ).astype(jnp.bfloat16)
    qkv = lax.all_to_all(qkv_cols, "seq", split_axis=1, concat_axis=2, tiled=True)
    queries = rms_norm(qkv[0].astype(jnp.float32), norm_gains[0]).astype(jnp.bfloat16)
    keys_now = rms_norm(qkv[1].astype(jnp.float32), norm_gains[1]).astype(jnp.bfloat16)
    local_keys = jnp.concatenate([cache_kv[0].reshape(-1, width), keys_now], axis=0)
    local_values = jnp.concatenate([cache_kv[1].reshape(-1, width), qkv[2]], axis=0)
    query_heads = queries.reshape(own_rows, HEADS, HEAD_DIM)
    peak_old = jnp.full((own_rows, HEADS), -1e30, jnp.float32)
    key_piece = lax.all_gather(local_keys, "seq", axis=0, tiled=True)
    value_piece = lax.all_gather(local_values, "seq", axis=0, tiled=True)
    count = key_piece.shape[0]
    scores = (
        jnp.einsum(
            "qhd,khd->qhk",
            query_heads,
            key_piece.reshape(count, HEADS, HEAD_DIM),
            preferred_element_type=jnp.float32,
        )
        * scale
    )
    peak_new = jnp.maximum(peak_old, jnp.max(scores, axis=-1))
    expo = jnp.exp(scores - peak_new[..., None])
    total_new = jnp.sum(expo, axis=-1)
    weights = expo.astype(jnp.bfloat16)
    summed_new = jnp.einsum(
        "qhk,khd->qhd",
        weights,
        value_piece.reshape(count, HEADS, HEAD_DIM),
        preferred_element_type=jnp.float32,
    )
    attended = (summed_new / total_new[..., None]).reshape(own_rows, width).astype(jnp.bfloat16)
    projected_cols = jnp.dot(
        lax.all_gather(attended, "seq", axis=0, tiled=True),
        w_out,
        preferred_element_type=jnp.float32,
    ).astype(jnp.bfloat16)
    projected = lax.all_to_all(projected_cols, "seq", split_axis=0, concat_axis=1, tiled=True)
    residual = residual + modulation[2] * projected.astype(jnp.float32)
    normed2 = (layer_norm(residual) * (1.0 + modulation[4]) + modulation[3]).astype(jnp.bfloat16)
    hidden = jax.nn.gelu(
        jnp.dot(
            lax.all_gather(normed2, "seq", axis=0, tiled=True),
            w_up,
            preferred_element_type=jnp.float32,
        ),
        approximate=True,
    ).astype(jnp.bfloat16)
    feed = lax.psum_scatter(
        jnp.dot(hidden, w_down, preferred_element_type=jnp.float32),
        "seq",
        scatter_dimension=0,
        tiled=True,
    )
    return (residual + modulation[5] * feed).astype(jnp.bfloat16)


def solution(mesh):
    in_specs = (
        P(("groups", "seq"), None),
        P(),
        P(None, None, "seq"),
        P(),
        P(None, None, ("groups", "seq"), None),
        P(None, "seq"),
        P(None, "seq"),
        P("seq", None),
    )
    out_specs = P(("groups", "seq"), None)
    local = staged if mesh.shape["seq"] == 16 else general
    return jax.shard_map(local, mesh=mesh, in_specs=in_specs, out_specs=out_specs, check_vma=False)
```

```python
import math

import jax
import jax.numpy as jnp
from jax import lax
from jax.experimental import pallas as pl
from jax.experimental.pallas import tpu as pltpu
from jax.sharding import PartitionSpec as P

HEAD_DIM = 128
HEADS = 20


def layer_norm(values):
    center = values - jnp.mean(values, axis=-1, keepdims=True)
    spread = jnp.mean(center * center, axis=-1, keepdims=True)
    return center * lax.rsqrt(spread + 1e-06)


def rms_norm(values, gain):
    return values * lax.rsqrt(jnp.mean(values * values, axis=-1, keepdims=True) + 1e-06) * gain


VMEM = pl.BlockSpec(memory_space=pltpu.VMEM)
HBM = pl.BlockSpec(memory_space=pltpu.HBM)
NT = (((1,), (1,)), ((), ()))


def call(body, outs, *operands, spec=VMEM, scratch=(), limit=24):
    return pl.pallas_call(
        body,
        out_shape=[jax.ShapeDtypeStruct(shape, dtype) for shape, dtype in outs],
        in_specs=[spec] * len(operands),
        out_specs=[VMEM] * len(outs),
        scratch_shapes=list(scratch),
        compiler_params=pltpu.CompilerParams(vmem_limit_bytes=limit << 20),
        cost_estimate=pl.CostEstimate(flops=0, bytes_accessed=0, transcendentals=0),
    )(*operands)


def load(*arrays):
    parts = []
    for i, array in enumerate(arrays):
        rows = array.shape[0]
        if array.size < 1 << 20:
            parts.append((i, None))
        else:
            cuts = [rows * k // 4 // 16 * 16 for k in range(4)] + [rows]
            parts += [(i, pl.ds(lo, hi - lo)) for lo, hi in zip(cuts, cuts[1:])]

    def body(*refs):
        sources, targets, sems = refs[: len(arrays)], refs[len(arrays) : -1], refs[-1]
        copies = []
        for n, (i, cut) in enumerate(parts):
            source, target = (sources[i], targets[i]) if cut is None else (sources[i].at[cut], targets[i].at[cut])
            copies.append(pltpu.make_async_copy(source, target, sems.at[n]))
        for copy in copies:
            copy.start()
        for copy in copies:
            copy.wait()

    outs = [(array.shape, array.dtype) for array in arrays]
    arrays = [pltpu.with_memory_space_constraint(array, pltpu.HBM) for array in arrays]
    return call(body, outs, *arrays, spec=HBM, scratch=[pltpu.SemaphoreType.DMA((len(parts),))])


def swap(values, offset):
    return lax.ppermute(values, "seq", [(i, i ^ offset) for i in range(16)])


def stack(pieces):
    def body(*refs):
        for i, ref in enumerate(refs[:-1]):
            refs[-1][i] = ref[...]

    return call(body, [((len(pieces), *pieces[0].shape), pieces[0].dtype)], *pieces)[0]


def load_beside(weights, before, beside):
    weights, _ = lax.optimization_barrier((weights, before))
    return lax.optimization_barrier((load(weights)[0], beside))


def gather(block, load_z=None, load_y=None):
    pieces = tuple(swap(block, 4 * z) for z in (1, 2, 3))
    if load_z is not None:
        load_z, pieces = load_beside(load_z, block, pieces)
    planes = stack([block, *pieces])
    across = swap(planes, 2)
    if load_y is not None:
        load_y, across = load_beside(load_y, planes, across)
    return [planes, across, swap(planes, 1), swap(across, 1)], load_z, load_y


def pack_tokens(own, got1, got2, got3, out, rows):
    for z, ref in enumerate((own, got1, got2, got3)):
        for half in range(2):
            row = 12 * half + 3 * z
            rows[row : row + 3, :] = ref[:, 2560 * half : 2560 * half + 2560].astype(jnp.float32)
    out[...] = rows[...].astype(jnp.bfloat16)


def place(stacks, target):
    me = lax.axis_index("seq")
    for slot, ref in enumerate(stacks):
        for z in range(4):
            target[me ^ (4 * z + 2 * (slot & 1) + (slot >> 1))] = ref[z]


def order(near_axis):
    near = lax.broadcasted_iota(jnp.int32, (48, 48), near_axis)
    token = lax.broadcasted_iota(jnp.int32, (48, 48), 1 - near_axis)
    block = (near * 171) >> 9
    device = lax.axis_index("seq") ^ (4 * (block & 3) + 2 * ((block >> 2) & 1) + (block >> 3))
    return (token == 3 * device + near - 3 * block).astype(jnp.bfloat16)


def normalize(values, shift, gain):
    return (layer_norm(values) * (1.0 + gain) + shift).astype(jnp.bfloat16)


def project_qkv(s0, s1, s2, s3, mod, weights, tokens_out, qkv_out, flat):
    for slot, ref in enumerate((s0, s1, s2, s3)):
        for half in range(2):
            piece = ref[12 * half : 12 * half + 12, :].astype(jnp.float32)
            flat[12 * slot : 12 * slot + 12, 2560 * half : 2560 * half + 2560] = piece
    tokens = flat[...]
    tokens_out[...] = tokens.astype(jnp.bfloat16)
    normed = normalize(tokens, mod[0:1, :], mod[1:2, :])
    qkv = lax.dot_general(normed, weights[...], NT, preferred_element_type=jnp.float32).astype(jnp.bfloat16)
    qkv_out[...] = jnp.dot(order(1), qkv, preferred_element_type=jnp.float32).astype(jnp.bfloat16)


def line_up(s0, s1, s2, s3, keys_out, values_out, keys, values):
    for slot, ref in enumerate((s0, s1, s2, s3)):
        for z in range(4):
            for token in range(3):
                row = 6 * (4 * slot + z) + 2 * token
                keys[row : row + 2, :] = ref[z, 0, token].astype(jnp.float32)
                values[row : row + 2, :] = ref[z, 1, token].astype(jnp.float32)
    keys_out[...] = keys[...].astype(jnp.bfloat16)
    values_out[...] = values[...].astype(jnp.bfloat16)


def attend(s0, s1, s2, s3, old_keys, old_values, gains, weights, out, slots, scores, expos, attended):
    place((s0, s1, s2, s3), slots)
    pieces = [slots[j] for j in range(16)]
    queries, keys, values = (
        jnp.concatenate([piece[:, 160 * i : 160 * i + 160] for piece in pieces], axis=1) for i in range(3)
    )
    queries = rms_norm(queries.astype(jnp.float32), gains[0:1, :]).astype(jnp.bfloat16)
    keys = rms_norm(keys.astype(jnp.float32), gains[1:2, :]).astype(jnp.bfloat16)
    keys = jnp.concatenate([old_keys[...], keys], axis=0)
    values = jnp.concatenate([old_values[...], values], axis=0)
    none = jnp.zeros((48, HEAD_DIM), jnp.bfloat16)
    pairs = []
    for head in range(0, HEADS, 2):
        first, second = (slice(HEAD_DIM * h, HEAD_DIM * (h + 1)) for h in (head, head + 1))
        pairs.append((slice(48 * head, 48 * (head + 2)), first, second, slice(HEAD_DIM * head, HEAD_DIM * (head + 2))))
    for rows, first, second, both in pairs:
        upper = jnp.concatenate([queries[:, first], none], axis=1)
        lower = jnp.concatenate([none, queries[:, second]], axis=1)
        diagonal = jnp.concatenate([upper, lower], axis=0)
        scores[rows, :] = lax.dot_general(diagonal, keys[:, both], NT, preferred_element_type=jnp.float32)
    scaled = scores[...] * (1.0 / math.sqrt(HEAD_DIM))
    expo = jnp.exp(scaled - jnp.max(scaled, axis=-1, keepdims=True))
    total = jnp.sum(expo, axis=-1, keepdims=True)
    expos[...] = expo.astype(jnp.bfloat16)
    for rows, first, second, both in pairs:
        summed = jnp.dot(expos[rows, :], values[:, both], preferred_element_type=jnp.float32) / total[rows]
        attended[:, first] = summed[:48, :HEAD_DIM].astype(jnp.bfloat16)
        attended[:, second] = summed[48:, HEAD_DIM:].astype(jnp.bfloat16)
    projected = lax.dot_general(attended[...], weights[...], NT, preferred_element_type=jnp.float32)
    out[...] = jnp.concatenate([projected[:24], projected[24:]], axis=1).astype(jnp.bfloat16)


def feed_forward(s0, s1, s2, s3, tokens, mod, w_up, w_down, keep, send, residual_out, slots):
    place((s0, s1, s2, s3), slots)
    pieces = [slots[j] for j in range(16)]
    upper = jnp.concatenate([piece[:, :320] for piece in pieces], axis=1)
    lower = jnp.concatenate([piece[:, 320:] for piece in pieces], axis=1)
    projected = jnp.concatenate([upper, lower], axis=0)
    projected = jnp.dot(order(0), projected, preferred_element_type=jnp.float32)
    residual = tokens[...].astype(jnp.float32) + mod[2:3, :] * projected
    residual_out[...] = residual[0:3]
    normed = normalize(residual, mod[3:4, :], mod[4:5, :])
    hidden = lax.dot_general(normed, w_up[...], NT, preferred_element_type=jnp.float32)
    hidden = jax.nn.gelu(hidden, approximate=True).astype(jnp.bfloat16)
    partial = jnp.dot(hidden, w_down[...], preferred_element_type=jnp.float32)
    keep[...] = partial[:24]
    send[...] = partial[24:].astype(jnp.bfloat16)


def add_near(keep, got, keep_out, send_out):
    total = keep[...] + got[...].astype(jnp.float32)
    keep_out[...] = total[:12]
    send_out[...] = jnp.concatenate([total[12:, :2560], total[12:, 2560:]], axis=0).astype(jnp.bfloat16)


def add_plane(keep, got, keep_out, send1, send2, send3):
    got = got[...].astype(jnp.float32)
    total = keep[...] + jnp.concatenate([got[:12], got[12:]], axis=1)
    keep_out[...] = total[0:3]
    for z, send in ((1, send1), (2, send2), (3, send3)):
        rows = [total[3 * z + i : 3 * z + i + 1, 640 * g : 640 * g + 640] for i in range(3) for g in range(8)]
        send[...] = jnp.concatenate(rows, axis=0).astype(jnp.bfloat16)


def finish(keep, got1, got2, got3, residual, mod, out):
    total = got1[...].astype(jnp.float32) + got2[...].astype(jnp.float32) + got3[...].astype(jnp.float32)
    rows = [jnp.concatenate([total[8 * i + g : 8 * i + g + 1] for g in range(8)], axis=1) for i in range(3)]
    total = keep[...] + jnp.concatenate(rows, axis=0)
    out[...] = (residual[...] + mod[5:6, :] * total).astype(jnp.bfloat16)


def staged(tokens, modulation, w_qkv, norm_gains, cache_kv, w_out, w_up, w_down):
    f32, bf16 = jnp.float32, jnp.bfloat16
    w_qkv = jnp.swapaxes(w_qkv, 1, 2).reshape(480, 5120)
    cache_kv = cache_kv.transpose(0, 2, 1, 3)
    pieces = tuple(swap(tokens, 4 * z) for z in (1, 2, 3))
    cache_pieces = tuple(swap(cache_kv, 4 * z) for z in (1, 2, 3))
    tokens, modulation, norm_gains, cache_kv, w_qkv = load(tokens, modulation, norm_gains, cache_kv, w_qkv)
    pieces, tokens = lax.optimization_barrier((pieces, tokens))
    planes = call(pack_tokens, [((24, 2560), bf16)], tokens, *pieces, scratch=[pltpu.VMEM((24, 2560), f32)])[0]
    across = swap(planes, 2)
    cache_planes = stack([cache_kv, *cache_pieces])
    across, cache_planes = lax.optimization_barrier((across, cache_planes))
    cache_across = swap(cache_planes, 2)
    near_tokens, qkv = call(
        project_qkv,
        [((48, 5120), bf16), ((48, 480), bf16)],
        planes,
        across,
        swap(planes, 1),
        swap(across, 1),
        modulation,
        w_qkv,
        scratch=[pltpu.VMEM((48, 5120), f32)],
    )
    qkv_stacks, w_out, w_up = gather(qkv, w_out.T, w_up.T)
    old_keys, old_values = call(
        line_up,
        [((96, 2560), bf16)] * 2,
        cache_planes,
        cache_across,
        swap(cache_planes, 1),
        swap(cache_across, 1),
        scratch=[pltpu.VMEM((96, 2560), f32)] * 2,
    )
    projected = call(
        attend,
        [((24, 640), bf16)],
        *qkv_stacks,
        old_keys,
        old_values,
        norm_gains,
        w_out,
        scratch=[
            pltpu.VMEM((16, 48, 480), bf16),
            pltpu.VMEM((48 * HEADS, 144), f32),
            pltpu.VMEM((48 * HEADS, 144), bf16),
            pltpu.VMEM((48, 2560), bf16),
        ],
    )[0]
    projected_stacks, _, w_down = gather(projected, None, w_down)
    keep, send, residual = call(
        feed_forward,
        [((24, 5120), f32), ((24, 5120), bf16), ((3, 5120), f32)],
        *projected_stacks,
        near_tokens,
        modulation,
        w_up,
        w_down,
        scratch=[pltpu.VMEM((16, 24, 640), bf16)],
    )
    keep, send = call(add_near, [((12, 5120), f32), ((24, 2560), bf16)], keep, swap(send, 1))
    keep, *sends = call(add_plane, [((3, 5120), f32)] + [((24, 640), bf16)] * 3, keep, swap(send, 2))
    got = [swap(send, 4 * z) for z, send in zip((1, 2, 3), sends)]
    return call(finish, [((3, 5120), bf16)], keep, *got, residual, modulation)[0]


def general(tokens, modulation, w_qkv, norm_gains, cache_kv, w_out, w_up, w_down):
    own_rows = tokens.shape[0]
    width = HEADS * HEAD_DIM
    scale = 1.0 / math.sqrt(HEAD_DIM)
    residual = tokens.astype(jnp.float32)
    normed = (layer_norm(residual) * (1.0 + modulation[1]) + modulation[0]).astype(jnp.bfloat16)
    qkv_cols = jnp.einsum(
        "td,kda->kta",
        lax.all_gather(normed, "seq", axis=0, tiled=True),
        w_qkv,
        preferred_element_type=jnp.float32,
    ).astype(jnp.bfloat16)
    qkv = lax.all_to_all(qkv_cols, "seq", split_axis=1, concat_axis=2, tiled=True)
    queries = rms_norm(qkv[0].astype(jnp.float32), norm_gains[0]).astype(jnp.bfloat16)
    keys_now = rms_norm(qkv[1].astype(jnp.float32), norm_gains[1]).astype(jnp.bfloat16)
    local_keys = jnp.concatenate([cache_kv[0].reshape(-1, width), keys_now], axis=0)
    local_values = jnp.concatenate([cache_kv[1].reshape(-1, width), qkv[2]], axis=0)
    query_heads = queries.reshape(own_rows, HEADS, HEAD_DIM)
    peak_old = jnp.full((own_rows, HEADS), -1e30, jnp.float32)
    key_piece = lax.all_gather(local_keys, "seq", axis=0, tiled=True)
    value_piece = lax.all_gather(local_values, "seq", axis=0, tiled=True)
    count = key_piece.shape[0]
    scores = (
        jnp.einsum(
            "qhd,khd->qhk",
            query_heads,
            key_piece.reshape(count, HEADS, HEAD_DIM),
            preferred_element_type=jnp.float32,
        )
        * scale
    )
    peak_new = jnp.maximum(peak_old, jnp.max(scores, axis=-1))
    expo = jnp.exp(scores - peak_new[..., None])
    total_new = jnp.sum(expo, axis=-1)
    weights = expo.astype(jnp.bfloat16)
    summed_new = jnp.einsum(
        "qhk,khd->qhd",
        weights,
        value_piece.reshape(count, HEADS, HEAD_DIM),
        preferred_element_type=jnp.float32,
    )
    attended = (summed_new / total_new[..., None]).reshape(own_rows, width).astype(jnp.bfloat16)
    projected_cols = jnp.dot(
        lax.all_gather(attended, "seq", axis=0, tiled=True),
        w_out,
        preferred_element_type=jnp.float32,
    ).astype(jnp.bfloat16)
    projected = lax.all_to_all(projected_cols, "seq", split_axis=0, concat_axis=1, tiled=True)
    residual = residual + modulation[2] * projected.astype(jnp.float32)
    normed2 = (layer_norm(residual) * (1.0 + modulation[4]) + modulation[3]).astype(jnp.bfloat16)
    hidden = jax.nn.gelu(
        jnp.dot(
            lax.all_gather(normed2, "seq", axis=0, tiled=True),
            w_up,
            preferred_element_type=jnp.float32,
        ),
        approximate=True,
    ).astype(jnp.bfloat16)
    feed = lax.psum_scatter(
        jnp.dot(hidden, w_down, preferred_element_type=jnp.float32),
        "seq",
        scatter_dimension=0,
        tiled=True,
    )
    return (residual + modulation[5] * feed).astype(jnp.bfloat16)


def solution(mesh):
    in_specs = (
        P(("groups", "seq"), None),
        P(),
        P(None, None, "seq"),
        P(),
        P(None, None, ("groups", "seq"), None),
        P(None, "seq"),
        P(None, "seq"),
        P("seq", None),
    )
    out_specs = P(("groups", "seq"), None)
    local = staged if mesh.shape["seq"] == 16 else general
    return jax.shard_map(local, mesh=mesh, in_specs=in_specs, out_specs=out_specs, check_vma=False)
```

```python
import math

import jax
import jax.numpy as jnp
from jax import lax
from jax.experimental import pallas as pl
from jax.experimental.pallas import tpu as pltpu
from jax.sharding import PartitionSpec as P

HEAD_DIM = 128
HEADS = 20


def layer_norm(values):
    center = values - jnp.mean(values, axis=-1, keepdims=True)
    spread = jnp.mean(center * center, axis=-1, keepdims=True)
    return center * lax.rsqrt(spread + 1e-06)


def rms_norm(values, gain):
    return values * lax.rsqrt(jnp.mean(values * values, axis=-1, keepdims=True) + 1e-06) * gain


VMEM = pl.BlockSpec(memory_space=pltpu.VMEM)
HBM = pl.BlockSpec(memory_space=pltpu.HBM)
NT = (((1,), (1,)), ((), ()))


def call(body, outs, *operands, spec=VMEM, scratch=(), limit=24):
    return pl.pallas_call(
        body,
        out_shape=[jax.ShapeDtypeStruct(shape, dtype) for shape, dtype in outs],
        in_specs=[spec] * len(operands),
        out_specs=[VMEM] * len(outs),
        scratch_shapes=list(scratch),
        compiler_params=pltpu.CompilerParams(vmem_limit_bytes=limit << 20),
        cost_estimate=pl.CostEstimate(flops=0, bytes_accessed=0, transcendentals=0),
    )(*operands)


def load(*arrays):
    parts = []
    for i, array in enumerate(arrays):
        rows = array.shape[0]
        if array.size < 1 << 20:
            parts.append((i, None))
        else:
            cuts = [rows * k // 4 // 16 * 16 for k in range(4)] + [rows]
            parts += [(i, pl.ds(lo, hi - lo)) for lo, hi in zip(cuts, cuts[1:])]

    def body(*refs):
        sources, targets, sems = refs[: len(arrays)], refs[len(arrays) : -1], refs[-1]
        copies = []
        for n, (i, cut) in enumerate(parts):
            source, target = (sources[i], targets[i]) if cut is None else (sources[i].at[cut], targets[i].at[cut])
            copies.append(pltpu.make_async_copy(source, target, sems.at[n]))
        for copy in copies:
            copy.start()
        for copy in copies:
            copy.wait()

    outs = [(array.shape, array.dtype) for array in arrays]
    arrays = [pltpu.with_memory_space_constraint(array, pltpu.HBM) for array in arrays]
    return call(body, outs, *arrays, spec=HBM, scratch=[pltpu.SemaphoreType.DMA((len(parts),))])


def swap(values, offset):
    return lax.ppermute(values, "seq", [(i, i ^ offset) for i in range(16)])


def stack(pieces):
    def body(*refs):
        for i, ref in enumerate(refs[:-1]):
            refs[-1][i] = ref[...]

    return call(body, [((len(pieces), *pieces[0].shape), pieces[0].dtype)], *pieces)[0]


def load_beside(weights, before, beside):
    weights, _ = lax.optimization_barrier((weights, before))
    return lax.optimization_barrier((load(weights)[0], beside))


def gather(block, load_z=None, load_y=None):
    pieces = tuple(swap(block, 4 * z) for z in (1, 2, 3))
    if load_z is not None:
        load_z, pieces = load_beside(load_z, block, pieces)
    planes = stack([block, *pieces])
    across = swap(planes, 2)
    if load_y is not None:
        load_y, across = load_beside(load_y, planes, across)
    return [planes, across, swap(planes, 1), swap(across, 1)], load_z, load_y


def pack_tokens(own, got1, got2, got3, out, rows):
    for z, ref in enumerate((own, got1, got2, got3)):
        for half in range(2):
            row = 12 * half + 3 * z
            rows[row : row + 3, :] = ref[:, 2560 * half : 2560 * half + 2560].astype(jnp.float32)
    out[...] = rows[...].astype(jnp.bfloat16)


def place(stacks, target):
    me = lax.axis_index("seq")
    for slot, ref in enumerate(stacks):
        for z in range(4):
            target[me ^ (4 * z + 2 * (slot & 1) + (slot >> 1))] = ref[z]


def order(near_axis):
    near = lax.broadcasted_iota(jnp.int32, (48, 48), near_axis)
    token = lax.broadcasted_iota(jnp.int32, (48, 48), 1 - near_axis)
    block = (near * 171) >> 9
    device = lax.axis_index("seq") ^ (4 * (block & 3) + 2 * ((block >> 2) & 1) + (block >> 3))
    return (token == 3 * device + near - 3 * block).astype(jnp.bfloat16)


def normalize(values, shift, gain):
    return (layer_norm(values) * (1.0 + gain) + shift).astype(jnp.bfloat16)


def project_qkv(s0, s1, s2, s3, mod, weights, tokens_out, qkv_out, flat):
    for slot, ref in enumerate((s0, s1, s2, s3)):
        for half in range(2):
            piece = ref[12 * half : 12 * half + 12, :].astype(jnp.float32)
            flat[12 * slot : 12 * slot + 12, 2560 * half : 2560 * half + 2560] = piece
    tokens = flat[...]
    tokens_out[...] = tokens.astype(jnp.bfloat16)
    normed = normalize(tokens, mod[0:1, :], mod[1:2, :])
    qkv = lax.dot_general(normed, weights[...], NT, preferred_element_type=jnp.float32).astype(jnp.bfloat16)
    qkv_out[...] = jnp.dot(order(1), qkv, preferred_element_type=jnp.float32).astype(jnp.bfloat16)


def line_up(s0, s1, s2, s3, keys_out, values_out, keys, values):
    for slot, ref in enumerate((s0, s1, s2, s3)):
        for z in range(4):
            for token in range(3):
                row = 6 * (4 * slot + z) + 2 * token
                keys[row : row + 2, :] = ref[z, 0, token].astype(jnp.float32)
                values[row : row + 2, :] = ref[z, 1, token].astype(jnp.float32)
    keys_out[...] = keys[...].astype(jnp.bfloat16)
    values_out[...] = values[...].astype(jnp.bfloat16)


def attend(s0, s1, s2, s3, old_keys, old_values, gains, weights, out, slots, scores, expos, attended):
    place((s0, s1, s2, s3), slots)
    pieces = [slots[j] for j in range(16)]
    queries, keys, values = (
        jnp.concatenate([piece[:, 160 * i : 160 * i + 160] for piece in pieces], axis=1) for i in range(3)
    )
    queries = rms_norm(queries.astype(jnp.float32), gains[0:1, :]).astype(jnp.bfloat16)
    keys = rms_norm(keys.astype(jnp.float32), gains[1:2, :]).astype(jnp.bfloat16)
    keys = jnp.concatenate([old_keys[...], keys], axis=0)
    values = jnp.concatenate([old_values[...], values], axis=0)
    none = jnp.zeros((48, HEAD_DIM), jnp.bfloat16)
    pairs = []
    for head in range(0, HEADS, 2):
        first, second = (slice(HEAD_DIM * h, HEAD_DIM * (h + 1)) for h in (head, head + 1))
        pairs.append((slice(48 * head, 48 * (head + 2)), first, second, slice(HEAD_DIM * head, HEAD_DIM * (head + 2))))
    for rows, first, second, both in pairs:
        upper = jnp.concatenate([queries[:, first], none], axis=1)
        lower = jnp.concatenate([none, queries[:, second]], axis=1)
        diagonal = jnp.concatenate([upper, lower], axis=0)
        scores[rows, :] = lax.dot_general(diagonal, keys[:, both], NT, preferred_element_type=jnp.float32)
    scaled = scores[...] * (1.0 / math.sqrt(HEAD_DIM))
    expo = jnp.exp(scaled - jnp.max(scaled, axis=-1, keepdims=True))
    total = jnp.sum(expo, axis=-1, keepdims=True)
    expos[...] = expo.astype(jnp.bfloat16)
    for rows, first, second, both in pairs:
        summed = jnp.dot(expos[rows, :], values[:, both], preferred_element_type=jnp.float32) / total[rows]
        attended[:, first] = summed[:48, :HEAD_DIM].astype(jnp.bfloat16)
        attended[:, second] = summed[48:, HEAD_DIM:].astype(jnp.bfloat16)
    projected = lax.dot_general(attended[...], weights[...], NT, preferred_element_type=jnp.float32)
    out[...] = jnp.concatenate([projected[:24], projected[24:]], axis=1).astype(jnp.bfloat16)


def feed_forward(s0, s1, s2, s3, tokens, mod, w_up, w_down, keep, send, residual_out, slots):
    place((s0, s1, s2, s3), slots)
    pieces = [slots[j] for j in range(16)]
    upper = jnp.concatenate([piece[:, :320] for piece in pieces], axis=1)
    lower = jnp.concatenate([piece[:, 320:] for piece in pieces], axis=1)
    projected = jnp.concatenate([upper, lower], axis=0)
    projected = jnp.dot(order(0), projected, preferred_element_type=jnp.float32)
    residual = tokens[...].astype(jnp.float32) + mod[2:3, :] * projected
    residual_out[...] = residual[0:3]
    normed = normalize(residual, mod[3:4, :], mod[4:5, :])
    hidden = lax.dot_general(normed, w_up[...], NT, preferred_element_type=jnp.float32)
    hidden = jax.nn.gelu(hidden, approximate=True).astype(jnp.bfloat16)
    partial = jnp.dot(hidden, w_down[...], preferred_element_type=jnp.float32)
    keep[...] = partial[:24]
    send[...] = partial[24:].astype(jnp.bfloat16)


def add_near(keep, got, keep_out, send_out):
    total = keep[...] + got[...].astype(jnp.float32)
    keep_out[...] = total[:12]
    send_out[...] = jnp.concatenate([total[12:, :2560], total[12:, 2560:]], axis=0).astype(jnp.bfloat16)


def add_plane(keep, got, keep_out, send1, send2, send3):
    got = got[...].astype(jnp.float32)
    total = keep[...] + jnp.concatenate([got[:12], got[12:]], axis=1)
    keep_out[...] = total[0:3]
    for z, send in ((1, send1), (2, send2), (3, send3)):
        rows = [total[3 * z + i : 3 * z + i + 1, 640 * g : 640 * g + 640] for i in range(3) for g in range(8)]
        send[...] = jnp.concatenate(rows, axis=0).astype(jnp.bfloat16)


def finish(keep, got1, got2, got3, residual, mod, out):
    total = got1[...].astype(jnp.float32) + got2[...].astype(jnp.float32) + got3[...].astype(jnp.float32)
    rows = [jnp.concatenate([total[8 * i + g : 8 * i + g + 1] for g in range(8)], axis=1) for i in range(3)]
    total = keep[...] + jnp.concatenate(rows, axis=0)
    out[...] = (residual[...] + mod[5:6, :] * total).astype(jnp.bfloat16)


def staged(tokens, modulation, w_qkv, norm_gains, cache_kv, w_out, w_up, w_down):
    f32, bf16 = jnp.float32, jnp.bfloat16
    w_qkv = jnp.swapaxes(w_qkv, 1, 2).reshape(480, 5120)
    cache_kv = cache_kv.transpose(0, 2, 1, 3)
    pieces = tuple(swap(tokens, 4 * z) for z in (1, 2, 3))
    cache_far = swap(cache_kv, 8)
    tokens, modulation, norm_gains, cache_kv, w_qkv = load(tokens, modulation, norm_gains, cache_kv, w_qkv)
    pieces, tokens = lax.optimization_barrier((pieces, tokens))
    planes = call(pack_tokens, [((24, 2560), bf16)], tokens, *pieces, scratch=[pltpu.VMEM((24, 2560), f32)])[0]
    across = swap(planes, 2)
    pair = stack([cache_kv, cache_far])
    cache_planes = stack([pair, swap(pair, 4)]).reshape(4, *cache_kv.shape)
    cache_across = swap(cache_planes, 2)
    near_tokens, qkv = call(
        project_qkv,
        [((48, 5120), bf16), ((48, 480), bf16)],
        planes,
        across,
        swap(planes, 1),
        swap(across, 1),
        modulation,
        w_qkv,
        scratch=[pltpu.VMEM((48, 5120), f32)],
    )
    qkv_stacks, w_out, w_up = gather(qkv, w_out.T, w_up.T)
    old_keys, old_values = call(
        line_up,
        [((96, 2560), bf16)] * 2,
        cache_planes,
        cache_across,
        swap(cache_planes, 1),
        swap(cache_across, 1),
        scratch=[pltpu.VMEM((96, 2560), f32)] * 2,
    )
    projected = call(
        attend,
        [((24, 640), bf16)],
        *qkv_stacks,
        old_keys,
        old_values,
        norm_gains,
        w_out,
        scratch=[
            pltpu.VMEM((16, 48, 480), bf16),
            pltpu.VMEM((48 * HEADS, 144), f32),
            pltpu.VMEM((48 * HEADS, 144), bf16),
            pltpu.VMEM((48, 2560), bf16),
        ],
    )[0]
    projected_stacks, _, w_down = gather(projected, None, w_down)
    keep, send, residual = call(
        feed_forward,
        [((24, 5120), f32), ((24, 5120), bf16), ((3, 5120), f32)],
        *projected_stacks,
        near_tokens,
        modulation,
        w_up,
        w_down,
        scratch=[pltpu.VMEM((16, 24, 640), bf16)],
    )
    keep, send = call(add_near, [((12, 5120), f32), ((24, 2560), bf16)], keep, swap(send, 1))
    keep, *sends = call(add_plane, [((3, 5120), f32)] + [((24, 640), bf16)] * 3, keep, swap(send, 2))
    got = [swap(send, 4 * z) for z, send in zip((3, 2, 1), sends[::-1])]
    return call(finish, [((3, 5120), bf16)], keep, *got, residual, modulation)[0]


def general(tokens, modulation, w_qkv, norm_gains, cache_kv, w_out, w_up, w_down):
    own_rows = tokens.shape[0]
    width = HEADS * HEAD_DIM
    scale = 1.0 / math.sqrt(HEAD_DIM)
    residual = tokens.astype(jnp.float32)
    normed = (layer_norm(residual) * (1.0 + modulation[1]) + modulation[0]).astype(jnp.bfloat16)
    qkv_cols = jnp.einsum(
        "td,kda->kta",
        lax.all_gather(normed, "seq", axis=0, tiled=True),
        w_qkv,
        preferred_element_type=jnp.float32,
    ).astype(jnp.bfloat16)
    qkv = lax.all_to_all(qkv_cols, "seq", split_axis=1, concat_axis=2, tiled=True)
    queries = rms_norm(qkv[0].astype(jnp.float32), norm_gains[0]).astype(jnp.bfloat16)
    keys_now = rms_norm(qkv[1].astype(jnp.float32), norm_gains[1]).astype(jnp.bfloat16)
    local_keys = jnp.concatenate([cache_kv[0].reshape(-1, width), keys_now], axis=0)
    local_values = jnp.concatenate([cache_kv[1].reshape(-1, width), qkv[2]], axis=0)
    query_heads = queries.reshape(own_rows, HEADS, HEAD_DIM)
    peak_old = jnp.full((own_rows, HEADS), -1e30, jnp.float32)
    key_piece = lax.all_gather(local_keys, "seq", axis=0, tiled=True)
    value_piece = lax.all_gather(local_values, "seq", axis=0, tiled=True)
    count = key_piece.shape[0]
    scores = (
        jnp.einsum(
            "qhd,khd->qhk",
            query_heads,
            key_piece.reshape(count, HEADS, HEAD_DIM),
            preferred_element_type=jnp.float32,
        )
        * scale
    )
    peak_new = jnp.maximum(peak_old, jnp.max(scores, axis=-1))
    expo = jnp.exp(scores - peak_new[..., None])
    total_new = jnp.sum(expo, axis=-1)
    weights = expo.astype(jnp.bfloat16)
    summed_new = jnp.einsum(
        "qhk,khd->qhd",
        weights,
        value_piece.reshape(count, HEADS, HEAD_DIM),
        preferred_element_type=jnp.float32,
    )
    attended = (summed_new / total_new[..., None]).reshape(own_rows, width).astype(jnp.bfloat16)
    projected_cols = jnp.dot(
        lax.all_gather(attended, "seq", axis=0, tiled=True),
        w_out,
        preferred_element_type=jnp.float32,
    ).astype(jnp.bfloat16)
    projected = lax.all_to_all(projected_cols, "seq", split_axis=0, concat_axis=1, tiled=True)
    residual = residual + modulation[2] * projected.astype(jnp.float32)
    normed2 = (layer_norm(residual) * (1.0 + modulation[4]) + modulation[3]).astype(jnp.bfloat16)
    hidden = jax.nn.gelu(
        jnp.dot(
            lax.all_gather(normed2, "seq", axis=0, tiled=True),
            w_up,
            preferred_element_type=jnp.float32,
        ),
        approximate=True,
    ).astype(jnp.bfloat16)
    feed = lax.psum_scatter(
        jnp.dot(hidden, w_down, preferred_element_type=jnp.float32),
        "seq",
        scatter_dimension=0,
        tiled=True,
    )
    return (residual + modulation[5] * feed).astype(jnp.bfloat16)


def solution(mesh):
    in_specs = (
        P(("groups", "seq"), None),
        P(),
        P(None, None, "seq"),
        P(),
        P(None, None, ("groups", "seq"), None),
        P(None, "seq"),
        P(None, "seq"),
        P("seq", None),
    )
    out_specs = P(("groups", "seq"), None)
    local = staged if mesh.shape["seq"] == 16 else general
    return jax.shard_map(local, mesh=mesh, in_specs=in_specs, out_specs=out_specs, check_vma=False)
```

```python
import math

import jax
import jax.numpy as jnp
from jax import lax
from jax.experimental import pallas as pl
from jax.experimental.pallas import tpu as pltpu
from jax.sharding import PartitionSpec as P

HEAD_DIM = 128
HEADS = 20


def layer_norm(values):
    center = values - jnp.mean(values, axis=-1, keepdims=True)
    spread = jnp.mean(center * center, axis=-1, keepdims=True)
    return center * lax.rsqrt(spread + 1e-06)


def rms_norm(values, gain):
    return values * lax.rsqrt(jnp.mean(values * values, axis=-1, keepdims=True) + 1e-06) * gain


VMEM = pl.BlockSpec(memory_space=pltpu.VMEM)
HBM = pl.BlockSpec(memory_space=pltpu.HBM)
NT = (((1,), (1,)), ((), ()))


def call(body, outs, *operands, spec=VMEM, scratch=(), limit=24):
    return pl.pallas_call(
        body,
        out_shape=[jax.ShapeDtypeStruct(shape, dtype) for shape, dtype in outs],
        in_specs=[spec] * len(operands),
        out_specs=[VMEM] * len(outs),
        scratch_shapes=list(scratch),
        compiler_params=pltpu.CompilerParams(vmem_limit_bytes=limit << 20),
        cost_estimate=pl.CostEstimate(flops=0, bytes_accessed=0, transcendentals=0),
    )(*operands)


def load(*arrays):
    parts = []
    for i, array in enumerate(arrays):
        rows = array.shape[0]
        if array.size < 1 << 20:
            parts.append((i, None))
        else:
            cuts = [rows * k // 4 // 16 * 16 for k in range(4)] + [rows]
            parts += [(i, pl.ds(lo, hi - lo)) for lo, hi in zip(cuts, cuts[1:])]

    def body(*refs):
        sources, targets, sems = refs[: len(arrays)], refs[len(arrays) : -1], refs[-1]
        copies = []
        for n, (i, cut) in enumerate(parts):
            source, target = (sources[i], targets[i]) if cut is None else (sources[i].at[cut], targets[i].at[cut])
            copies.append(pltpu.make_async_copy(source, target, sems.at[n]))
        for copy in copies:
            copy.start()
        for copy in copies:
            copy.wait()

    outs = [(array.shape, array.dtype) for array in arrays]
    arrays = [pltpu.with_memory_space_constraint(array, pltpu.HBM) for array in arrays]
    return call(body, outs, *arrays, spec=HBM, scratch=[pltpu.SemaphoreType.DMA((len(parts),))])


def swap(values, offset):
    return lax.ppermute(values, "seq", [(i, i ^ offset) for i in range(16)])


def stack(pieces):
    def body(*refs):
        for i, ref in enumerate(refs[:-1]):
            refs[-1][i] = ref[...]

    return call(body, [((len(pieces), *pieces[0].shape), pieces[0].dtype)], *pieces)[0]


def load_beside(weights, before, beside):
    weights, _ = lax.optimization_barrier((weights, before))
    return lax.optimization_barrier((load(weights)[0], beside))


def gather(block, load_z=None, load_y=None):
    pieces = tuple(swap(block, 4 * z) for z in (1, 2, 3))
    if load_z is not None:
        load_z, pieces = load_beside(load_z, block, pieces)
    planes = stack([block, *pieces])
    across = swap(planes, 2)
    if load_y is not None:
        load_y, across = load_beside(load_y, planes, across)
    return [planes, across, swap(planes, 1), swap(across, 1)], load_z, load_y


def pack_tokens(own, got1, got2, got3, out, rows):
    for z, ref in enumerate((own, got1, got2, got3)):
        for half in range(2):
            row = 12 * half + 3 * z
            rows[row : row + 3, :] = ref[:, 2560 * half : 2560 * half + 2560].astype(jnp.float32)
    out[...] = rows[...].astype(jnp.bfloat16)


def place(stacks, target):
    me = lax.axis_index("seq")
    for slot, ref in enumerate(stacks):
        for z in range(4):
            target[me ^ (4 * z + 2 * (slot & 1) + (slot >> 1))] = ref[z]


def order(near_axis):
    near = lax.broadcasted_iota(jnp.int32, (48, 48), near_axis)
    token = lax.broadcasted_iota(jnp.int32, (48, 48), 1 - near_axis)
    block = (near * 171) >> 9
    device = lax.axis_index("seq") ^ (4 * (block & 3) + ((block >> 2) & 1) + 2 * (block >> 3))
    return (token == 3 * device + near - 3 * block).astype(jnp.bfloat16)


def normalize(values, shift, gain):
    return (layer_norm(values) * (1.0 + gain) + shift).astype(jnp.bfloat16)


def project_qkv(s0, s1, s2, s3, mod, weights, tokens_out, qkv_out, flat):
    for slot, ref in enumerate((s0, s2, s1, s3)):
        for half in range(2):
            piece = ref[12 * half : 12 * half + 12, :].astype(jnp.float32)
            flat[12 * slot : 12 * slot + 12, 2560 * half : 2560 * half + 2560] = piece
    tokens = flat[...]
    tokens_out[...] = tokens.astype(jnp.bfloat16)
    normed = normalize(tokens, mod[0:1, :], mod[1:2, :])
    qkv = lax.dot_general(normed, weights[...], NT, preferred_element_type=jnp.float32).astype(jnp.bfloat16)
    qkv_out[...] = jnp.dot(order(1), qkv, preferred_element_type=jnp.float32).astype(jnp.bfloat16)


def line_up(s0, s1, s2, s3, keys_out, values_out, keys, values):
    for slot, ref in enumerate((s0, s1, s2, s3)):
        for z in range(4):
            for token in range(3):
                row = 6 * (4 * slot + z) + 2 * token
                keys[row : row + 2, :] = ref[z, 0, token].astype(jnp.float32)
                values[row : row + 2, :] = ref[z, 1, token].astype(jnp.float32)
    keys_out[...] = keys[...].astype(jnp.bfloat16)
    values_out[...] = values[...].astype(jnp.bfloat16)


def attend(s0, s1, s2, s3, old_keys, old_values, gains, weights, out, slots, scores, expos, attended):
    place((s0, s1, s2, s3), slots)
    pieces = [slots[j] for j in range(16)]
    queries, keys, values = (
        jnp.concatenate([piece[:, 160 * i : 160 * i + 160] for piece in pieces], axis=1) for i in range(3)
    )
    queries = rms_norm(queries.astype(jnp.float32), gains[0:1, :]).astype(jnp.bfloat16)
    keys = rms_norm(keys.astype(jnp.float32), gains[1:2, :]).astype(jnp.bfloat16)
    keys = jnp.concatenate([old_keys[...], keys], axis=0)
    values = jnp.concatenate([old_values[...], values], axis=0)
    none = jnp.zeros((48, HEAD_DIM), jnp.bfloat16)
    pairs = []
    for head in range(0, HEADS, 2):
        first, second = (slice(HEAD_DIM * h, HEAD_DIM * (h + 1)) for h in (head, head + 1))
        pairs.append((slice(48 * head, 48 * (head + 2)), first, second, slice(HEAD_DIM * head, HEAD_DIM * (head + 2))))
    for rows, first, second, both in pairs:
        upper = jnp.concatenate([queries[:, first], none], axis=1)
        lower = jnp.concatenate([none, queries[:, second]], axis=1)
        diagonal = jnp.concatenate([upper, lower], axis=0)
        scores[rows, :] = lax.dot_general(diagonal, keys[:, both], NT, preferred_element_type=jnp.float32)
    scaled = scores[...] * (1.0 / math.sqrt(HEAD_DIM))
    expo = jnp.exp(scaled - jnp.max(scaled, axis=-1, keepdims=True))
    total = jnp.sum(expo, axis=-1, keepdims=True)
    expos[...] = expo.astype(jnp.bfloat16)
    for rows, first, second, both in pairs:
        summed = jnp.dot(expos[rows, :], values[:, both], preferred_element_type=jnp.float32) / total[rows]
        attended[:, first] = summed[:48, :HEAD_DIM].astype(jnp.bfloat16)
        attended[:, second] = summed[48:, HEAD_DIM:].astype(jnp.bfloat16)
    projected = lax.dot_general(attended[...], weights[...], NT, preferred_element_type=jnp.float32)
    out[...] = jnp.concatenate([projected[:24], projected[24:]], axis=1).astype(jnp.bfloat16)


def feed_forward(s0, s1, s2, s3, tokens, mod, w_up, w_down, keep, send, residual_out, slots):
    place((s0, s1, s2, s3), slots)
    pieces = [slots[j] for j in range(16)]
    upper = jnp.concatenate([piece[:, :320] for piece in pieces], axis=1)
    lower = jnp.concatenate([piece[:, 320:] for piece in pieces], axis=1)
    projected = jnp.concatenate([upper, lower], axis=0)
    projected = jnp.dot(order(0), projected, preferred_element_type=jnp.float32)
    residual = tokens[...].astype(jnp.float32) + mod[2:3, :] * projected
    residual_out[...] = residual[0:3]
    normed = normalize(residual, mod[3:4, :], mod[4:5, :])
    hidden = lax.dot_general(normed, w_up[...], NT, preferred_element_type=jnp.float32)
    hidden = jax.nn.gelu(hidden, approximate=True).astype(jnp.bfloat16)
    partial = jnp.dot(hidden, w_down[...], preferred_element_type=jnp.float32)
    first = lax.axis_index("seq") & 1 == 0
    keep[...] = jnp.where(first, partial[:24], partial[24:])
    send[...] = jnp.where(first, partial[24:], partial[:24]).astype(jnp.bfloat16)


def add_cores(keep, got, own_out, send0, send1, send2, send3):
    got = got[...].astype(jnp.float32)
    total = keep[...] + jnp.concatenate([got[12:], got[:12]], axis=0)
    for z, send in enumerate((send0, send1, send2, send3)):
        block = jnp.concatenate([total[3 * z : 3 * z + 3], total[12 + 3 * z : 15 + 3 * z]], axis=0)
        if z == 0:
            own_out[...] = block
        quarters = [block[:, 1280 * q : 1280 * q + 1280] for q in range(4)]
        send[...] = jnp.concatenate(quarters, axis=0).astype(jnp.bfloat16)


def add_chips(own, got0, got1, got2, got3, keep, send):
    def whole(got):
        got = got[...].astype(jnp.float32)
        return jnp.concatenate([got[6 * q : 6 * q + 6] for q in range(4)], axis=1)

    first = lax.axis_index("seq") & 1 == 0
    total = jnp.where(first, own[...], whole(got0)) + whole(got1) + whole(got2) + whole(got3)
    keep[...] = total[:3]
    send[...] = total[3:]


def finish(keep, got, residual, mod, out):
    out[...] = (residual[...] + mod[5:6, :] * (keep[...] + got[...])).astype(jnp.bfloat16)


def staged(tokens, modulation, w_qkv, norm_gains, cache_kv, w_out, w_up, w_down):
    f32, bf16 = jnp.float32, jnp.bfloat16
    w_qkv = jnp.swapaxes(w_qkv, 1, 2).reshape(480, 5120)
    cache_kv = cache_kv.transpose(0, 2, 1, 3)
    pieces = tuple(swap(tokens, 4 * z) for z in (1, 2, 3))
    cache_far = swap(cache_kv, 8)
    tokens, modulation, norm_gains, cache_kv, w_qkv = load(tokens, modulation, norm_gains, cache_kv, w_qkv)
    pieces, tokens = lax.optimization_barrier((pieces, tokens))
    planes = call(pack_tokens, [((24, 2560), bf16)], tokens, *pieces, scratch=[pltpu.VMEM((24, 2560), f32)])[0]
    across = swap(planes, 2)
    pair = stack([cache_kv, cache_far])
    cache_planes = stack([pair, swap(pair, 4)]).reshape(4, *cache_kv.shape)
    cache_across = swap(cache_planes, 2)
    near_tokens, qkv = call(
        project_qkv,
        [((48, 5120), bf16), ((48, 480), bf16)],
        planes,
        across,
        swap(planes, 1),
        swap(across, 1),
        modulation,
        w_qkv,
        scratch=[pltpu.VMEM((48, 5120), f32)],
    )
    qkv_stacks, w_out, w_up = gather(qkv, w_out.T, w_up.T)
    old_keys, old_values = call(
        line_up,
        [((96, 2560), bf16)] * 2,
        cache_planes,
        cache_across,
        swap(cache_planes, 1),
        swap(cache_across, 1),
        scratch=[pltpu.VMEM((96, 2560), f32)] * 2,
    )
    projected = call(
        attend,
        [((24, 640), bf16)],
        *qkv_stacks,
        old_keys,
        old_values,
        norm_gains,
        w_out,
        scratch=[
            pltpu.VMEM((16, 48, 480), bf16),
            pltpu.VMEM((48 * HEADS, 144), f32),
            pltpu.VMEM((48 * HEADS, 144), bf16),
            pltpu.VMEM((48, 2560), bf16),
        ],
    )[0]
    projected_stacks, _, w_down = gather(projected, None, w_down)
    keep, send, residual = call(
        feed_forward,
        [((24, 5120), f32), ((24, 5120), bf16), ((3, 5120), f32)],
        *projected_stacks,
        near_tokens,
        modulation,
        w_up,
        w_down,
        scratch=[pltpu.VMEM((16, 24, 640), bf16)],
    )
    own, *sends = call(add_cores, [((6, 5120), f32)] + [((24, 1280), bf16)] * 4, keep, swap(send, 1))
    got = []
    for z, send in enumerate(sends):
        pairs = [(i, i ^ 4 * z ^ 2 * (i & 1)) for i in range(16)]
        got.append(lax.ppermute(send, "seq", [(i, j) for i, j in pairs if i != j]))
    keep, send = call(add_chips, [((3, 5120), f32)] * 2, own, got[0], *[got[k] for k in (3, 2, 1)])
    return call(finish, [((3, 5120), bf16)], keep, swap(send, 1), residual, modulation)[0]


def general(tokens, modulation, w_qkv, norm_gains, cache_kv, w_out, w_up, w_down):
    own_rows = tokens.shape[0]
    width = HEADS * HEAD_DIM
    scale = 1.0 / math.sqrt(HEAD_DIM)
    residual = tokens.astype(jnp.float32)
    normed = (layer_norm(residual) * (1.0 + modulation[1]) + modulation[0]).astype(jnp.bfloat16)
    qkv_cols = jnp.einsum(
        "td,kda->kta",
        lax.all_gather(normed, "seq", axis=0, tiled=True),
        w_qkv,
        preferred_element_type=jnp.float32,
    ).astype(jnp.bfloat16)
    qkv = lax.all_to_all(qkv_cols, "seq", split_axis=1, concat_axis=2, tiled=True)
    queries = rms_norm(qkv[0].astype(jnp.float32), norm_gains[0]).astype(jnp.bfloat16)
    keys_now = rms_norm(qkv[1].astype(jnp.float32), norm_gains[1]).astype(jnp.bfloat16)
    local_keys = jnp.concatenate([cache_kv[0].reshape(-1, width), keys_now], axis=0)
    local_values = jnp.concatenate([cache_kv[1].reshape(-1, width), qkv[2]], axis=0)
    query_heads = queries.reshape(own_rows, HEADS, HEAD_DIM)
    peak_old = jnp.full((own_rows, HEADS), -1e30, jnp.float32)
    key_piece = lax.all_gather(local_keys, "seq", axis=0, tiled=True)
    value_piece = lax.all_gather(local_values, "seq", axis=0, tiled=True)
    count = key_piece.shape[0]
    scores = (
        jnp.einsum(
            "qhd,khd->qhk",
            query_heads,
            key_piece.reshape(count, HEADS, HEAD_DIM),
            preferred_element_type=jnp.float32,
        )
        * scale
    )
    peak_new = jnp.maximum(peak_old, jnp.max(scores, axis=-1))
    expo = jnp.exp(scores - peak_new[..., None])
    total_new = jnp.sum(expo, axis=-1)
    weights = expo.astype(jnp.bfloat16)
    summed_new = jnp.einsum(
        "qhk,khd->qhd",
        weights,
        value_piece.reshape(count, HEADS, HEAD_DIM),
        preferred_element_type=jnp.float32,
    )
    attended = (summed_new / total_new[..., None]).reshape(own_rows, width).astype(jnp.bfloat16)
    projected_cols = jnp.dot(
        lax.all_gather(attended, "seq", axis=0, tiled=True),
        w_out,
        preferred_element_type=jnp.float32,
    ).astype(jnp.bfloat16)
    projected = lax.all_to_all(projected_cols, "seq", split_axis=0, concat_axis=1, tiled=True)
    residual = residual + modulation[2] * projected.astype(jnp.float32)
    normed2 = (layer_norm(residual) * (1.0 + modulation[4]) + modulation[3]).astype(jnp.bfloat16)
    hidden = jax.nn.gelu(
        jnp.dot(
            lax.all_gather(normed2, "seq", axis=0, tiled=True),
            w_up,
            preferred_element_type=jnp.float32,
        ),
        approximate=True,
    ).astype(jnp.bfloat16)
    feed = lax.psum_scatter(
        jnp.dot(hidden, w_down, preferred_element_type=jnp.float32),
        "seq",
        scatter_dimension=0,
        tiled=True,
    )
    return (residual + modulation[5] * feed).astype(jnp.bfloat16)


def solution(mesh):
    in_specs = (
        P(("groups", "seq"), None),
        P(),
        P(None, None, "seq"),
        P(),
        P(None, None, ("groups", "seq"), None),
        P(None, "seq"),
        P(None, "seq"),
        P("seq", None),
    )
    out_specs = P(("groups", "seq"), None)
    local = staged if mesh.shape["seq"] == 16 else general
    return jax.shard_map(local, mesh=mesh, in_specs=in_specs, out_specs=out_specs, check_vma=False)
```

```python
import math

import jax
import jax.numpy as jnp
from jax import lax
from jax.experimental import pallas as pl
from jax.experimental.pallas import tpu as pltpu
from jax.sharding import PartitionSpec as P

HEAD_DIM = 128
HEADS = 20
QKV_CUT, UP_CUT, DOWN_CUT = 2560, 2560, 2560


def layer_norm(values):
    center = values - jnp.mean(values, axis=-1, keepdims=True)
    spread = jnp.mean(center * center, axis=-1, keepdims=True)
    return center * lax.rsqrt(spread + 1e-06)


def rms_norm(values, gain):
    return values * lax.rsqrt(jnp.mean(values * values, axis=-1, keepdims=True) + 1e-06) * gain


VMEM = pl.BlockSpec(memory_space=pltpu.VMEM)
HBM = pl.BlockSpec(memory_space=pltpu.HBM)
NT = (((1,), (1,)), ((), ()))


def call(body, outs, *operands, spec=VMEM, scratch=(), limit=24):
    return pl.pallas_call(
        body,
        out_shape=[jax.ShapeDtypeStruct(shape, dtype) for shape, dtype in outs],
        in_specs=[spec] * len(operands),
        out_specs=[VMEM] * len(outs),
        scratch_shapes=list(scratch),
        compiler_params=pltpu.CompilerParams(vmem_limit_bytes=limit << 20),
        cost_estimate=pl.CostEstimate(flops=0, bytes_accessed=0, transcendentals=0),
    )(*operands)


def load(*parts):
    parts = [part if isinstance(part, tuple) else (part, None, None, False) for part in parts]
    arrays = [pltpu.with_memory_space_constraint(array, pltpu.HBM) for array, *_ in parts]
    outs, buffers, pieces = [], [], []
    for i, (array, lo, hi, turn) in enumerate(parts):
        if lo is None:
            outs.append((array.shape, array.dtype))
            pieces.append((i, None, None, None))
            continue
        shape = (array.shape[0], hi - lo)
        outs.append((shape[::-1] if turn else shape, array.dtype))
        if turn:
            buffers.append(pltpu.VMEM(shape, array.dtype))
        size = min(640, hi - lo)
        for start in range(0, hi - lo, size):
            pieces.append((i, pl.ds(lo + start, size), pl.ds(start, size), len(buffers) - 1 if turn else None))

    def body(*refs):
        sources, targets = refs[: len(arrays)], refs[len(arrays) : 2 * len(arrays)]
        sems, *held = refs[2 * len(arrays) :]
        copies = []
        for n, (i, cut, into, buffer) in enumerate(pieces):
            target = targets[i] if buffer is None else held[buffer]
            source = sources[i] if cut is None else sources[i].at[:, cut]
            target = target if cut is None else target.at[:, into]
            copies.append(pltpu.make_async_copy(source, target, sems.at[n]))
        for copy in copies:
            copy.start()
        for copy, (i, _, into, buffer) in zip(copies, pieces):
            copy.wait()
            if buffer is not None:
                targets[i][into, :] = held[buffer][:, into].T

    return call(body, outs, *arrays, spec=HBM, scratch=[pltpu.SemaphoreType.DMA((len(pieces),)), *buffers])


def swap(values, offset):
    return lax.ppermute(values, "seq", [(i, i ^ offset) for i in range(16)])


def stack(pieces):
    def body(*refs):
        for i, ref in enumerate(refs[:-1]):
            refs[-1][i] = ref[...]

    return call(body, [((len(pieces), *pieces[0].shape), pieces[0].dtype)], *pieces)[0]


def load_beside(parts, before, beside):
    arrays, _ = lax.optimization_barrier(([array for array, *_ in parts], before))
    return lax.optimization_barrier((load(*[(array, *part[1:]) for array, part in zip(arrays, parts)]), beside))


def gather(block, load_z, load_y):
    pieces = tuple(swap(block, 4 * z) for z in (1, 2, 3))
    loaded_z, pieces = load_beside(load_z, block, pieces)
    planes = stack([block, *pieces])
    across = swap(planes, 2)
    loaded_y, across = load_beside(load_y, planes, across)
    return [planes, across, swap(planes, 1), swap(across, 1)], loaded_z + loaded_y


def pack_tokens(own, got1, got2, got3, out, rows):
    for z, ref in enumerate((own, got1, got2, got3)):
        for half in range(2):
            row = 12 * half + 3 * z
            rows[row : row + 3, :] = ref[:, 2560 * half : 2560 * half + 2560].astype(jnp.float32)
    out[...] = rows[...].astype(jnp.bfloat16)


def place(stacks, target):
    me = lax.axis_index("seq")
    for slot, ref in enumerate(stacks):
        for z in range(4):
            target[me ^ (4 * z + 2 * (slot & 1) + (slot >> 1))] = ref[z]


def order(near_axis):
    near = lax.broadcasted_iota(jnp.int32, (48, 48), near_axis)
    token = lax.broadcasted_iota(jnp.int32, (48, 48), 1 - near_axis)
    block = (near * 171) >> 9
    device = lax.axis_index("seq") ^ (4 * (block & 3) + ((block >> 2) & 1) + 2 * (block >> 3))
    return (token == 3 * device + near - 3 * block).astype(jnp.bfloat16)


def normalize(values, shift, gain):
    return (layer_norm(values) * (1.0 + gain) + shift).astype(jnp.bfloat16)


def matmul(values, *weights):
    total, row = None, 0
    for part in weights:
        rows = part.shape[0]
        product = jnp.dot(values[:, row : row + rows], part[...], preferred_element_type=jnp.float32)
        total, row = product if total is None else total + product, row + rows
    return total


def project_qkv(s0, s1, s2, s3, mod, weights1, weights2, tokens_out, qkv_out, flat):
    for slot, ref in enumerate((s0, s2, s1, s3)):
        for half in range(2):
            piece = ref[12 * half : 12 * half + 12, :].astype(jnp.float32)
            flat[12 * slot : 12 * slot + 12, 2560 * half : 2560 * half + 2560] = piece
    tokens = flat[...]
    tokens_out[...] = tokens.astype(jnp.bfloat16)
    normed = normalize(tokens, mod[0:1, :], mod[1:2, :])
    qkv = matmul(normed, weights1, weights2).astype(jnp.bfloat16)
    qkv_out[...] = jnp.dot(order(1), qkv, preferred_element_type=jnp.float32).astype(jnp.bfloat16)


def line_up(s0, s1, s2, s3, keys_out, values_out, keys, values):
    for slot, ref in enumerate((s0, s1, s2, s3)):
        for z in range(4):
            for token in range(3):
                row = 6 * (4 * slot + z) + 2 * token
                keys[row : row + 2, :] = ref[z, 0, token].astype(jnp.float32)
                values[row : row + 2, :] = ref[z, 1, token].astype(jnp.float32)
    keys_out[...] = keys[...].astype(jnp.bfloat16)
    values_out[...] = values[...].astype(jnp.bfloat16)


def attend(s0, s1, s2, s3, old_keys, old_values, gains, weights, out, slots, scores, expos, attended):
    place((s0, s1, s2, s3), slots)
    pieces = [slots[j] for j in range(16)]
    queries, keys, values = (
        jnp.concatenate([piece[:, 160 * i : 160 * i + 160] for piece in pieces], axis=1) for i in range(3)
    )
    queries = rms_norm(queries.astype(jnp.float32), gains[0:1, :]).astype(jnp.bfloat16)
    keys = rms_norm(keys.astype(jnp.float32), gains[1:2, :]).astype(jnp.bfloat16)
    keys = jnp.concatenate([old_keys[...], keys], axis=0)
    values = jnp.concatenate([old_values[...], values], axis=0)
    none = jnp.zeros((48, HEAD_DIM), jnp.bfloat16)
    pairs = []
    for head in range(0, HEADS, 2):
        first, second = (slice(HEAD_DIM * h, HEAD_DIM * (h + 1)) for h in (head, head + 1))
        pairs.append((slice(48 * head, 48 * (head + 2)), first, second, slice(HEAD_DIM * head, HEAD_DIM * (head + 2))))
    for rows, first, second, both in pairs:
        upper = jnp.concatenate([queries[:, first], none], axis=1)
        lower = jnp.concatenate([none, queries[:, second]], axis=1)
        diagonal = jnp.concatenate([upper, lower], axis=0)
        scores[rows, :] = lax.dot_general(diagonal, keys[:, both], NT, preferred_element_type=jnp.float32)
    scaled = scores[...] * (1.0 / math.sqrt(HEAD_DIM))
    expo = jnp.exp(scaled - jnp.max(scaled, axis=-1, keepdims=True))
    total = jnp.sum(expo, axis=-1, keepdims=True)
    expos[...] = expo.astype(jnp.bfloat16)
    for rows, first, second, both in pairs:
        summed = jnp.dot(expos[rows, :], values[:, both], preferred_element_type=jnp.float32) / total[rows]
        attended[:, first] = summed[:48, :HEAD_DIM].astype(jnp.bfloat16)
        attended[:, second] = summed[48:, HEAD_DIM:].astype(jnp.bfloat16)
    projected = lax.dot_general(attended[...], weights[...], NT, preferred_element_type=jnp.float32)
    out[...] = jnp.concatenate([projected[:24], projected[24:]], axis=1).astype(jnp.bfloat16)


def feed_forward(s0, s1, s2, s3, tokens, mod, w_up1, w_up2, w_down1, w_down2, keep, send, residual_out, slots):
    place((s0, s1, s2, s3), slots)
    pieces = [slots[j] for j in range(16)]
    upper = jnp.concatenate([piece[:, :320] for piece in pieces], axis=1)
    lower = jnp.concatenate([piece[:, 320:] for piece in pieces], axis=1)
    projected = jnp.concatenate([upper, lower], axis=0)
    projected = jnp.dot(order(0), projected, preferred_element_type=jnp.float32)
    residual = tokens[...].astype(jnp.float32) + mod[2:3, :] * projected
    residual_out[...] = residual[0:3]
    normed = normalize(residual, mod[3:4, :], mod[4:5, :])
    hidden = matmul(normed, w_up1, w_up2)
    hidden = jax.nn.gelu(hidden, approximate=True).astype(jnp.bfloat16)
    first = lax.axis_index("seq") & 1 == 0
    middle = w_down1.shape[1]
    for cols, weights in ((slice(0, middle), w_down1), (slice(middle, None), w_down2)):
        partial = jnp.dot(hidden, weights[...], preferred_element_type=jnp.float32)
        keep[:, cols] = jnp.where(first, partial[:24], partial[24:])
        send[:, cols] = jnp.where(first, partial[24:], partial[:24]).astype(jnp.bfloat16)


def add_cores(keep, got, own_out, send0, send1, send2, send3):
    got = got[...].astype(jnp.float32)
    total = keep[...] + jnp.concatenate([got[12:], got[:12]], axis=0)
    for z, send in enumerate((send0, send1, send2, send3)):
        block = jnp.concatenate([total[3 * z : 3 * z + 3], total[12 + 3 * z : 15 + 3 * z]], axis=0)
        if z == 0:
            own_out[...] = block
        quarters = [block[:, 1280 * q : 1280 * q + 1280] for q in range(4)]
        send[...] = jnp.concatenate(quarters, axis=0).astype(jnp.bfloat16)


def add_chips(own, got0, got1, got2, got3, keep, send):
    def whole(got):
        got = got[...].astype(jnp.float32)
        return jnp.concatenate([got[6 * q : 6 * q + 6] for q in range(4)], axis=1)

    first = lax.axis_index("seq") & 1 == 0
    total = jnp.where(first, own[...], whole(got0)) + whole(got1) + whole(got2) + whole(got3)
    keep[...] = total[:3]
    send[...] = total[3:]


def finish(keep, got, residual, mod, out):
    out[...] = (residual[...] + mod[5:6, :] * (keep[...] + got[...])).astype(jnp.bfloat16)


def staged(tokens, modulation, w_qkv, norm_gains, cache_kv, w_out, w_up, w_down):
    f32, bf16 = jnp.float32, jnp.bfloat16
    w_qkv = jnp.swapaxes(w_qkv, 1, 2).reshape(480, 5120)
    cache_kv = cache_kv.transpose(0, 2, 1, 3)
    pieces = tuple(swap(tokens, 4 * z) for z in (1, 2, 3))
    cache_far = swap(cache_kv, 8)
    tokens, modulation, norm_gains, cache_kv, w_qkv1 = load(
        tokens, modulation, norm_gains, cache_kv, (w_qkv, 0, QKV_CUT, True)
    )
    pieces, tokens = lax.optimization_barrier((pieces, tokens))
    planes = call(pack_tokens, [((24, 2560), bf16)], tokens, *pieces, scratch=[pltpu.VMEM((24, 2560), f32)])[0]
    across = swap(planes, 2)
    (w_qkv2,), across = load_beside([(w_qkv, QKV_CUT, 5120, True)], planes, across)
    pair = stack([cache_kv, cache_far])
    cache_planes = stack([pair, swap(pair, 4)]).reshape(4, *cache_kv.shape)
    cache_across = swap(cache_planes, 2)
    near_tokens, qkv = call(
        project_qkv,
        [((48, 5120), bf16), ((48, 480), bf16)],
        planes,
        across,
        swap(planes, 1),
        swap(across, 1),
        modulation,
        w_qkv1,
        w_qkv2,
        scratch=[pltpu.VMEM((48, 5120), f32)],
    )
    w_up, w_out = w_up.T, w_out.T
    qkv_stacks, (w_up1, w_up2, w_out) = gather(
        qkv, [(w_up, 0, UP_CUT, True)], [(w_up, UP_CUT, 5120, True), (w_out, 0, 2560, False)]
    )
    old_keys, old_values = call(
        line_up,
        [((96, 2560), bf16)] * 2,
        cache_planes,
        cache_across,
        swap(cache_planes, 1),
        swap(cache_across, 1),
        scratch=[pltpu.VMEM((96, 2560), f32)] * 2,
    )
    projected = call(
        attend,
        [((24, 640), bf16)],
        *qkv_stacks,
        old_keys,
        old_values,
        norm_gains,
        w_out,
        scratch=[
            pltpu.VMEM((16, 48, 480), bf16),
            pltpu.VMEM((48 * HEADS, 144), f32),
            pltpu.VMEM((48 * HEADS, 144), bf16),
            pltpu.VMEM((48, 2560), bf16),
        ],
    )[0]
    projected_stacks, (w_down1, w_down2) = gather(
        projected, [(w_down, 0, DOWN_CUT, False)], [(w_down, DOWN_CUT, 5120, False)]
    )
    keep, send, residual = call(
        feed_forward,
        [((24, 5120), f32), ((24, 5120), bf16), ((3, 5120), f32)],
        *projected_stacks,
        near_tokens,
        modulation,
        w_up1,
        w_up2,
        w_down1,
        w_down2,
        scratch=[pltpu.VMEM((16, 24, 640), bf16)],
    )
    own, *sends = call(add_cores, [((6, 5120), f32)] + [((24, 1280), bf16)] * 4, keep, swap(send, 1))
    got = []
    for z, send in enumerate(sends):
        pairs = [(i, i ^ 4 * z ^ 2 * (i & 1)) for i in range(16)]
        got.append(lax.ppermute(send, "seq", [(i, j) for i, j in pairs if i != j]))
    keep, send = call(add_chips, [((3, 5120), f32)] * 2, own, got[0], *[got[k] for k in (3, 2, 1)])
    return call(finish, [((3, 5120), bf16)], keep, swap(send, 1), residual, modulation)[0]


def general(tokens, modulation, w_qkv, norm_gains, cache_kv, w_out, w_up, w_down):
    own_rows = tokens.shape[0]
    width = HEADS * HEAD_DIM
    scale = 1.0 / math.sqrt(HEAD_DIM)
    residual = tokens.astype(jnp.float32)
    normed = (layer_norm(residual) * (1.0 + modulation[1]) + modulation[0]).astype(jnp.bfloat16)
    qkv_cols = jnp.einsum(
        "td,kda->kta",
        lax.all_gather(normed, "seq", axis=0, tiled=True),
        w_qkv,
        preferred_element_type=jnp.float32,
    ).astype(jnp.bfloat16)
    qkv = lax.all_to_all(qkv_cols, "seq", split_axis=1, concat_axis=2, tiled=True)
    queries = rms_norm(qkv[0].astype(jnp.float32), norm_gains[0]).astype(jnp.bfloat16)
    keys_now = rms_norm(qkv[1].astype(jnp.float32), norm_gains[1]).astype(jnp.bfloat16)
    local_keys = jnp.concatenate([cache_kv[0].reshape(-1, width), keys_now], axis=0)
    local_values = jnp.concatenate([cache_kv[1].reshape(-1, width), qkv[2]], axis=0)
    query_heads = queries.reshape(own_rows, HEADS, HEAD_DIM)
    peak_old = jnp.full((own_rows, HEADS), -1e30, jnp.float32)
    key_piece = lax.all_gather(local_keys, "seq", axis=0, tiled=True)
    value_piece = lax.all_gather(local_values, "seq", axis=0, tiled=True)
    count = key_piece.shape[0]
    scores = (
        jnp.einsum(
            "qhd,khd->qhk",
            query_heads,
            key_piece.reshape(count, HEADS, HEAD_DIM),
            preferred_element_type=jnp.float32,
        )
        * scale
    )
    peak_new = jnp.maximum(peak_old, jnp.max(scores, axis=-1))
    expo = jnp.exp(scores - peak_new[..., None])
    total_new = jnp.sum(expo, axis=-1)
    weights = expo.astype(jnp.bfloat16)
    summed_new = jnp.einsum(
        "qhk,khd->qhd",
        weights,
        value_piece.reshape(count, HEADS, HEAD_DIM),
        preferred_element_type=jnp.float32,
    )
    attended = (summed_new / total_new[..., None]).reshape(own_rows, width).astype(jnp.bfloat16)
    projected_cols = jnp.dot(
        lax.all_gather(attended, "seq", axis=0, tiled=True),
        w_out,
        preferred_element_type=jnp.float32,
    ).astype(jnp.bfloat16)
    projected = lax.all_to_all(projected_cols, "seq", split_axis=0, concat_axis=1, tiled=True)
    residual = residual + modulation[2] * projected.astype(jnp.float32)
    normed2 = (layer_norm(residual) * (1.0 + modulation[4]) + modulation[3]).astype(jnp.bfloat16)
    hidden = jax.nn.gelu(
        jnp.dot(
            lax.all_gather(normed2, "seq", axis=0, tiled=True),
            w_up,
            preferred_element_type=jnp.float32,
        ),
        approximate=True,
    ).astype(jnp.bfloat16)
    feed = lax.psum_scatter(
        jnp.dot(hidden, w_down, preferred_element_type=jnp.float32),
        "seq",
        scatter_dimension=0,
        tiled=True,
    )
    return (residual + modulation[5] * feed).astype(jnp.bfloat16)


def solution(mesh):
    in_specs = (
        P(("groups", "seq"), None),
        P(),
        P(None, None, "seq"),
        P(),
        P(None, None, ("groups", "seq"), None),
        P(None, "seq"),
        P(None, "seq"),
        P("seq", None),
    )
    out_specs = P(("groups", "seq"), None)
    local = staged if mesh.shape["seq"] == 16 else general
    return jax.shard_map(local, mesh=mesh, in_specs=in_specs, out_specs=out_specs, check_vma=False)
```

```python
import math

import jax
import jax.numpy as jnp
from jax import lax
from jax.experimental import pallas as pl
from jax.experimental.pallas import tpu as pltpu
from jax.sharding import PartitionSpec as P

HEAD_DIM = 128
HEADS = 20
QKV_CUT, UP_CUT, DOWN_CUT = 2560, 2560, 2560


def layer_norm(values):
    center = values - jnp.mean(values, axis=-1, keepdims=True)
    spread = jnp.mean(center * center, axis=-1, keepdims=True)
    return center * lax.rsqrt(spread + 1e-06)


def rms_norm(values, gain):
    return values * lax.rsqrt(jnp.mean(values * values, axis=-1, keepdims=True) + 1e-06) * gain


VMEM = pl.BlockSpec(memory_space=pltpu.VMEM)
HBM = pl.BlockSpec(memory_space=pltpu.HBM)
NT = (((1,), (1,)), ((), ()))


def call(body, outs, *operands, spec=VMEM, scratch=(), limit=24):
    return pl.pallas_call(
        body,
        out_shape=[jax.ShapeDtypeStruct(shape, dtype) for shape, dtype in outs],
        in_specs=[spec] * len(operands),
        out_specs=[VMEM] * len(outs),
        scratch_shapes=list(scratch),
        compiler_params=pltpu.CompilerParams(vmem_limit_bytes=limit << 20),
        cost_estimate=pl.CostEstimate(flops=0, bytes_accessed=0, transcendentals=0),
    )(*operands)


def load(*parts):
    parts = [part if isinstance(part, tuple) else (part, None, None, False) for part in parts]
    arrays = [pltpu.with_memory_space_constraint(array, pltpu.HBM) for array, *_ in parts]
    outs, buffers, pieces = [], [], []
    for i, (array, lo, hi, turn) in enumerate(parts):
        if lo is None:
            outs.append((array.shape, array.dtype))
            pieces.append((i, None, None, None))
            continue
        shape = (array.shape[0], hi - lo)
        outs.append((shape[::-1] if turn else shape, array.dtype))
        if turn:
            buffers.append(pltpu.VMEM(shape, array.dtype))
        size = min(640, hi - lo)
        for start in range(0, hi - lo, size):
            pieces.append((i, pl.ds(lo + start, size), pl.ds(start, size), len(buffers) - 1 if turn else None))

    def body(*refs):
        sources, targets = refs[: len(arrays)], refs[len(arrays) : 2 * len(arrays)]
        sems, *held = refs[2 * len(arrays) :]
        copies = []
        for n, (i, cut, into, buffer) in enumerate(pieces):
            target = targets[i] if buffer is None else held[buffer]
            source = sources[i] if cut is None else sources[i].at[:, cut]
            target = target if cut is None else target.at[:, into]
            copies.append(pltpu.make_async_copy(source, target, sems.at[n]))
        for copy in copies:
            copy.start()
        for copy, (i, _, into, buffer) in zip(copies, pieces):
            copy.wait()
            if buffer is not None:
                targets[i][into, :] = held[buffer][:, into].T

    return call(body, outs, *arrays, spec=HBM, scratch=[pltpu.SemaphoreType.DMA((len(pieces),)), *buffers])


def swap(values, offset):
    return lax.ppermute(values, "seq", [(i, i ^ offset) for i in range(16)])


def stack(pieces):
    def body(*refs):
        for i, ref in enumerate(refs[:-1]):
            refs[-1][i] = ref[...]

    return call(body, [((len(pieces), *pieces[0].shape), pieces[0].dtype)], *pieces)[0]


def load_beside(parts, before, beside):
    arrays, _ = lax.optimization_barrier(([array for array, *_ in parts], before))
    return lax.optimization_barrier((load(*[(array, *part[1:]) for array, part in zip(arrays, parts)]), beside))


def gather(block, load_z, load_y):
    pieces = tuple(swap(block, 4 * z) for z in (1, 2, 3))
    loaded_z, pieces = load_beside(load_z, block, pieces)
    planes = stack([block, *pieces])
    across = swap(planes, 2)
    loaded_y, across = load_beside(load_y, planes, across)
    return [planes, across, swap(planes, 1), swap(across, 1)], loaded_z + loaded_y


def pack_tokens(own, got1, got2, got3, out, rows):
    for z, ref in enumerate((own, got1, got2, got3)):
        for half in range(2):
            row = 12 * half + 3 * z
            rows[row : row + 3, :] = ref[:, 2560 * half : 2560 * half + 2560].astype(jnp.float32)
    out[...] = rows[...].astype(jnp.bfloat16)


def place(stacks, target):
    me = lax.axis_index("seq")
    for slot, ref in enumerate(stacks):
        for z in range(4):
            target[me ^ (4 * z + 2 * (slot & 1) + (slot >> 1))] = ref[z]


def order(near_axis):
    near = lax.broadcasted_iota(jnp.int32, (48, 48), near_axis)
    token = lax.broadcasted_iota(jnp.int32, (48, 48), 1 - near_axis)
    block = (near * 171) >> 9
    device = lax.axis_index("seq") ^ (4 * (block & 3) + ((block >> 2) & 1) + 2 * (block >> 3))
    return (token == 3 * device + near - 3 * block).astype(jnp.bfloat16)


def normalize(values, shift, gain):
    return (layer_norm(values) * (1.0 + gain) + shift).astype(jnp.bfloat16)


def matmul(values, *weights):
    total, row = None, 0
    for part in weights:
        rows = part.shape[0]
        product = jnp.dot(values[:, row : row + rows], part[...], preferred_element_type=jnp.float32)
        total, row = product if total is None else total + product, row + rows
    return total


def unpack_tokens(stacks, rows):
    for slot, ref in enumerate(stacks):
        for half in range(2):
            piece = ref[12 * half : 12 * half + 12, :].astype(jnp.float32)
            rows[12 * slot : 12 * slot + 12, 2560 * half : 2560 * half + 2560] = piece


def project_qkv(s0, s2, s1, s3, mod, weights1, weights2, qkv_out, rows):
    unpack_tokens((s0, s2, s1, s3), rows)
    normed = normalize(rows[...], mod[0:1, :], mod[1:2, :])
    qkv = matmul(normed, weights1, weights2).astype(jnp.bfloat16)
    qkv_out[...] = jnp.dot(order(1), qkv, preferred_element_type=jnp.float32).astype(jnp.bfloat16)


def order_tokens(s0, s2, s1, s3, out, rows):
    unpack_tokens((s0, s2, s1, s3), rows)
    tokens = rows[...].astype(jnp.bfloat16)
    out[...] = jnp.dot(order(1), tokens, preferred_element_type=jnp.float32).astype(jnp.bfloat16)


def line_up(s0, s1, s2, s3, keys_out, values_out, keys, values):
    for slot, ref in enumerate((s0, s1, s2, s3)):
        for z in range(4):
            for token in range(3):
                row = 6 * (4 * slot + z) + 2 * token
                keys[row : row + 2, :] = ref[z, 0, token].astype(jnp.float32)
                values[row : row + 2, :] = ref[z, 1, token].astype(jnp.float32)
    keys_out[...] = keys[...].astype(jnp.bfloat16)
    values_out[...] = values[...].astype(jnp.bfloat16)


def attend(s0, s1, s2, s3, old_keys, old_values, gains, weights, out, slots, scores, expos, attended):
    place((s0, s1, s2, s3), slots)
    pieces = [slots[j] for j in range(16)]
    queries, keys, values = (
        jnp.concatenate([piece[:, 160 * i : 160 * i + 160] for piece in pieces], axis=1) for i in range(3)
    )
    queries = rms_norm(queries.astype(jnp.float32), gains[0:1, :]).astype(jnp.bfloat16)
    keys = rms_norm(keys.astype(jnp.float32), gains[1:2, :]).astype(jnp.bfloat16)
    keys = jnp.concatenate([old_keys[...], keys], axis=0)
    values = jnp.concatenate([old_values[...], values], axis=0)
    none = jnp.zeros((48, HEAD_DIM), jnp.bfloat16)
    pairs = []
    for head in range(0, HEADS, 2):
        first, second = (slice(HEAD_DIM * h, HEAD_DIM * (h + 1)) for h in (head, head + 1))
        pairs.append((slice(48 * head, 48 * (head + 2)), first, second, slice(HEAD_DIM * head, HEAD_DIM * (head + 2))))
    for rows, first, second, both in pairs:
        upper = jnp.concatenate([queries[:, first], none], axis=1)
        lower = jnp.concatenate([none, queries[:, second]], axis=1)
        diagonal = jnp.concatenate([upper, lower], axis=0)
        scores[rows, :] = lax.dot_general(diagonal, keys[:, both], NT, preferred_element_type=jnp.float32)
    scaled = scores[...] * (1.0 / math.sqrt(HEAD_DIM))
    expo = jnp.exp(scaled - jnp.max(scaled, axis=-1, keepdims=True))
    total = jnp.sum(expo, axis=-1, keepdims=True)
    expos[...] = expo.astype(jnp.bfloat16)
    for rows, first, second, both in pairs:
        summed = jnp.dot(expos[rows, :], values[:, both], preferred_element_type=jnp.float32) / total[rows]
        attended[:, first] = summed[:48, :HEAD_DIM].astype(jnp.bfloat16)
        attended[:, second] = summed[48:, HEAD_DIM:].astype(jnp.bfloat16)
    projected = lax.dot_general(attended[...], weights[...], NT, preferred_element_type=jnp.float32)
    out[...] = jnp.concatenate([projected[:24], projected[24:]], axis=1).astype(jnp.bfloat16)


def line_up_projected(stacks, slots):
    place(stacks, slots)
    pieces = [slots[j] for j in range(16)]
    upper = jnp.concatenate([piece[:, :320] for piece in pieces], axis=1)
    lower = jnp.concatenate([piece[:, 320:] for piece in pieces], axis=1)
    return jnp.concatenate([upper, lower], axis=0)


def own_residual(s0, s1, s2, s3, tokens, mod, out, slots):
    projected = line_up_projected((s0, s1, s2, s3), slots)
    own = jnp.dot(order(0)[0:16], projected, preferred_element_type=jnp.float32)[0:3]
    out[...] = tokens[...].astype(jnp.float32) + mod[2:3, :] * own


def feed_forward(s0, s1, s2, s3, tokens, mod, w_up1, w_up2, w_down1, w_down2, keep, send, slots):
    projected = line_up_projected((s0, s1, s2, s3), slots)
    residual = tokens[...].astype(jnp.float32) + mod[2:3, :] * projected.astype(jnp.float32)
    normed = normalize(residual, mod[3:4, :], mod[4:5, :])
    hidden = matmul(normed, w_up1, w_up2)
    hidden = jax.nn.gelu(hidden, approximate=True).astype(jnp.bfloat16)
    hidden = jnp.dot(order(0), hidden, preferred_element_type=jnp.float32).astype(jnp.bfloat16)
    first = lax.axis_index("seq") & 1 == 0
    middle = w_down1.shape[1]
    for cols, weights in ((slice(0, middle), w_down1), (slice(middle, None), w_down2)):
        partial = jnp.dot(hidden, weights[...], preferred_element_type=jnp.float32)
        keep[:, cols] = jnp.where(first, partial[:24], partial[24:])
        send[:, cols] = jnp.where(first, partial[24:], partial[:24]).astype(jnp.bfloat16)


def add_cores(keep, got, own_out, send0, send1, send2, send3):
    got = got[...].astype(jnp.float32)
    total = keep[...] + jnp.concatenate([got[12:], got[:12]], axis=0)
    for z, send in enumerate((send0, send1, send2, send3)):
        block = jnp.concatenate([total[3 * z : 3 * z + 3], total[12 + 3 * z : 15 + 3 * z]], axis=0)
        if z == 0:
            own_out[...] = block
        quarters = [block[:, 1280 * q : 1280 * q + 1280] for q in range(4)]
        send[...] = jnp.concatenate(quarters, axis=0).astype(jnp.bfloat16)


def add_chips(own, got0, got1, got2, got3, keep, send):
    def whole(got):
        got = got[...].astype(jnp.float32)
        return jnp.concatenate([got[6 * q : 6 * q + 6] for q in range(4)], axis=1)

    first = lax.axis_index("seq") & 1 == 0
    total = jnp.where(first, own[...], whole(got0)) + whole(got1) + whole(got2) + whole(got3)
    keep[...] = total[:3]
    send[...] = total[3:]


def finish(keep, got, residual, mod, out):
    out[...] = (residual[...] + mod[5:6, :] * (keep[...] + got[...])).astype(jnp.bfloat16)


def staged(tokens, modulation, w_qkv, norm_gains, cache_kv, w_out, w_up, w_down):
    f32, bf16 = jnp.float32, jnp.bfloat16
    w_qkv = jnp.swapaxes(w_qkv, 1, 2).reshape(480, 5120)
    cache_kv = cache_kv.transpose(0, 2, 1, 3)
    pieces = tuple(swap(tokens, 4 * z) for z in (1, 2, 3))
    cache_far = swap(cache_kv, 8)
    tokens, modulation, norm_gains, cache_kv, w_qkv1 = load(
        tokens, modulation, norm_gains, cache_kv, (w_qkv, 0, QKV_CUT, True)
    )
    pieces, tokens = lax.optimization_barrier((pieces, tokens))
    planes = call(pack_tokens, [((24, 2560), bf16)], tokens, *pieces, scratch=[pltpu.VMEM((24, 2560), f32)])[0]
    across = swap(planes, 2)
    (w_qkv2,), across = load_beside([(w_qkv, QKV_CUT, 5120, True)], planes, across)
    pair = stack([cache_kv, cache_far])
    cache_planes = stack([pair, swap(pair, 4)]).reshape(4, *cache_kv.shape)
    cache_across = swap(cache_planes, 2)
    token_stacks = [planes, swap(planes, 1), across, swap(across, 1)]
    qkv = call(
        project_qkv,
        [((48, 480), bf16)],
        *token_stacks,
        modulation,
        w_qkv1,
        w_qkv2,
        scratch=[pltpu.VMEM((48, 5120), f32)],
    )[0]
    all_tokens = call(order_tokens, [((48, 5120), bf16)], *token_stacks, scratch=[pltpu.VMEM((48, 5120), f32)])[0]
    w_up, w_out = w_up.T, w_out.T
    qkv_stacks, (w_up1, w_up2, w_out) = gather(
        qkv, [(w_up, 0, UP_CUT, True)], [(w_up, UP_CUT, 5120, True), (w_out, 0, 2560, False)]
    )
    old_keys, old_values = call(
        line_up,
        [((96, 2560), bf16)] * 2,
        cache_planes,
        cache_across,
        swap(cache_planes, 1),
        swap(cache_across, 1),
        scratch=[pltpu.VMEM((96, 2560), f32)] * 2,
    )
    projected = call(
        attend,
        [((24, 640), bf16)],
        *qkv_stacks,
        old_keys,
        old_values,
        norm_gains,
        w_out,
        scratch=[
            pltpu.VMEM((16, 48, 480), bf16),
            pltpu.VMEM((48 * HEADS, 144), f32),
            pltpu.VMEM((48 * HEADS, 144), bf16),
            pltpu.VMEM((48, 2560), bf16),
        ],
    )[0]
    projected_stacks, (w_down1, w_down2) = gather(
        projected, [(w_down, 0, DOWN_CUT, False)], [(w_down, DOWN_CUT, 5120, False)]
    )
    keep, send = call(
        feed_forward,
        [((24, 5120), f32), ((24, 5120), bf16)],
        *projected_stacks,
        all_tokens,
        modulation,
        w_up1,
        w_up2,
        w_down1,
        w_down2,
        scratch=[pltpu.VMEM((16, 24, 640), bf16)],
    )
    keep, projected_stacks = lax.optimization_barrier((keep, projected_stacks))
    slots = pltpu.VMEM((16, 24, 640), bf16)
    residual = call(own_residual, [((3, 5120), f32)], *projected_stacks, tokens, modulation, scratch=[slots])[0]
    own, *sends = call(add_cores, [((6, 5120), f32)] + [((24, 1280), bf16)] * 4, keep, swap(send, 1))
    got = []
    for z, send in enumerate(sends):
        pairs = [(i, i ^ 4 * z ^ 2 * (i & 1)) for i in range(16)]
        got.append(lax.ppermute(send, "seq", [(i, j) for i, j in pairs if i != j]))
    keep, send = call(add_chips, [((3, 5120), f32)] * 2, own, got[0], *[got[k] for k in (3, 2, 1)])
    return call(finish, [((3, 5120), bf16)], keep, swap(send, 1), residual, modulation)[0]


def general(tokens, modulation, w_qkv, norm_gains, cache_kv, w_out, w_up, w_down):
    own_rows = tokens.shape[0]
    width = HEADS * HEAD_DIM
    scale = 1.0 / math.sqrt(HEAD_DIM)
    residual = tokens.astype(jnp.float32)
    normed = (layer_norm(residual) * (1.0 + modulation[1]) + modulation[0]).astype(jnp.bfloat16)
    qkv_cols = jnp.einsum(
        "td,kda->kta",
        lax.all_gather(normed, "seq", axis=0, tiled=True),
        w_qkv,
        preferred_element_type=jnp.float32,
    ).astype(jnp.bfloat16)
    qkv = lax.all_to_all(qkv_cols, "seq", split_axis=1, concat_axis=2, tiled=True)
    queries = rms_norm(qkv[0].astype(jnp.float32), norm_gains[0]).astype(jnp.bfloat16)
    keys_now = rms_norm(qkv[1].astype(jnp.float32), norm_gains[1]).astype(jnp.bfloat16)
    local_keys = jnp.concatenate([cache_kv[0].reshape(-1, width), keys_now], axis=0)
    local_values = jnp.concatenate([cache_kv[1].reshape(-1, width), qkv[2]], axis=0)
    query_heads = queries.reshape(own_rows, HEADS, HEAD_DIM)
    peak_old = jnp.full((own_rows, HEADS), -1e30, jnp.float32)
    key_piece = lax.all_gather(local_keys, "seq", axis=0, tiled=True)
    value_piece = lax.all_gather(local_values, "seq", axis=0, tiled=True)
    count = key_piece.shape[0]
    scores = (
        jnp.einsum(
            "qhd,khd->qhk",
            query_heads,
            key_piece.reshape(count, HEADS, HEAD_DIM),
            preferred_element_type=jnp.float32,
        )
        * scale
    )
    peak_new = jnp.maximum(peak_old, jnp.max(scores, axis=-1))
    expo = jnp.exp(scores - peak_new[..., None])
    total_new = jnp.sum(expo, axis=-1)
    weights = expo.astype(jnp.bfloat16)
    summed_new = jnp.einsum(
        "qhk,khd->qhd",
        weights,
        value_piece.reshape(count, HEADS, HEAD_DIM),
        preferred_element_type=jnp.float32,
    )
    attended = (summed_new / total_new[..., None]).reshape(own_rows, width).astype(jnp.bfloat16)
    projected_cols = jnp.dot(
        lax.all_gather(attended, "seq", axis=0, tiled=True),
        w_out,
        preferred_element_type=jnp.float32,
    ).astype(jnp.bfloat16)
    projected = lax.all_to_all(projected_cols, "seq", split_axis=0, concat_axis=1, tiled=True)
    residual = residual + modulation[2] * projected.astype(jnp.float32)
    normed2 = (layer_norm(residual) * (1.0 + modulation[4]) + modulation[3]).astype(jnp.bfloat16)
    hidden = jax.nn.gelu(
        jnp.dot(
            lax.all_gather(normed2, "seq", axis=0, tiled=True),
            w_up,
            preferred_element_type=jnp.float32,
        ),
        approximate=True,
    ).astype(jnp.bfloat16)
    feed = lax.psum_scatter(
        jnp.dot(hidden, w_down, preferred_element_type=jnp.float32),
        "seq",
        scatter_dimension=0,
        tiled=True,
    )
    return (residual + modulation[5] * feed).astype(jnp.bfloat16)


def solution(mesh):
    in_specs = (
        P(("groups", "seq"), None),
        P(),
        P(None, None, "seq"),
        P(),
        P(None, None, ("groups", "seq"), None),
        P(None, "seq"),
        P(None, "seq"),
        P("seq", None),
    )
    out_specs = P(("groups", "seq"), None)
    local = staged if mesh.shape["seq"] == 16 else general
    return jax.shard_map(local, mesh=mesh, in_specs=in_specs, out_specs=out_specs, check_vma=False)
```

```python
import math

import jax
import jax.numpy as jnp
from jax import lax
from jax.experimental import pallas as pl
from jax.experimental.pallas import tpu as pltpu
from jax.sharding import PartitionSpec as P

HEAD_DIM = 128
HEADS = 20
QKV_CUT, UP_CUT, DOWN_CUT = 2560, 2560, 2560


def layer_norm(values):
    center = values - jnp.mean(values, axis=-1, keepdims=True)
    spread = jnp.mean(center * center, axis=-1, keepdims=True)
    return center * lax.rsqrt(spread + 1e-06)


def rms_norm(values, gain):
    return values * lax.rsqrt(jnp.mean(values * values, axis=-1, keepdims=True) + 1e-06) * gain


VMEM = pl.BlockSpec(memory_space=pltpu.VMEM)
HBM = pl.BlockSpec(memory_space=pltpu.HBM)
NT = (((1,), (1,)), ((), ()))


def call(body, outs, *operands, spec=VMEM, scratch=(), limit=24):
    return pl.pallas_call(
        body,
        out_shape=[jax.ShapeDtypeStruct(shape, dtype) for shape, dtype in outs],
        in_specs=[spec] * len(operands),
        out_specs=[VMEM] * len(outs),
        scratch_shapes=list(scratch),
        compiler_params=pltpu.CompilerParams(vmem_limit_bytes=limit << 20),
        cost_estimate=pl.CostEstimate(flops=0, bytes_accessed=0, transcendentals=0),
    )(*operands)


def load(*parts):
    parts = [part if isinstance(part, tuple) else (part, None, None, False) for part in parts]
    arrays = [pltpu.with_memory_space_constraint(array, pltpu.HBM) for array, *_ in parts]
    outs, buffers, pieces = [], [], []
    for i, (array, lo, hi, turn) in enumerate(parts):
        if lo is None:
            outs.append((array.shape, array.dtype))
            pieces.append((i, None, None, None))
            continue
        shape = (array.shape[0], hi - lo)
        outs.append((shape[::-1] if turn else shape, array.dtype))
        if turn:
            buffers.append(pltpu.VMEM(shape, array.dtype))
        size = min(640, hi - lo)
        for start in range(0, hi - lo, size):
            pieces.append((i, pl.ds(lo + start, size), pl.ds(start, size), len(buffers) - 1 if turn else None))

    def body(*refs):
        sources, targets = refs[: len(arrays)], refs[len(arrays) : 2 * len(arrays)]
        sems, *held = refs[2 * len(arrays) :]
        copies = []
        for n, (i, cut, into, buffer) in enumerate(pieces):
            target = targets[i] if buffer is None else held[buffer]
            source = sources[i] if cut is None else sources[i].at[:, cut]
            target = target if cut is None else target.at[:, into]
            copies.append(pltpu.make_async_copy(source, target, sems.at[n]))
        for copy in copies:
            copy.start()
        for copy, (i, _, into, buffer) in zip(copies, pieces):
            copy.wait()
            if buffer is not None:
                targets[i][into, :] = held[buffer][:, into].T

    return call(body, outs, *arrays, spec=HBM, scratch=[pltpu.SemaphoreType.DMA((len(pieces),)), *buffers])


def swap(values, offset):
    return lax.ppermute(values, "seq", [(i, i ^ offset) for i in range(16)])


def stack(pieces):
    def body(*refs):
        for i, ref in enumerate(refs[:-1]):
            refs[-1][i] = ref[...]

    return call(body, [((len(pieces), *pieces[0].shape), pieces[0].dtype)], *pieces)[0]


def load_beside(parts, before, beside):
    arrays, _ = lax.optimization_barrier(([array for array, *_ in parts], before))
    return lax.optimization_barrier((load(*[(array, *part[1:]) for array, part in zip(arrays, parts)]), beside))


def gather(block, load_z, load_y):
    pieces = tuple(swap(block, 4 * z) for z in (1, 2, 3))
    loaded_z, pieces = load_beside(load_z, block, pieces)
    planes = stack([block, *pieces])
    across = swap(planes, 2)
    loaded_y, across = load_beside(load_y, planes, across)
    return [planes, across, swap(planes, 1), swap(across, 1)], loaded_z + loaded_y


def pack_tokens(own, got1, got2, got3, out, rows):
    for z, ref in enumerate((own, got1, got2, got3)):
        for half in range(2):
            row = 12 * half + 3 * z
            rows[row : row + 3, :] = ref[:, 2560 * half : 2560 * half + 2560].astype(jnp.float32)
    out[...] = rows[...].astype(jnp.bfloat16)


def place(stacks, target):
    me = lax.axis_index("seq")
    for slot, ref in enumerate(stacks):
        for z in range(4):
            target[me ^ (4 * z + 2 * (slot & 1) + (slot >> 1))] = ref[z]


def order(near_axis):
    near = lax.broadcasted_iota(jnp.int32, (48, 48), near_axis)
    token = lax.broadcasted_iota(jnp.int32, (48, 48), 1 - near_axis)
    block = (near * 171) >> 9
    device = lax.axis_index("seq") ^ (4 * (block & 3) + ((block >> 2) & 1) + 2 * (block >> 3))
    return (token == 3 * device + near - 3 * block).astype(jnp.bfloat16)


def normalize(values, shift, gain):
    return (layer_norm(values) * (1.0 + gain) + shift).astype(jnp.bfloat16)


def matmul(values, *weights):
    total, row = None, 0
    for part in weights:
        rows = part.shape[0]
        product = jnp.dot(values[:, row : row + rows], part[...], preferred_element_type=jnp.float32)
        total, row = product if total is None else total + product, row + rows
    return total


def unpack_tokens(stacks, rows):
    for slot, ref in enumerate(stacks):
        for half in range(2):
            piece = ref[12 * half : 12 * half + 12, :].astype(jnp.float32)
            rows[12 * slot : 12 * slot + 12, 2560 * half : 2560 * half + 2560] = piece


def project_qkv(s0, s2, s1, s3, mod, weights1, weights2, qkv_out, rows):
    unpack_tokens((s0, s2, s1, s3), rows)
    normed = normalize(rows[...], mod[0:1, :], mod[1:2, :])
    qkv = matmul(normed, weights1, weights2).astype(jnp.bfloat16)
    qkv_out[...] = jnp.dot(order(1), qkv, preferred_element_type=jnp.float32).astype(jnp.bfloat16)


def order_tokens(s0, s2, s1, s3, out, rows):
    unpack_tokens((s0, s2, s1, s3), rows)
    tokens = rows[...].astype(jnp.bfloat16)
    out[...] = jnp.dot(order(1), tokens, preferred_element_type=jnp.float32).astype(jnp.bfloat16)


def line_up(s0, s1, s2, s3, keys_out, values_out, keys, values):
    for slot, ref in enumerate((s0, s1, s2, s3)):
        for z in range(4):
            for token in range(3):
                row = 6 * (4 * slot + z) + 2 * token
                keys[row : row + 2, :] = ref[z, 0, token].astype(jnp.float32)
                values[row : row + 2, :] = ref[z, 1, token].astype(jnp.float32)
    keys_out[...] = keys[...].astype(jnp.bfloat16)
    values_out[...] = values[...].astype(jnp.bfloat16)


def attend(s0, s1, s2, s3, old_keys, old_values, gains, weights, out, slots, scores, expos, attended):
    place((s0, s1, s2, s3), slots)
    pieces = [slots[j] for j in range(16)]
    queries, keys, values = (
        jnp.concatenate([piece[:, 160 * i : 160 * i + 160] for piece in pieces], axis=1) for i in range(3)
    )
    queries = rms_norm(queries.astype(jnp.float32), gains[0:1, :]).astype(jnp.bfloat16)
    keys = rms_norm(keys.astype(jnp.float32), gains[1:2, :]).astype(jnp.bfloat16)
    keys = jnp.concatenate([old_keys[...], keys], axis=0)
    values = jnp.concatenate([old_values[...], values], axis=0)
    none = jnp.zeros((48, HEAD_DIM), jnp.bfloat16)
    pairs = []
    for head in range(0, HEADS, 2):
        first, second = (slice(HEAD_DIM * h, HEAD_DIM * (h + 1)) for h in (head, head + 1))
        pairs.append((slice(48 * head, 48 * (head + 2)), first, second, slice(HEAD_DIM * head, HEAD_DIM * (head + 2))))
    for rows, first, second, both in pairs:
        upper = jnp.concatenate([queries[:, first], none], axis=1)
        lower = jnp.concatenate([none, queries[:, second]], axis=1)
        diagonal = jnp.concatenate([upper, lower], axis=0)
        scores[rows, :] = lax.dot_general(diagonal, keys[:, both], NT, preferred_element_type=jnp.float32)
    scaled = scores[...] * (1.0 / math.sqrt(HEAD_DIM))
    expo = jnp.exp(scaled - jnp.max(scaled, axis=-1, keepdims=True))
    total = jnp.sum(expo, axis=-1, keepdims=True)
    expos[...] = expo.astype(jnp.bfloat16)
    for rows, first, second, both in pairs:
        summed = jnp.dot(expos[rows, :], values[:, both], preferred_element_type=jnp.float32) / total[rows]
        attended[:, first] = summed[:48, :HEAD_DIM].astype(jnp.bfloat16)
        attended[:, second] = summed[48:, HEAD_DIM:].astype(jnp.bfloat16)
    projected = lax.dot_general(attended[...], weights[...], NT, preferred_element_type=jnp.float32)
    out[...] = jnp.concatenate([projected[:24], projected[24:]], axis=1).astype(jnp.bfloat16)


def line_up_projected(stacks, slots):
    place(stacks, slots)
    pieces = [slots[j] for j in range(16)]
    upper = jnp.concatenate([piece[:, :320] for piece in pieces], axis=1)
    lower = jnp.concatenate([piece[:, 320:] for piece in pieces], axis=1)
    return jnp.concatenate([upper, lower], axis=0)


def own_residual(s0, s1, s2, s3, tokens, mod, out, slots):
    projected = line_up_projected((s0, s1, s2, s3), slots)
    own = jnp.dot(order(0)[0:16], projected, preferred_element_type=jnp.float32)[0:3]
    out[...] = tokens[...].astype(jnp.float32) + mod[2:3, :] * own


def feed_forward(s0, s1, s2, s3, tokens, mod, w_up1, w_up2, w_down1, w_down2, keep, send, slots):
    projected = line_up_projected((s0, s1, s2, s3), slots)
    residual = tokens[...].astype(jnp.float32) + mod[2:3, :] * projected.astype(jnp.float32)
    normed = normalize(residual, mod[3:4, :], mod[4:5, :])
    hidden = matmul(normed, w_up1, w_up2)
    hidden = jax.nn.gelu(hidden, approximate=True).astype(jnp.bfloat16)
    hidden = jnp.dot(order(0), hidden, preferred_element_type=jnp.float32).astype(jnp.bfloat16)
    first = lax.axis_index("seq") & 1 == 0
    middle = w_down1.shape[1]
    for cols, weights in ((slice(0, middle), w_down1), (slice(middle, None), w_down2)):
        partial = jnp.dot(hidden, weights[...], preferred_element_type=jnp.float32)
        keep[:, cols] = jnp.where(first, partial[:24], partial[24:])
        send[:, cols] = jnp.where(first, partial[24:], partial[:24]).astype(jnp.bfloat16)


def add_cores(keep, got, own_out, send0, send1, send2, send3):
    got = got[...].astype(jnp.float32)
    total = keep[...] + jnp.concatenate([got[12:], got[:12]], axis=0)
    for z, send in enumerate((send0, send1, send2, send3)):
        block = jnp.concatenate([total[3 * z : 3 * z + 3], total[12 + 3 * z : 15 + 3 * z]], axis=0)
        if z == 0:
            own_out[...] = block
        quarters = [block[:, 1280 * q : 1280 * q + 1280] for q in range(4)]
        send[...] = jnp.concatenate(quarters, axis=0).astype(jnp.bfloat16)


def add_chips(own, got3, got2, got1, got0, keep, send):
    def whole(got):
        got = got[...].astype(jnp.float32)
        return jnp.concatenate([got[6 * q : 6 * q + 6] for q in range(4)], axis=1)

    first = lax.axis_index("seq") & 1 == 0
    total = jnp.where(first, own[...], whole(got0)) + whole(got1) + whole(got2) + whole(got3)
    keep[...] = total[:3]
    send[...] = total[3:]


def finish(keep, got, residual, mod, out):
    out[...] = (residual[...] + mod[5:6, :] * (keep[...] + got[...])).astype(jnp.bfloat16)


def staged(tokens, modulation, w_qkv, norm_gains, cache_kv, w_out, w_up, w_down):
    f32, bf16 = jnp.float32, jnp.bfloat16
    w_qkv = jnp.swapaxes(w_qkv, 1, 2).reshape(480, 5120)
    cache_kv = cache_kv.transpose(0, 2, 1, 3)
    pieces = tuple(swap(tokens, 4 * z) for z in (1, 2, 3))
    cache_far = swap(cache_kv, 8)
    tokens, modulation, norm_gains, cache_kv, w_qkv1 = load(
        tokens, modulation, norm_gains, cache_kv, (w_qkv, 0, QKV_CUT, True)
    )
    pieces, tokens = lax.optimization_barrier((pieces, tokens))
    planes = call(pack_tokens, [((24, 2560), bf16)], tokens, *pieces, scratch=[pltpu.VMEM((24, 2560), f32)])[0]
    across = swap(planes, 2)
    (w_qkv2,), across = load_beside([(w_qkv, QKV_CUT, 5120, True)], planes, across)
    pair = stack([cache_kv, cache_far])
    cache_planes = stack([pair, swap(pair, 4)]).reshape(4, *cache_kv.shape)
    cache_across = swap(cache_planes, 2)
    token_stacks = [planes, swap(planes, 1), across, swap(across, 1)]
    qkv = call(
        project_qkv,
        [((48, 480), bf16)],
        *token_stacks,
        modulation,
        w_qkv1,
        w_qkv2,
        scratch=[pltpu.VMEM((48, 5120), f32)],
    )[0]
    all_tokens = call(order_tokens, [((48, 5120), bf16)], *token_stacks, scratch=[pltpu.VMEM((48, 5120), f32)])[0]
    w_up, w_out = w_up.T, w_out.T
    qkv_stacks, (w_up1, w_up2, w_out) = gather(
        qkv, [(w_up, 0, UP_CUT, True)], [(w_up, UP_CUT, 5120, True), (w_out, 0, 2560, False)]
    )
    old_keys, old_values = call(
        line_up,
        [((96, 2560), bf16)] * 2,
        cache_planes,
        cache_across,
        swap(cache_planes, 1),
        swap(cache_across, 1),
        scratch=[pltpu.VMEM((96, 2560), f32)] * 2,
    )
    projected = call(
        attend,
        [((24, 640), bf16)],
        *qkv_stacks,
        old_keys,
        old_values,
        norm_gains,
        w_out,
        scratch=[
            pltpu.VMEM((16, 48, 480), bf16),
            pltpu.VMEM((48 * HEADS, 144), f32),
            pltpu.VMEM((48 * HEADS, 144), bf16),
            pltpu.VMEM((48, 2560), bf16),
        ],
    )[0]
    projected_stacks, (w_down1, w_down2) = gather(
        projected, [(w_down, 0, DOWN_CUT, False)], [(w_down, DOWN_CUT, 5120, False)]
    )
    keep, send = call(
        feed_forward,
        [((24, 5120), f32), ((24, 5120), bf16)],
        *projected_stacks,
        all_tokens,
        modulation,
        w_up1,
        w_up2,
        w_down1,
        w_down2,
        scratch=[pltpu.VMEM((16, 24, 640), bf16)],
    )
    keep, projected_stacks = lax.optimization_barrier((keep, projected_stacks))
    slots = pltpu.VMEM((16, 24, 640), bf16)
    residual = call(own_residual, [((3, 5120), f32)], *projected_stacks, tokens, modulation, scratch=[slots])[0]
    own, *sends = call(add_cores, [((6, 5120), f32)] + [((24, 1280), bf16)] * 4, keep, swap(send, 1))
    got = []
    for z, send in enumerate(sends):
        pairs = [(i, i ^ 4 * z ^ 2 * (i & 1)) for i in range(16)]
        got.append(lax.ppermute(send, "seq", [(i, j) for i, j in pairs if i != j]))
    keep, send = call(add_chips, [((3, 5120), f32)] * 2, own, *[got[k] for k in (3, 2, 1, 0)])
    return call(finish, [((3, 5120), bf16)], keep, swap(send, 1), residual, modulation)[0]


def general(tokens, modulation, w_qkv, norm_gains, cache_kv, w_out, w_up, w_down):
    own_rows = tokens.shape[0]
    width = HEADS * HEAD_DIM
    scale = 1.0 / math.sqrt(HEAD_DIM)
    residual = tokens.astype(jnp.float32)
    normed = (layer_norm(residual) * (1.0 + modulation[1]) + modulation[0]).astype(jnp.bfloat16)
    qkv_cols = jnp.einsum(
        "td,kda->kta",
        lax.all_gather(normed, "seq", axis=0, tiled=True),
        w_qkv,
        preferred_element_type=jnp.float32,
    ).astype(jnp.bfloat16)
    qkv = lax.all_to_all(qkv_cols, "seq", split_axis=1, concat_axis=2, tiled=True)
    queries = rms_norm(qkv[0].astype(jnp.float32), norm_gains[0]).astype(jnp.bfloat16)
    keys_now = rms_norm(qkv[1].astype(jnp.float32), norm_gains[1]).astype(jnp.bfloat16)
    local_keys = jnp.concatenate([cache_kv[0].reshape(-1, width), keys_now], axis=0)
    local_values = jnp.concatenate([cache_kv[1].reshape(-1, width), qkv[2]], axis=0)
    query_heads = queries.reshape(own_rows, HEADS, HEAD_DIM)
    peak_old = jnp.full((own_rows, HEADS), -1e30, jnp.float32)
    key_piece = lax.all_gather(local_keys, "seq", axis=0, tiled=True)
    value_piece = lax.all_gather(local_values, "seq", axis=0, tiled=True)
    count = key_piece.shape[0]
    scores = (
        jnp.einsum(
            "qhd,khd->qhk",
            query_heads,
            key_piece.reshape(count, HEADS, HEAD_DIM),
            preferred_element_type=jnp.float32,
        )
        * scale
    )
    peak_new = jnp.maximum(peak_old, jnp.max(scores, axis=-1))
    expo = jnp.exp(scores - peak_new[..., None])
    total_new = jnp.sum(expo, axis=-1)
    weights = expo.astype(jnp.bfloat16)
    summed_new = jnp.einsum(
        "qhk,khd->qhd",
        weights,
        value_piece.reshape(count, HEADS, HEAD_DIM),
        preferred_element_type=jnp.float32,
    )
    attended = (summed_new / total_new[..., None]).reshape(own_rows, width).astype(jnp.bfloat16)
    projected_cols = jnp.dot(
        lax.all_gather(attended, "seq", axis=0, tiled=True),
        w_out,
        preferred_element_type=jnp.float32,
    ).astype(jnp.bfloat16)
    projected = lax.all_to_all(projected_cols, "seq", split_axis=0, concat_axis=1, tiled=True)
    residual = residual + modulation[2] * projected.astype(jnp.float32)
    normed2 = (layer_norm(residual) * (1.0 + modulation[4]) + modulation[3]).astype(jnp.bfloat16)
    hidden = jax.nn.gelu(
        jnp.dot(
            lax.all_gather(normed2, "seq", axis=0, tiled=True),
            w_up,
            preferred_element_type=jnp.float32,
        ),
        approximate=True,
    ).astype(jnp.bfloat16)
    feed = lax.psum_scatter(
        jnp.dot(hidden, w_down, preferred_element_type=jnp.float32),
        "seq",
        scatter_dimension=0,
        tiled=True,
    )
    return (residual + modulation[5] * feed).astype(jnp.bfloat16)


def solution(mesh):
    in_specs = (
        P(("groups", "seq"), None),
        P(),
        P(None, None, "seq"),
        P(),
        P(None, None, ("groups", "seq"), None),
        P(None, "seq"),
        P(None, "seq"),
        P("seq", None),
    )
    out_specs = P(("groups", "seq"), None)
    local = staged if mesh.shape["seq"] == 16 else general
    return jax.shard_map(local, mesh=mesh, in_specs=in_specs, out_specs=out_specs, check_vma=False)
```

```python
import math

import jax
import jax.numpy as jnp
from jax import lax
from jax.experimental import pallas as pl
from jax.experimental.pallas import tpu as pltpu
from jax.sharding import PartitionSpec as P

HEAD_DIM = 128
HEADS = 20
QKV_CUT, UP_CUT, DOWN_CUT = 1920, 1920, 1920


def layer_norm(values):
    center = values - jnp.mean(values, axis=-1, keepdims=True)
    spread = jnp.mean(center * center, axis=-1, keepdims=True)
    return center * lax.rsqrt(spread + 1e-06)


def rms_norm(values, gain):
    return values * lax.rsqrt(jnp.mean(values * values, axis=-1, keepdims=True) + 1e-06) * gain


VMEM = pl.BlockSpec(memory_space=pltpu.VMEM)
HBM = pl.BlockSpec(memory_space=pltpu.HBM)
NT = (((1,), (1,)), ((), ()))


def call(body, outs, *operands, spec=VMEM, scratch=(), limit=24):
    return pl.pallas_call(
        body,
        out_shape=[jax.ShapeDtypeStruct(shape, dtype) for shape, dtype in outs],
        in_specs=[spec] * len(operands),
        out_specs=[VMEM] * len(outs),
        scratch_shapes=list(scratch),
        compiler_params=pltpu.CompilerParams(vmem_limit_bytes=limit << 20),
        cost_estimate=pl.CostEstimate(flops=0, bytes_accessed=0, transcendentals=0),
    )(*operands)


def load(*parts):
    parts = [part if isinstance(part, tuple) else (part, None, None, False) for part in parts]
    arrays = [pltpu.with_memory_space_constraint(array, pltpu.HBM) for array, *_ in parts]
    outs, buffers, pieces = [], [], []
    for i, (array, lo, hi, turn) in enumerate(parts):
        if lo is None:
            outs.append((array.shape, array.dtype))
            pieces.append((i, None, None, None))
            continue
        shape = (array.shape[0], hi - lo)
        outs.append((shape[::-1] if turn else shape, array.dtype))
        if turn:
            buffers.append(pltpu.VMEM(shape, array.dtype))
        size = min(640, hi - lo)
        for start in range(0, hi - lo, size):
            pieces.append((i, pl.ds(lo + start, size), pl.ds(start, size), len(buffers) - 1 if turn else None))

    def body(*refs):
        sources, targets = refs[: len(arrays)], refs[len(arrays) : 2 * len(arrays)]
        sems, *held = refs[2 * len(arrays) :]
        copies = []
        for n, (i, cut, into, buffer) in enumerate(pieces):
            target = targets[i] if buffer is None else held[buffer]
            source = sources[i] if cut is None else sources[i].at[:, cut]
            target = target if cut is None else target.at[:, into]
            copies.append(pltpu.make_async_copy(source, target, sems.at[n]))
        for copy in copies:
            copy.start()
        for copy, (i, _, into, buffer) in zip(copies, pieces):
            copy.wait()
            if buffer is not None:
                targets[i][into, :] = held[buffer][:, into].T

    return call(body, outs, *arrays, spec=HBM, scratch=[pltpu.SemaphoreType.DMA((len(pieces),)), *buffers])


def swap(values, offset):
    return lax.ppermute(values, "seq", [(i, i ^ offset) for i in range(16)])


def stack(pieces):
    def body(*refs):
        for i, ref in enumerate(refs[:-1]):
            refs[-1][i] = ref[...]

    return call(body, [((len(pieces), *pieces[0].shape), pieces[0].dtype)], *pieces)[0]


def load_beside(parts, before, beside):
    arrays, _ = lax.optimization_barrier(([array for array, *_ in parts], before))
    return lax.optimization_barrier((load(*[(array, *part[1:]) for array, part in zip(arrays, parts)]), beside))


def gather(block, load_z, load_y):
    pieces = tuple(swap(block, 4 * z) for z in (1, 2, 3))
    loaded_z, pieces = load_beside(load_z, block, pieces)
    planes = stack([block, *pieces])
    across = swap(planes, 2)
    loaded_y, across = load_beside(load_y, planes, across)
    return [planes, across, swap(planes, 1), swap(across, 1)], loaded_z + loaded_y


def pack_tokens(own, got1, got2, got3, out, rows):
    for z, ref in enumerate((own, got1, got2, got3)):
        for half in range(2):
            row = 12 * half + 3 * z
            rows[row : row + 3, :] = ref[:, 2560 * half : 2560 * half + 2560].astype(jnp.float32)
    out[...] = rows[:24, :].astype(jnp.bfloat16)


def place(stacks, target):
    me = lax.axis_index("seq")
    for slot, ref in enumerate(stacks):
        for z in range(4):
            target[me ^ (4 * z + 2 * (slot & 1) + (slot >> 1))] = ref[z]


def order(near_axis):
    near = lax.broadcasted_iota(jnp.int32, (48, 48), near_axis)
    token = lax.broadcasted_iota(jnp.int32, (48, 48), 1 - near_axis)
    block = (near * 171) >> 9
    device = lax.axis_index("seq") ^ (4 * (block & 3) + ((block >> 2) & 1) + 2 * (block >> 3))
    return (token == 3 * device + near - 3 * block).astype(jnp.bfloat16)


def normalize(values, shift, gain):
    return (layer_norm(values) * (1.0 + gain) + shift).astype(jnp.bfloat16)


def matmul(values, *weights):
    total, row = None, 0
    for part in weights:
        rows = part.shape[0]
        product = jnp.dot(values[:, row : row + rows], part[...], preferred_element_type=jnp.float32)
        total, row = product if total is None else total + product, row + rows
    return total


def unpack_tokens(stacks, rows):
    for slot, ref in enumerate(stacks):
        values = ref[...].astype(jnp.float32)
        for half in range(2):
            piece = values[12 * half : 12 * half + 12]
            rows[12 * slot : 12 * slot + 12, 2560 * half : 2560 * half + 2560] = piece


def project_qkv(s0, s2, s1, s3, mod, weights1, weights2, qkv_out, rows):
    unpack_tokens((s0, s2, s1, s3), rows)
    normed = normalize(rows[:48, :], mod[0:1, :], mod[1:2, :])
    qkv = matmul(normed, weights1, weights2).astype(jnp.bfloat16)
    qkv_out[...] = jnp.dot(order(1), qkv, preferred_element_type=jnp.float32).astype(jnp.bfloat16)


def order_tokens(s0, s2, s1, s3, out, rows):
    unpack_tokens((s0, s2, s1, s3), rows)
    tokens = rows[:48, :].astype(jnp.bfloat16)
    out[...] = jnp.dot(order(1), tokens, preferred_element_type=jnp.float32).astype(jnp.bfloat16)


def line_up(s0, s1, s2, s3, keys_out, values_out, keys, values):
    for slot, ref in enumerate((s0, s1, s2, s3)):
        for z in range(4):
            for token in range(3):
                row = 6 * (4 * slot + z) + 2 * token
                keys[row : row + 2, :] = ref[z, 0, token].astype(jnp.float32)
                values[row : row + 2, :] = ref[z, 1, token].astype(jnp.float32)
    keys_out[...] = keys[:96, :].astype(jnp.bfloat16)
    values_out[...] = values[:96, :].astype(jnp.bfloat16)


def attend(s0, s1, s2, s3, old_keys, old_values, gains, weights, out, slots, scores, expos, attended):
    place((s0, s1, s2, s3), slots)
    pieces = [slots[j] for j in range(16)]
    queries, keys, values = (
        jnp.concatenate([piece[:, 160 * i : 160 * i + 160] for piece in pieces], axis=1) for i in range(3)
    )
    queries = rms_norm(queries.astype(jnp.float32), gains[0:1, :]).astype(jnp.bfloat16)
    keys = rms_norm(keys.astype(jnp.float32), gains[1:2, :]).astype(jnp.bfloat16)
    keys = jnp.concatenate([old_keys[...], keys], axis=0)
    values = jnp.concatenate([old_values[...], values], axis=0)
    none = jnp.zeros((48, HEAD_DIM), jnp.bfloat16)
    pairs = []
    for head in range(0, HEADS, 2):
        first, second = (slice(HEAD_DIM * h, HEAD_DIM * (h + 1)) for h in (head, head + 1))
        pairs.append((slice(48 * head, 48 * (head + 2)), first, second, slice(HEAD_DIM * head, HEAD_DIM * (head + 2))))
    for rows, first, second, both in pairs:
        upper = jnp.concatenate([queries[:, first], none], axis=1)
        lower = jnp.concatenate([none, queries[:, second]], axis=1)
        diagonal = jnp.concatenate([upper, lower], axis=0)
        scores[rows, :] = lax.dot_general(diagonal, keys[:, both], NT, preferred_element_type=jnp.float32)
    scaled = scores[...] * (1.0 / math.sqrt(HEAD_DIM))
    expo = jnp.exp(scaled - jnp.max(scaled, axis=-1, keepdims=True))
    total = jnp.sum(expo, axis=-1, keepdims=True)
    expos[...] = expo.astype(jnp.bfloat16)
    for rows, first, second, both in pairs:
        summed = jnp.dot(expos[rows, :], values[:, both], preferred_element_type=jnp.float32) / total[rows]
        attended[:, first] = summed[:48, :HEAD_DIM].astype(jnp.bfloat16)
        attended[:, second] = summed[48:, HEAD_DIM:].astype(jnp.bfloat16)
    projected = lax.dot_general(attended[...], weights[...], NT, preferred_element_type=jnp.float32)
    out[...] = jnp.concatenate([projected[:24], projected[24:]], axis=1).astype(jnp.bfloat16)


def line_up_projected(stacks, slots):
    place(stacks, slots)
    pieces = [slots[j] for j in range(16)]
    upper = jnp.concatenate([piece[:, :320] for piece in pieces], axis=1)
    lower = jnp.concatenate([piece[:, 320:] for piece in pieces], axis=1)
    return jnp.concatenate([upper, lower], axis=0)


def own_residual(s0, s1, s2, s3, tokens, mod, out, slots):
    projected = line_up_projected((s0, s1, s2, s3), slots)
    own = jnp.dot(order(0)[0:16], projected, preferred_element_type=jnp.float32)[0:3]
    out[...] = tokens[...].astype(jnp.float32) + mod[2:3, :] * own


def feed_forward(s0, s1, s2, s3, tokens, mod, w_up1, w_up2, w_down1, w_down2, keep, send, slots):
    projected = line_up_projected((s0, s1, s2, s3), slots)
    residual = tokens[...].astype(jnp.float32) + mod[2:3, :] * projected.astype(jnp.float32)
    normed = normalize(residual, mod[3:4, :], mod[4:5, :])
    hidden = matmul(normed, w_up1, w_up2)
    hidden = jax.nn.gelu(hidden, approximate=True).astype(jnp.bfloat16)
    hidden = jnp.dot(order(0), hidden, preferred_element_type=jnp.float32).astype(jnp.bfloat16)
    first = lax.axis_index("seq") & 1 == 0
    middle = w_down1.shape[1]
    for cols, weights in ((slice(0, middle), w_down1), (slice(middle, None), w_down2)):
        partial = jnp.dot(hidden, weights[...], preferred_element_type=jnp.float32)
        keep[:, cols] = jnp.where(first, partial[:24], partial[24:])
        send[:, cols] = jnp.where(first, partial[24:], partial[:24]).astype(jnp.bfloat16)


def add_cores(keep, got, own_out, send0, send1, send2, send3):
    got = got[...].astype(jnp.float32)
    total = keep[...] + jnp.concatenate([got[12:], got[:12]], axis=0)
    for z, send in enumerate((send0, send1, send2, send3)):
        block = jnp.concatenate([total[3 * z : 3 * z + 3], total[12 + 3 * z : 15 + 3 * z]], axis=0)
        if z == 0:
            own_out[...] = block
        quarters = [block[:, 1280 * q : 1280 * q + 1280] for q in range(4)]
        send[...] = jnp.concatenate(quarters, axis=0).astype(jnp.bfloat16)


def add_chips(own, got3, got2, got1, got0, keep, send):
    def whole(got):
        got = got[...].astype(jnp.float32)
        return jnp.concatenate([got[6 * q : 6 * q + 6] for q in range(4)], axis=1)

    first = lax.axis_index("seq") & 1 == 0
    total = jnp.where(first, own[...], whole(got0)) + whole(got1) + whole(got2) + whole(got3)
    keep[...] = total[:3]
    send[...] = total[3:]


def finish(keep, got, residual, mod, out):
    out[...] = (residual[...] + mod[5:6, :] * (keep[...] + got[...])).astype(jnp.bfloat16)


def staged(tokens, modulation, w_qkv, norm_gains, cache_kv, w_out, w_up, w_down):
    f32, bf16 = jnp.float32, jnp.bfloat16
    w_qkv = jnp.swapaxes(w_qkv, 1, 2).reshape(480, 5120)
    cache_kv = cache_kv.transpose(0, 2, 1, 3)
    pieces = tuple(swap(tokens, 4 * z) for z in (1, 2, 3))
    cache_far = swap(cache_kv, 8)
    tokens, modulation, norm_gains, cache_kv, w_qkv1 = load(
        tokens, modulation, norm_gains, cache_kv, (w_qkv, 0, QKV_CUT, True)
    )
    pieces, tokens = lax.optimization_barrier((pieces, tokens))
    planes = call(pack_tokens, [((24, 2560), bf16)], tokens, *pieces, scratch=[pltpu.VMEM((32, 2560), f32)])[0]
    across = swap(planes, 2)
    (w_qkv2,), across = load_beside([(w_qkv, QKV_CUT, 5120, True)], planes, across)
    pair = stack([cache_kv, cache_far])
    cache_planes = stack([pair, swap(pair, 4)]).reshape(4, *cache_kv.shape)
    cache_across = swap(cache_planes, 2)
    token_stacks = [planes, swap(planes, 1), across, swap(across, 1)]
    qkv = call(
        project_qkv,
        [((48, 480), bf16)],
        *token_stacks,
        modulation,
        w_qkv1,
        w_qkv2,
        scratch=[pltpu.VMEM((56, 5120), f32)],
    )[0]
    all_tokens = call(order_tokens, [((48, 5120), bf16)], *token_stacks, scratch=[pltpu.VMEM((56, 5120), f32)])[0]
    w_up, w_out = w_up.T, w_out.T
    qkv_stacks, (w_up1, w_up2, w_out) = gather(
        qkv, [(w_up, 0, UP_CUT, True)], [(w_up, UP_CUT, 5120, True), (w_out, 0, 2560, False)]
    )
    old_keys, old_values = call(
        line_up,
        [((96, 2560), bf16)] * 2,
        cache_planes,
        cache_across,
        swap(cache_planes, 1),
        swap(cache_across, 1),
        scratch=[pltpu.VMEM((104, 2560), f32)] * 2,
    )
    projected = call(
        attend,
        [((24, 640), bf16)],
        *qkv_stacks,
        old_keys,
        old_values,
        norm_gains,
        w_out,
        scratch=[
            pltpu.VMEM((16, 48, 480), bf16),
            pltpu.VMEM((48 * HEADS, 144), f32),
            pltpu.VMEM((48 * HEADS, 144), bf16),
            pltpu.VMEM((48, 2560), bf16),
        ],
    )[0]
    projected_stacks, (w_down1, w_down2) = gather(
        projected, [(w_down, 0, DOWN_CUT, False)], [(w_down, DOWN_CUT, 5120, False)]
    )
    keep, send = call(
        feed_forward,
        [((24, 5120), f32), ((24, 5120), bf16)],
        *projected_stacks,
        all_tokens,
        modulation,
        w_up1,
        w_up2,
        w_down1,
        w_down2,
        scratch=[pltpu.VMEM((16, 24, 640), bf16)],
    )
    keep, projected_stacks = lax.optimization_barrier((keep, projected_stacks))
    slots = pltpu.VMEM((16, 24, 640), bf16)
    residual = call(own_residual, [((3, 5120), f32)], *projected_stacks, tokens, modulation, scratch=[slots])[0]
    own, *sends = call(add_cores, [((6, 5120), f32)] + [((24, 1280), bf16)] * 4, keep, swap(send, 1))
    got = []
    for z, send in enumerate(sends):
        pairs = [(i, i ^ 4 * z ^ 2 * (i & 1)) for i in range(16)]
        got.append(lax.ppermute(send, "seq", [(i, j) for i, j in pairs if i != j]))
    keep, send = call(add_chips, [((3, 5120), f32)] * 2, own, *[got[k] for k in (3, 2, 1, 0)])
    return call(finish, [((3, 5120), bf16)], keep, swap(send, 1), residual, modulation)[0]


def general(tokens, modulation, w_qkv, norm_gains, cache_kv, w_out, w_up, w_down):
    own_rows = tokens.shape[0]
    width = HEADS * HEAD_DIM
    scale = 1.0 / math.sqrt(HEAD_DIM)
    residual = tokens.astype(jnp.float32)
    normed = (layer_norm(residual) * (1.0 + modulation[1]) + modulation[0]).astype(jnp.bfloat16)
    qkv_cols = jnp.einsum(
        "td,kda->kta",
        lax.all_gather(normed, "seq", axis=0, tiled=True),
        w_qkv,
        preferred_element_type=jnp.float32,
    ).astype(jnp.bfloat16)
    qkv = lax.all_to_all(qkv_cols, "seq", split_axis=1, concat_axis=2, tiled=True)
    queries = rms_norm(qkv[0].astype(jnp.float32), norm_gains[0]).astype(jnp.bfloat16)
    keys_now = rms_norm(qkv[1].astype(jnp.float32), norm_gains[1]).astype(jnp.bfloat16)
    local_keys = jnp.concatenate([cache_kv[0].reshape(-1, width), keys_now], axis=0)
    local_values = jnp.concatenate([cache_kv[1].reshape(-1, width), qkv[2]], axis=0)
    query_heads = queries.reshape(own_rows, HEADS, HEAD_DIM)
    peak_old = jnp.full((own_rows, HEADS), -1e30, jnp.float32)
    key_piece = lax.all_gather(local_keys, "seq", axis=0, tiled=True)
    value_piece = lax.all_gather(local_values, "seq", axis=0, tiled=True)
    count = key_piece.shape[0]
    scores = (
        jnp.einsum(
            "qhd,khd->qhk",
            query_heads,
            key_piece.reshape(count, HEADS, HEAD_DIM),
            preferred_element_type=jnp.float32,
        )
        * scale
    )
    peak_new = jnp.maximum(peak_old, jnp.max(scores, axis=-1))
    expo = jnp.exp(scores - peak_new[..., None])
    total_new = jnp.sum(expo, axis=-1)
    weights = expo.astype(jnp.bfloat16)
    summed_new = jnp.einsum(
        "qhk,khd->qhd",
        weights,
        value_piece.reshape(count, HEADS, HEAD_DIM),
        preferred_element_type=jnp.float32,
    )
    attended = (summed_new / total_new[..., None]).reshape(own_rows, width).astype(jnp.bfloat16)
    projected_cols = jnp.dot(
        lax.all_gather(attended, "seq", axis=0, tiled=True),
        w_out,
        preferred_element_type=jnp.float32,
    ).astype(jnp.bfloat16)
    projected = lax.all_to_all(projected_cols, "seq", split_axis=0, concat_axis=1, tiled=True)
    residual = residual + modulation[2] * projected.astype(jnp.float32)
    normed2 = (layer_norm(residual) * (1.0 + modulation[4]) + modulation[3]).astype(jnp.bfloat16)
    hidden = jax.nn.gelu(
        jnp.dot(
            lax.all_gather(normed2, "seq", axis=0, tiled=True),
            w_up,
            preferred_element_type=jnp.float32,
        ),
        approximate=True,
    ).astype(jnp.bfloat16)
    feed = lax.psum_scatter(
        jnp.dot(hidden, w_down, preferred_element_type=jnp.float32),
        "seq",
        scatter_dimension=0,
        tiled=True,
    )
    return (residual + modulation[5] * feed).astype(jnp.bfloat16)


def solution(mesh):
    in_specs = (
        P(("groups", "seq"), None),
        P(),
        P(None, None, "seq"),
        P(),
        P(None, None, ("groups", "seq"), None),
        P(None, "seq"),
        P(None, "seq"),
        P("seq", None),
    )
    out_specs = P(("groups", "seq"), None)
    local = staged if mesh.shape["seq"] == 16 else general
    return jax.shard_map(local, mesh=mesh, in_specs=in_specs, out_specs=out_specs, check_vma=False)
```

```python
import math

import jax
import jax.numpy as jnp
from jax import lax
from jax.experimental import pallas as pl
from jax.experimental.pallas import tpu as pltpu
from jax.sharding import PartitionSpec as P

HEAD_DIM = 128
HEADS = 20
QKV_CUT, UP_CUT, DOWN_CUT = 1920, 1920, 1920


def layer_norm(values):
    center = values - jnp.mean(values, axis=-1, keepdims=True)
    spread = jnp.mean(center * center, axis=-1, keepdims=True)
    return center * lax.rsqrt(spread + 1e-06)


def rms_norm(values, gain):
    return values * lax.rsqrt(jnp.mean(values * values, axis=-1, keepdims=True) + 1e-06) * gain


VMEM = pl.BlockSpec(memory_space=pltpu.VMEM)
HBM = pl.BlockSpec(memory_space=pltpu.HBM)
NT = (((1,), (1,)), ((), ()))


def call(body, outs, *operands, spec=VMEM, scratch=(), limit=24):
    return pl.pallas_call(
        body,
        out_shape=[jax.ShapeDtypeStruct(shape, dtype) for shape, dtype in outs],
        in_specs=[spec] * len(operands),
        out_specs=[VMEM] * len(outs),
        scratch_shapes=list(scratch),
        compiler_params=pltpu.CompilerParams(vmem_limit_bytes=limit << 20),
        cost_estimate=pl.CostEstimate(flops=0, bytes_accessed=0, transcendentals=0),
    )(*operands)


def load(*parts):
    parts = [part if isinstance(part, tuple) else (part, None, None, False) for part in parts]
    arrays = [pltpu.with_memory_space_constraint(array, pltpu.HBM) for array, *_ in parts]
    outs, buffers, pieces = [], [], []
    for i, (array, lo, hi, turn) in enumerate(parts):
        if lo is None:
            outs.append((array.shape, array.dtype))
            pieces.append((i, None, None, None))
            continue
        shape = (array.shape[0], hi - lo)
        outs.append((shape[::-1] if turn else shape, array.dtype))
        if turn:
            buffers.append(pltpu.VMEM(shape, array.dtype))
        size = min(640, hi - lo)
        for start in range(0, hi - lo, size):
            pieces.append((i, pl.ds(lo + start, size), pl.ds(start, size), len(buffers) - 1 if turn else None))

    def body(*refs):
        sources, targets = refs[: len(arrays)], refs[len(arrays) : 2 * len(arrays)]
        sems, *held = refs[2 * len(arrays) :]
        copies = []
        for n, (i, cut, into, buffer) in enumerate(pieces):
            target = targets[i] if buffer is None else held[buffer]
            source = sources[i] if cut is None else sources[i].at[:, cut]
            target = target if cut is None else target.at[:, into]
            copies.append(pltpu.make_async_copy(source, target, sems.at[n]))
        for copy in copies:
            copy.start()
        for copy, (i, _, into, buffer) in zip(copies, pieces):
            copy.wait()
            if buffer is not None:
                targets[i][into, :] = held[buffer][:, into].T

    return call(body, outs, *arrays, spec=HBM, scratch=[pltpu.SemaphoreType.DMA((len(pieces),)), *buffers])


def swap(values, offset):
    return lax.ppermute(values, "seq", [(i, i ^ offset) for i in range(16)])


def stack(pieces):
    def body(*refs):
        for i, ref in enumerate(refs[:-1]):
            refs[-1][i] = ref[...]

    return call(body, [((len(pieces), *pieces[0].shape), pieces[0].dtype)], *pieces)[0]


def load_beside(parts, before, beside):
    arrays, _ = lax.optimization_barrier(([array for array, *_ in parts], before))
    return lax.optimization_barrier((load(*[(array, *part[1:]) for array, part in zip(arrays, parts)]), beside))


def gather(block, load_z, load_y):
    pieces = tuple(swap(block, 4 * z) for z in (1, 2, 3))
    loaded_z, pieces = load_beside(load_z, block, pieces)
    planes = stack([block, *pieces])
    across = swap(planes, 2)
    loaded_y, across = load_beside(load_y, planes, across)
    return [planes, across, swap(planes, 1), swap(across, 1)], loaded_z + loaded_y


def pack_tokens(own, got1, got2, got3, out, rows):
    for z, ref in enumerate((own, got1, got2, got3)):
        for half in range(2):
            row = 12 * half + 3 * z
            rows[row : row + 3, :] = ref[:, 2560 * half : 2560 * half + 2560].astype(jnp.float32)
    out[...] = rows[:24, :].astype(jnp.bfloat16)


def place(stacks, target):
    me = lax.axis_index("seq")
    for slot, ref in enumerate(stacks):
        for z in range(4):
            target[me ^ (4 * z + 2 * (slot & 1) + (slot >> 1))] = ref[z]


def order(near_axis):
    near = lax.broadcasted_iota(jnp.int32, (48, 48), near_axis)
    token = lax.broadcasted_iota(jnp.int32, (48, 48), 1 - near_axis)
    block = (near * 171) >> 9
    device = lax.axis_index("seq") ^ (4 * (block & 3) + ((block >> 2) & 1) + 2 * (block >> 3))
    return (token == 3 * device + near - 3 * block).astype(jnp.bfloat16)


def normalize(values, shift, gain):
    return (layer_norm(values) * (1.0 + gain) + shift).astype(jnp.bfloat16)


def matmul(values, *weights):
    total, row = None, 0
    for part in weights:
        rows = part.shape[0]
        product = jnp.dot(values[:, row : row + rows], part[...], preferred_element_type=jnp.float32)
        total, row = product if total is None else total + product, row + rows
    return total


def unpack_tokens(stacks, rows):
    for slot, ref in enumerate(stacks):
        values = ref[...].astype(jnp.float32)
        for half in range(2):
            piece = values[12 * half : 12 * half + 12]
            rows[12 * slot : 12 * slot + 12, 2560 * half : 2560 * half + 2560] = piece


def project_qkv(s0, s2, s1, s3, mod, weights1, weights2, qkv_out, rows):
    unpack_tokens((s0, s2, s1, s3), rows)
    normed = normalize(rows[:48, :], mod[0:1, :], mod[1:2, :])
    qkv = matmul(normed, weights1, weights2).astype(jnp.bfloat16)
    qkv_out[...] = jnp.dot(order(1), qkv, preferred_element_type=jnp.float32).astype(jnp.bfloat16)


def order_tokens(s0, s2, s1, s3, out, rows):
    unpack_tokens((s0, s2, s1, s3), rows)
    tokens = rows[:48, :].astype(jnp.bfloat16)
    out[...] = jnp.dot(order(1), tokens, preferred_element_type=jnp.float32).astype(jnp.bfloat16)


def line_up(s0, s1, s2, s3, keys_out, values_out, keys, values):
    for slot, ref in enumerate((s0, s1, s2, s3)):
        for z in range(4):
            for token in range(3):
                row = 6 * (4 * slot + z) + 2 * token
                keys[row : row + 2, :] = ref[z, 0, token].astype(jnp.float32)
                values[row : row + 2, :] = ref[z, 1, token].astype(jnp.float32)
    keys_out[...] = keys[:96, :].astype(jnp.bfloat16)
    values_out[...] = values[:96, :].astype(jnp.bfloat16)


def attend(s0, s1, s2, s3, old_keys, old_values, gains, weights, out, slots, scores, expos, attended):
    place((s0, s1, s2, s3), slots)
    pieces = [slots[j] for j in range(16)]
    queries, keys, values = (
        jnp.concatenate([piece[:, 160 * i : 160 * i + 160] for piece in pieces], axis=1) for i in range(3)
    )
    queries = rms_norm(queries.astype(jnp.float32), gains[0:1, :]).astype(jnp.bfloat16)
    keys = rms_norm(keys.astype(jnp.float32), gains[1:2, :]).astype(jnp.bfloat16)
    keys = jnp.concatenate([old_keys[...], keys], axis=0)
    values = jnp.concatenate([old_values[...], values], axis=0)
    none = jnp.zeros((48, HEAD_DIM), jnp.bfloat16)
    pairs = []
    for head in range(0, HEADS, 2):
        first, second = (slice(HEAD_DIM * h, HEAD_DIM * (h + 1)) for h in (head, head + 1))
        pairs.append((slice(48 * head, 48 * (head + 2)), first, second, slice(HEAD_DIM * head, HEAD_DIM * (head + 2))))
    for rows, first, second, both in pairs:
        upper = jnp.concatenate([queries[:, first], none], axis=1)
        lower = jnp.concatenate([none, queries[:, second]], axis=1)
        diagonal = jnp.concatenate([upper, lower], axis=0)
        scores[rows, :] = lax.dot_general(diagonal, keys[:, both], NT, preferred_element_type=jnp.float32)
    scaled = scores[...] * (1.0 / math.sqrt(HEAD_DIM))
    expo = jnp.exp(scaled - jnp.max(scaled, axis=-1, keepdims=True))
    total = 1.0 / jnp.sum(expo, axis=-1, keepdims=True)
    expos[...] = expo.astype(jnp.bfloat16)
    for rows, first, second, both in pairs:
        summed = jnp.dot(expos[rows, :], values[:, both], preferred_element_type=jnp.float32) * total[rows]
        attended[:, first] = summed[:48, :HEAD_DIM].astype(jnp.bfloat16)
        attended[:, second] = summed[48:, HEAD_DIM:].astype(jnp.bfloat16)
    projected = matmul(attended[...], weights)
    out[...] = jnp.concatenate([projected[:24], projected[24:]], axis=1).astype(jnp.bfloat16)


def line_up_projected(stacks, slots):
    place(stacks, slots)
    pieces = [slots[j] for j in range(16)]
    upper = jnp.concatenate([piece[:, :320] for piece in pieces], axis=1)
    lower = jnp.concatenate([piece[:, 320:] for piece in pieces], axis=1)
    return jnp.concatenate([upper, lower], axis=0)


def own_residual(s0, s1, s2, s3, tokens, mod, out, slots):
    projected = line_up_projected((s0, s1, s2, s3), slots)
    own = jnp.dot(order(0)[0:16], projected, preferred_element_type=jnp.float32)[0:3]
    out[...] = tokens[...].astype(jnp.float32) + mod[2:3, :] * own


def feed_forward(s0, s1, s2, s3, tokens, mod, w_up1, w_up2, w_down1, w_down2, keep, send, slots):
    projected = line_up_projected((s0, s1, s2, s3), slots)
    residual = tokens[...].astype(jnp.float32) + mod[2:3, :] * projected.astype(jnp.float32)
    normed = normalize(residual, mod[3:4, :], mod[4:5, :])
    hidden = matmul(normed, w_up1, w_up2)
    hidden = jax.nn.gelu(hidden, approximate=True).astype(jnp.bfloat16)
    hidden = jnp.dot(order(0), hidden, preferred_element_type=jnp.float32).astype(jnp.bfloat16)
    first = lax.axis_index("seq") & 1 == 0
    middle = w_down1.shape[1]
    for cols, weights in ((slice(0, middle), w_down1), (slice(middle, None), w_down2)):
        partial = jnp.dot(hidden, weights[...], preferred_element_type=jnp.float32)
        keep[:, cols] = jnp.where(first, partial[:24], partial[24:])
        send[:, cols] = jnp.where(first, partial[24:], partial[:24]).astype(jnp.bfloat16)


def add_cores(keep, got, own_out, send0, send1, send2, send3):
    got = got[...].astype(jnp.float32)
    total = keep[...] + jnp.concatenate([got[12:], got[:12]], axis=0)
    for z, send in enumerate((send0, send1, send2, send3)):
        block = jnp.concatenate([total[3 * z : 3 * z + 3], total[12 + 3 * z : 15 + 3 * z]], axis=0)
        if z == 0:
            own_out[...] = block
        quarters = [block[:, 1280 * q : 1280 * q + 1280] for q in range(4)]
        send[...] = jnp.concatenate(quarters, axis=0).astype(jnp.bfloat16)


def add_chips(own, got3, got2, got1, got0, keep, send):
    def whole(got):
        got = got[...].astype(jnp.float32)
        return jnp.concatenate([got[6 * q : 6 * q + 6] for q in range(4)], axis=1)

    first = lax.axis_index("seq") & 1 == 0
    total = jnp.where(first, own[...], whole(got0)) + whole(got1) + whole(got2) + whole(got3)
    keep[...] = total[:3]
    send[...] = total[3:]


def finish(keep, got, residual, mod, out):
    out[...] = (residual[...] + mod[5:6, :] * (keep[...] + got[...])).astype(jnp.bfloat16)


def staged(tokens, modulation, w_qkv, norm_gains, cache_kv, w_out, w_up, w_down):
    f32, bf16 = jnp.float32, jnp.bfloat16
    w_qkv = jnp.swapaxes(w_qkv, 1, 2).reshape(480, 5120)
    cache_kv = cache_kv.transpose(0, 2, 1, 3)
    pieces = tuple(swap(tokens, 4 * z) for z in (1, 2, 3))
    cache_far = swap(cache_kv, 8)
    tokens, modulation, norm_gains, cache_kv, w_qkv1 = load(
        tokens, modulation, norm_gains, cache_kv, (w_qkv, 0, QKV_CUT, True)
    )
    pieces, tokens = lax.optimization_barrier((pieces, tokens))
    planes = call(pack_tokens, [((24, 2560), bf16)], tokens, *pieces, scratch=[pltpu.VMEM((32, 2560), f32)])[0]
    across = swap(planes, 2)
    (w_qkv2,), across = load_beside([(w_qkv, QKV_CUT, 5120, True)], planes, across)
    pair = stack([cache_kv, cache_far])
    cache_planes = stack([pair, swap(pair, 4)]).reshape(4, *cache_kv.shape)
    cache_across = swap(cache_planes, 2)
    token_stacks = [planes, swap(planes, 1), across, swap(across, 1)]
    qkv = call(
        project_qkv,
        [((48, 480), bf16)],
        *token_stacks,
        modulation,
        w_qkv1,
        w_qkv2,
        scratch=[pltpu.VMEM((56, 5120), f32)],
    )[0]
    all_tokens = call(order_tokens, [((48, 5120), bf16)], *token_stacks, scratch=[pltpu.VMEM((56, 5120), f32)])[0]
    w_up, w_out = w_up.T, w_out.T
    qkv_stacks, (w_up1, w_up2, w_out) = gather(
        qkv, [(w_up, 0, UP_CUT, True)], [(w_up, UP_CUT, 5120, True), (w_out, 0, 2560, True)]
    )
    old_keys, old_values = call(
        line_up,
        [((96, 2560), bf16)] * 2,
        cache_planes,
        cache_across,
        swap(cache_planes, 1),
        swap(cache_across, 1),
        scratch=[pltpu.VMEM((104, 2560), f32)] * 2,
    )
    projected = call(
        attend,
        [((24, 640), bf16)],
        *qkv_stacks,
        old_keys,
        old_values,
        norm_gains,
        w_out,
        scratch=[
            pltpu.VMEM((16, 48, 480), bf16),
            pltpu.VMEM((48 * HEADS, 144), f32),
            pltpu.VMEM((48 * HEADS, 144), bf16),
            pltpu.VMEM((48, 2560), bf16),
        ],
    )[0]
    projected_stacks, (w_down1, w_down2) = gather(
        projected, [(w_down, 0, DOWN_CUT, False)], [(w_down, DOWN_CUT, 5120, False)]
    )
    keep, send = call(
        feed_forward,
        [((24, 5120), f32), ((24, 5120), bf16)],
        *projected_stacks,
        all_tokens,
        modulation,
        w_up1,
        w_up2,
        w_down1,
        w_down2,
        scratch=[pltpu.VMEM((16, 24, 640), bf16)],
    )
    keep, projected_stacks = lax.optimization_barrier((keep, projected_stacks))
    slots = pltpu.VMEM((16, 24, 640), bf16)
    residual = call(own_residual, [((3, 5120), f32)], *projected_stacks, tokens, modulation, scratch=[slots])[0]
    own, *sends = call(add_cores, [((6, 5120), f32)] + [((24, 1280), bf16)] * 4, keep, swap(send, 1))
    got = []
    for z, send in enumerate(sends):
        pairs = [(i, i ^ 4 * z ^ 2 * (i & 1)) for i in range(16)]
        got.append(lax.ppermute(send, "seq", [(i, j) for i, j in pairs if i != j]))
    keep, send = call(add_chips, [((3, 5120), f32)] * 2, own, *[got[k] for k in (3, 2, 1, 0)])
    return call(finish, [((3, 5120), bf16)], keep, swap(send, 1), residual, modulation)[0]


def general(tokens, modulation, w_qkv, norm_gains, cache_kv, w_out, w_up, w_down):
    own_rows = tokens.shape[0]
    width = HEADS * HEAD_DIM
    scale = 1.0 / math.sqrt(HEAD_DIM)
    residual = tokens.astype(jnp.float32)
    normed = (layer_norm(residual) * (1.0 + modulation[1]) + modulation[0]).astype(jnp.bfloat16)
    qkv_cols = jnp.einsum(
        "td,kda->kta",
        lax.all_gather(normed, "seq", axis=0, tiled=True),
        w_qkv,
        preferred_element_type=jnp.float32,
    ).astype(jnp.bfloat16)
    qkv = lax.all_to_all(qkv_cols, "seq", split_axis=1, concat_axis=2, tiled=True)
    queries = rms_norm(qkv[0].astype(jnp.float32), norm_gains[0]).astype(jnp.bfloat16)
    keys_now = rms_norm(qkv[1].astype(jnp.float32), norm_gains[1]).astype(jnp.bfloat16)
    local_keys = jnp.concatenate([cache_kv[0].reshape(-1, width), keys_now], axis=0)
    local_values = jnp.concatenate([cache_kv[1].reshape(-1, width), qkv[2]], axis=0)
    query_heads = queries.reshape(own_rows, HEADS, HEAD_DIM)
    peak_old = jnp.full((own_rows, HEADS), -1e30, jnp.float32)
    key_piece = lax.all_gather(local_keys, "seq", axis=0, tiled=True)
    value_piece = lax.all_gather(local_values, "seq", axis=0, tiled=True)
    count = key_piece.shape[0]
    scores = (
        jnp.einsum(
            "qhd,khd->qhk",
            query_heads,
            key_piece.reshape(count, HEADS, HEAD_DIM),
            preferred_element_type=jnp.float32,
        )
        * scale
    )
    peak_new = jnp.maximum(peak_old, jnp.max(scores, axis=-1))
    expo = jnp.exp(scores - peak_new[..., None])
    total_new = jnp.sum(expo, axis=-1)
    weights = expo.astype(jnp.bfloat16)
    summed_new = jnp.einsum(
        "qhk,khd->qhd",
        weights,
        value_piece.reshape(count, HEADS, HEAD_DIM),
        preferred_element_type=jnp.float32,
    )
    attended = (summed_new / total_new[..., None]).reshape(own_rows, width).astype(jnp.bfloat16)
    projected_cols = jnp.dot(
        lax.all_gather(attended, "seq", axis=0, tiled=True),
        w_out,
        preferred_element_type=jnp.float32,
    ).astype(jnp.bfloat16)
    projected = lax.all_to_all(projected_cols, "seq", split_axis=0, concat_axis=1, tiled=True)
    residual = residual + modulation[2] * projected.astype(jnp.float32)
    normed2 = (layer_norm(residual) * (1.0 + modulation[4]) + modulation[3]).astype(jnp.bfloat16)
    hidden = jax.nn.gelu(
        jnp.dot(
            lax.all_gather(normed2, "seq", axis=0, tiled=True),
            w_up,
            preferred_element_type=jnp.float32,
        ),
        approximate=True,
    ).astype(jnp.bfloat16)
    feed = lax.psum_scatter(
        jnp.dot(hidden, w_down, preferred_element_type=jnp.float32),
        "seq",
        scatter_dimension=0,
        tiled=True,
    )
    return (residual + modulation[5] * feed).astype(jnp.bfloat16)


def solution(mesh):
    in_specs = (
        P(("groups", "seq"), None),
        P(),
        P(None, None, "seq"),
        P(),
        P(None, None, ("groups", "seq"), None),
        P(None, "seq"),
        P(None, "seq"),
        P("seq", None),
    )
    out_specs = P(("groups", "seq"), None)
    local = staged if mesh.shape["seq"] == 16 else general
    return jax.shard_map(local, mesh=mesh, in_specs=in_specs, out_specs=out_specs, check_vma=False)
```

```python
import math

import jax
import jax.numpy as jnp
from jax import lax
from jax.experimental import pallas as pl
from jax.experimental.pallas import tpu as pltpu
from jax.sharding import PartitionSpec as P

HEAD_DIM = 128
HEADS = 20
QKV_CUT, UP_CUT, DOWN_CUT = 1920, 1920, 1920


def layer_norm(values):
    center = values - jnp.mean(values, axis=-1, keepdims=True)
    spread = jnp.mean(center * center, axis=-1, keepdims=True)
    return center * lax.rsqrt(spread + 1e-06)


def rms_norm(values, gain):
    return values * lax.rsqrt(jnp.mean(values * values, axis=-1, keepdims=True) + 1e-06) * gain


VMEM = pl.BlockSpec(memory_space=pltpu.VMEM)
HBM = pl.BlockSpec(memory_space=pltpu.HBM)
NT = (((1,), (1,)), ((), ()))


def call(body, outs, *operands, spec=VMEM, scratch=(), limit=24):
    return pl.pallas_call(
        body,
        out_shape=[jax.ShapeDtypeStruct(shape, dtype) for shape, dtype in outs],
        in_specs=[spec] * len(operands),
        out_specs=[VMEM] * len(outs),
        scratch_shapes=list(scratch),
        compiler_params=pltpu.CompilerParams(vmem_limit_bytes=limit << 20),
        cost_estimate=pl.CostEstimate(flops=0, bytes_accessed=0, transcendentals=0),
    )(*operands)


def load(*parts):
    parts = [part if isinstance(part, tuple) else (part, None, None, False) for part in parts]
    arrays = [pltpu.with_memory_space_constraint(array, pltpu.HBM) for array, *_ in parts]
    outs, buffers, pieces = [], [], []
    for i, (array, lo, hi, turn) in enumerate(parts):
        if lo is None:
            outs.append((array.shape, array.dtype))
            pieces.append((i, None, None, None))
            continue
        shape = (array.shape[0], hi - lo)
        outs.append((shape[::-1] if turn else shape, array.dtype))
        if turn:
            buffers.append(pltpu.VMEM(shape, array.dtype))
        size = min(640, hi - lo)
        for start in range(0, hi - lo, size):
            pieces.append((i, pl.ds(lo + start, size), pl.ds(start, size), len(buffers) - 1 if turn else None))

    def body(*refs):
        sources, targets = refs[: len(arrays)], refs[len(arrays) : 2 * len(arrays)]
        sems, *held = refs[2 * len(arrays) :]
        copies = []
        for n, (i, cut, into, buffer) in enumerate(pieces):
            target = targets[i] if buffer is None else held[buffer]
            source = sources[i] if cut is None else sources[i].at[:, cut]
            target = target if cut is None else target.at[:, into]
            copies.append(pltpu.make_async_copy(source, target, sems.at[n]))
        for copy in copies:
            copy.start()
        for copy, (i, _, into, buffer) in zip(copies, pieces):
            copy.wait()
            if buffer is not None:
                targets[i][into, :] = held[buffer][:, into].T

    return call(body, outs, *arrays, spec=HBM, scratch=[pltpu.SemaphoreType.DMA((len(pieces),)), *buffers])


def swap(values, offset):
    return lax.ppermute(values, "seq", [(i, i ^ offset) for i in range(16)])


def stack(pieces):
    def body(*refs):
        for i, ref in enumerate(refs[:-1]):
            refs[-1][i] = ref[...]

    return call(body, [((len(pieces), *pieces[0].shape), pieces[0].dtype)], *pieces)[0]


def load_beside(parts, before, beside):
    arrays, _ = lax.optimization_barrier(([array for array, *_ in parts], before))
    return lax.optimization_barrier((load(*[(array, *part[1:]) for array, part in zip(arrays, parts)]), beside))


def gather(block, load_z, load_y):
    pieces = tuple(swap(block, 4 * z) for z in (1, 2, 3))
    loaded_z, pieces = load_beside(load_z, block, pieces)
    planes = stack([block, *pieces])
    across = swap(planes, 2)
    loaded_y, across = load_beside(load_y, planes, across)
    return [planes, across, swap(planes, 1), swap(across, 1)], loaded_z + loaded_y


def pack_tokens(own, got1, got2, got3, out, rows):
    for z, ref in enumerate((own, got1, got2, got3)):
        for half in range(2):
            row = 12 * half + 3 * z
            rows[row : row + 3, :] = ref[:, 2560 * half : 2560 * half + 2560].astype(jnp.float32)
    out[...] = rows[:24, :].astype(jnp.bfloat16)


def place(stacks, target):
    me = lax.axis_index("seq")
    for slot, ref in enumerate(stacks):
        for z in range(4):
            target[me ^ (4 * z + 2 * (slot & 1) + (slot >> 1))] = ref[z]


def order(near_axis):
    near = lax.broadcasted_iota(jnp.int32, (48, 48), near_axis)
    token = lax.broadcasted_iota(jnp.int32, (48, 48), 1 - near_axis)
    block = (near * 171) >> 9
    device = lax.axis_index("seq") ^ (4 * (block & 3) + ((block >> 2) & 1) + 2 * (block >> 3))
    return (token == 3 * device + near - 3 * block).astype(jnp.bfloat16)


def normalize(values, shift, gain):
    return (layer_norm(values) * (1.0 + gain) + shift).astype(jnp.bfloat16)


def matmul(values, *weights):
    total, row = None, 0
    for part in weights:
        rows = part.shape[0]
        product = jnp.dot(values[:, row : row + rows], part[...], preferred_element_type=jnp.float32)
        total, row = product if total is None else total + product, row + rows
    return total


def unpack_tokens(stacks, rows):
    for slot, ref in enumerate(stacks):
        values = ref[...].astype(jnp.float32)
        for half in range(2):
            piece = values[12 * half : 12 * half + 12]
            rows[12 * slot : 12 * slot + 12, 2560 * half : 2560 * half + 2560] = piece


def project_qkv(s0, s2, s1, s3, mod, weights1, weights2, qkv_out, rows):
    unpack_tokens((s0, s2, s1, s3), rows)
    normed = normalize(rows[:48, :], mod[0:1, :], mod[1:2, :])
    qkv = matmul(normed, weights1, weights2).astype(jnp.bfloat16)
    qkv_out[...] = jnp.dot(order(1), qkv, preferred_element_type=jnp.float32).astype(jnp.bfloat16)


def order_tokens(s0, s2, s1, s3, out, rows):
    unpack_tokens((s0, s2, s1, s3), rows)
    tokens = rows[:48, :].astype(jnp.bfloat16)
    out[...] = jnp.dot(order(1), tokens, preferred_element_type=jnp.float32).astype(jnp.bfloat16)


def line_up(s0, s1, s2, s3, keys_out, values_out, keys, values):
    for slot, ref in enumerate((s0, s1, s2, s3)):
        for z in range(4):
            for token in range(3):
                row = 6 * (4 * slot + z) + 2 * token
                keys[row : row + 2, :] = ref[z, 0, token].astype(jnp.float32)
                values[row : row + 2, :] = ref[z, 1, token].astype(jnp.float32)
    keys_out[...] = keys[:96, :].astype(jnp.bfloat16)
    values_out[...] = values[:96, :].astype(jnp.bfloat16)


def attend(s0, s1, s2, s3, old_keys, old_values, gains, weights, out, slots, scores, expos, attended):
    place((s0, s1, s2, s3), slots)
    pieces = [slots[j] for j in range(16)]
    queries, keys, values = (
        jnp.concatenate([piece[:, 160 * i : 160 * i + 160] for piece in pieces], axis=1) for i in range(3)
    )
    queries = rms_norm(queries.astype(jnp.float32), gains[0:1, :]).astype(jnp.bfloat16)
    keys = rms_norm(keys.astype(jnp.float32), gains[1:2, :]).astype(jnp.bfloat16)
    keys = jnp.concatenate([old_keys[...], keys], axis=0)
    values = jnp.concatenate([old_values[...], values], axis=0)
    none = jnp.zeros((48, HEAD_DIM), jnp.bfloat16)
    pairs = []
    for head in range(0, HEADS, 2):
        first, second = (slice(HEAD_DIM * h, HEAD_DIM * (h + 1)) for h in (head, head + 1))
        pairs.append((slice(48 * head, 48 * (head + 2)), first, second, slice(HEAD_DIM * head, HEAD_DIM * (head + 2))))
    for rows, first, second, both in pairs:
        upper = jnp.concatenate([queries[:, first], none], axis=1)
        lower = jnp.concatenate([none, queries[:, second]], axis=1)
        diagonal = jnp.concatenate([upper, lower], axis=0)
        scores[rows, :] = lax.dot_general(diagonal, keys[:, both], NT, preferred_element_type=jnp.float32)
    scaled = scores[...] * (1.0 / math.sqrt(HEAD_DIM))
    expo = jnp.exp(scaled - jnp.max(scaled, axis=-1, keepdims=True))
    total = jnp.sum(expo, axis=-1, keepdims=True)
    expos[...] = expo.astype(jnp.bfloat16)
    for rows, first, second, both in pairs:
        summed = jnp.dot(expos[rows, :], values[:, both], preferred_element_type=jnp.float32) / total[rows]
        attended[:, first] = summed[:48, :HEAD_DIM].astype(jnp.bfloat16)
        attended[:, second] = summed[48:, HEAD_DIM:].astype(jnp.bfloat16)
    projected = lax.dot_general(attended[...], weights[...], NT, preferred_element_type=jnp.float32)
    out[...] = jnp.concatenate([projected[:24], projected[24:]], axis=1).astype(jnp.bfloat16)


def line_up_projected(stacks, slots):
    place(stacks, slots)
    pieces = [slots[j] for j in range(16)]
    upper = jnp.concatenate([piece[:, :320] for piece in pieces], axis=1)
    lower = jnp.concatenate([piece[:, 320:] for piece in pieces], axis=1)
    return jnp.concatenate([upper, lower], axis=0)


def own_residual(s0, s1, s2, s3, tokens, mod, out, slots):
    projected = line_up_projected((s0, s1, s2, s3), slots)
    own = jnp.dot(order(0)[0:16], projected, preferred_element_type=jnp.float32)[0:3]
    out[...] = tokens[...].astype(jnp.float32) + mod[2:3, :] * own


def feed_forward(s0, s1, s2, s3, tokens, mod, w_up1, w_up2, w_down1, w_down2, keep, send, slots):
    projected = line_up_projected((s0, s1, s2, s3), slots)
    residual = tokens[...].astype(jnp.float32) + mod[2:3, :] * projected.astype(jnp.float32)
    normed = normalize(residual, mod[3:4, :], mod[4:5, :])
    hidden = matmul(normed, w_up1, w_up2)
    hidden = jax.nn.gelu(hidden, approximate=True).astype(jnp.bfloat16)
    hidden = jnp.dot(order(0), hidden, preferred_element_type=jnp.float32).astype(jnp.bfloat16)
    first = lax.axis_index("seq") & 1 == 0
    middle = w_down1.shape[1]
    for cols, weights in ((slice(0, middle), w_down1), (slice(middle, None), w_down2)):
        partial = jnp.dot(hidden, weights[...], preferred_element_type=jnp.float32)
        keep[:, cols] = jnp.where(first, partial[:24], partial[24:])
        send[:, cols] = jnp.where(first, partial[24:], partial[:24]).astype(jnp.bfloat16)


def add_cores(keep, got, own_out, send0, send1, send2, send3):
    got = got[...].astype(jnp.float32)
    total = keep[...] + jnp.concatenate([got[12:], got[:12]], axis=0)
    for z, send in enumerate((send0, send1, send2, send3)):
        block = jnp.concatenate([total[3 * z : 3 * z + 3], total[12 + 3 * z : 15 + 3 * z]], axis=0)
        if z == 0:
            own_out[...] = block
        quarters = [block[:, 1280 * q : 1280 * q + 1280] for q in range(4)]
        send[...] = jnp.concatenate(quarters, axis=0).astype(jnp.bfloat16)


def add_chips(own, got3, got2, got1, got0, keep, send):
    def whole(got):
        got = got[...].astype(jnp.float32)
        return jnp.concatenate([got[6 * q : 6 * q + 6] for q in range(4)], axis=1)

    first = lax.axis_index("seq") & 1 == 0
    total = jnp.where(first, own[...], whole(got0)) + whole(got1) + whole(got2) + whole(got3)
    keep[...] = total[:3]
    send[...] = total[3:].astype(jnp.bfloat16)


def finish(keep, got, residual, mod, out):
    out[...] = (residual[...] + mod[5:6, :] * (keep[...] + got[...].astype(jnp.float32))).astype(jnp.bfloat16)


def staged(tokens, modulation, w_qkv, norm_gains, cache_kv, w_out, w_up, w_down):
    f32, bf16 = jnp.float32, jnp.bfloat16
    w_qkv = jnp.swapaxes(w_qkv, 1, 2).reshape(480, 5120)
    cache_kv = cache_kv.transpose(0, 2, 1, 3)
    pieces = tuple(swap(tokens, 4 * z) for z in (1, 2, 3))
    cache_far = swap(cache_kv, 8)
    tokens, modulation, norm_gains, cache_kv, w_qkv1 = load(
        tokens, modulation, norm_gains, cache_kv, (w_qkv, 0, QKV_CUT, True)
    )
    pieces, tokens = lax.optimization_barrier((pieces, tokens))
    planes = call(pack_tokens, [((24, 2560), bf16)], tokens, *pieces, scratch=[pltpu.VMEM((32, 2560), f32)])[0]
    across = swap(planes, 2)
    (w_qkv2,), across = load_beside([(w_qkv, QKV_CUT, 5120, True)], planes, across)
    pair = stack([cache_kv, cache_far])
    cache_planes = stack([pair, swap(pair, 4)]).reshape(4, *cache_kv.shape)
    cache_across = swap(cache_planes, 2)
    token_stacks = [planes, swap(planes, 1), across, swap(across, 1)]
    qkv = call(
        project_qkv,
        [((48, 480), bf16)],
        *token_stacks,
        modulation,
        w_qkv1,
        w_qkv2,
        scratch=[pltpu.VMEM((56, 5120), f32)],
    )[0]
    all_tokens = call(order_tokens, [((48, 5120), bf16)], *token_stacks, scratch=[pltpu.VMEM((56, 5120), f32)])[0]
    w_up, w_out = w_up.T, w_out.T
    qkv_stacks, (w_up1, w_up2, w_out) = gather(
        qkv, [(w_up, 0, UP_CUT, True)], [(w_up, UP_CUT, 5120, True), (w_out, 0, 2560, False)]
    )
    old_keys, old_values = call(
        line_up,
        [((96, 2560), bf16)] * 2,
        cache_planes,
        cache_across,
        swap(cache_planes, 1),
        swap(cache_across, 1),
        scratch=[pltpu.VMEM((104, 2560), f32)] * 2,
    )
    projected = call(
        attend,
        [((24, 640), bf16)],
        *qkv_stacks,
        old_keys,
        old_values,
        norm_gains,
        w_out,
        scratch=[
            pltpu.VMEM((16, 48, 480), bf16),
            pltpu.VMEM((48 * HEADS, 144), f32),
            pltpu.VMEM((48 * HEADS, 144), bf16),
            pltpu.VMEM((48, 2560), bf16),
        ],
    )[0]
    projected_stacks, (w_down1, w_down2) = gather(
        projected, [(w_down, 0, DOWN_CUT, False)], [(w_down, DOWN_CUT, 5120, False)]
    )
    keep, send = call(
        feed_forward,
        [((24, 5120), f32), ((24, 5120), bf16)],
        *projected_stacks,
        all_tokens,
        modulation,
        w_up1,
        w_up2,
        w_down1,
        w_down2,
        scratch=[pltpu.VMEM((16, 24, 640), bf16)],
    )
    keep, projected_stacks = lax.optimization_barrier((keep, projected_stacks))
    slots = pltpu.VMEM((16, 24, 640), bf16)
    residual = call(own_residual, [((3, 5120), f32)], *projected_stacks, tokens, modulation, scratch=[slots])[0]
    own, *sends = call(add_cores, [((6, 5120), f32)] + [((24, 1280), bf16)] * 4, keep, swap(send, 1))
    got = []
    for z, send in enumerate(sends):
        pairs = [(i, i ^ 4 * z ^ 2 * (i & 1)) for i in range(16)]
        got.append(lax.ppermute(send, "seq", [(i, j) for i, j in pairs if i != j]))
    keep, send = call(add_chips, [((3, 5120), f32), ((3, 5120), bf16)], own, *[got[k] for k in (3, 2, 1, 0)])
    return call(finish, [((3, 5120), bf16)], keep, swap(send, 1), residual, modulation)[0]


def general(tokens, modulation, w_qkv, norm_gains, cache_kv, w_out, w_up, w_down):
    own_rows = tokens.shape[0]
    width = HEADS * HEAD_DIM
    scale = 1.0 / math.sqrt(HEAD_DIM)
    residual = tokens.astype(jnp.float32)
    normed = (layer_norm(residual) * (1.0 + modulation[1]) + modulation[0]).astype(jnp.bfloat16)
    qkv_cols = jnp.einsum(
        "td,kda->kta",
        lax.all_gather(normed, "seq", axis=0, tiled=True),
        w_qkv,
        preferred_element_type=jnp.float32,
    ).astype(jnp.bfloat16)
    qkv = lax.all_to_all(qkv_cols, "seq", split_axis=1, concat_axis=2, tiled=True)
    queries = rms_norm(qkv[0].astype(jnp.float32), norm_gains[0]).astype(jnp.bfloat16)
    keys_now = rms_norm(qkv[1].astype(jnp.float32), norm_gains[1]).astype(jnp.bfloat16)
    local_keys = jnp.concatenate([cache_kv[0].reshape(-1, width), keys_now], axis=0)
    local_values = jnp.concatenate([cache_kv[1].reshape(-1, width), qkv[2]], axis=0)
    query_heads = queries.reshape(own_rows, HEADS, HEAD_DIM)
    peak_old = jnp.full((own_rows, HEADS), -1e30, jnp.float32)
    key_piece = lax.all_gather(local_keys, "seq", axis=0, tiled=True)
    value_piece = lax.all_gather(local_values, "seq", axis=0, tiled=True)
    count = key_piece.shape[0]
    scores = (
        jnp.einsum(
            "qhd,khd->qhk",
            query_heads,
            key_piece.reshape(count, HEADS, HEAD_DIM),
            preferred_element_type=jnp.float32,
        )
        * scale
    )
    peak_new = jnp.maximum(peak_old, jnp.max(scores, axis=-1))
    expo = jnp.exp(scores - peak_new[..., None])
    total_new = jnp.sum(expo, axis=-1)
    weights = expo.astype(jnp.bfloat16)
    summed_new = jnp.einsum(
        "qhk,khd->qhd",
        weights,
        value_piece.reshape(count, HEADS, HEAD_DIM),
        preferred_element_type=jnp.float32,
    )
    attended = (summed_new / total_new[..., None]).reshape(own_rows, width).astype(jnp.bfloat16)
    projected_cols = jnp.dot(
        lax.all_gather(attended, "seq", axis=0, tiled=True),
        w_out,
        preferred_element_type=jnp.float32,
    ).astype(jnp.bfloat16)
    projected = lax.all_to_all(projected_cols, "seq", split_axis=0, concat_axis=1, tiled=True)
    residual = residual + modulation[2] * projected.astype(jnp.float32)
    normed2 = (layer_norm(residual) * (1.0 + modulation[4]) + modulation[3]).astype(jnp.bfloat16)
    hidden = jax.nn.gelu(
        jnp.dot(
            lax.all_gather(normed2, "seq", axis=0, tiled=True),
            w_up,
            preferred_element_type=jnp.float32,
        ),
        approximate=True,
    ).astype(jnp.bfloat16)
    feed = lax.psum_scatter(
        jnp.dot(hidden, w_down, preferred_element_type=jnp.float32),
        "seq",
        scatter_dimension=0,
        tiled=True,
    )
    return (residual + modulation[5] * feed).astype(jnp.bfloat16)


def solution(mesh):
    in_specs = (
        P(("groups", "seq"), None),
        P(),
        P(None, None, "seq"),
        P(),
        P(None, None, ("groups", "seq"), None),
        P(None, "seq"),
        P(None, "seq"),
        P("seq", None),
    )
    out_specs = P(("groups", "seq"), None)
    local = staged if mesh.shape["seq"] == 16 else general
    return jax.shard_map(local, mesh=mesh, in_specs=in_specs, out_specs=out_specs, check_vma=False)
```
